32 devices in a mesh: dp: 8 (over y, x, core), ctx: 4 (over z).
Axes of the slice: x: 2, y: 2, z: 4, core: 2. Of those that a mesh axis runs over, the one named last changes fastest.
Arguments:
- inputs: bfloat16 [8192, 2048], P(('dp', 'ctx')), may hold values from -6 to 6
- span_table: int32 [4, 2], replicated, may hold values from 0 to 7, as said below
- ln_gain: bfloat16 [2048], P(('dp', 'ctx')), may hold values from 0.5 to 1.5
- ln_bias: bfloat16 [2048], P(('dp', 'ctx')), may hold values from -2 to 2
- qkv_weight: bfloat16 [2048, 6144], P(('dp', 'ctx')), may hold values from -0.125 to 0.125
- qkv_bias: bfloat16 [6144], P(('dp', 'ctx')), may hold values from -0.19921875 to 0.19921875
- out_weight: bfloat16 [2048, 2048], P(('dp', 'ctx')), may hold values from -2 to 2
- out_bias: bfloat16 [2048], P(('dp', 'ctx')), may hold values from -2 to 2
- fc1_weight: bfloat16 [2048, 8192], P(('dp', 'ctx')), may hold values from -0.125 to 0.125
- fc1_bias: bfloat16 [8192], P(('dp', 'ctx')), may hold values from -2 to 2
- fc2_weight: bfloat16 [8192, 2048], P(('dp', 'ctx')), may hold values from -0.0625 to 0.0625
- fc2_bias: bfloat16 [2048], P(('dp', 'ctx')), may hold values from -2 to 2
- cotangent: bfloat16 [8192, 2048], P(('dp', 'ctx')), may hold values from -6 to 6
Outputs:
- output: bfloat16 [8192, 2048], P(('dp', 'ctx'))
- input_grad: bfloat16 [8192, 2048], P(('dp', 'ctx'))
- ln_gain_grad: float32 [2048], P(('dp', 'ctx'))
- ln_bias_grad: float32 [2048], P(('dp', 'ctx'))
- qkv_weight_grad: float32 [2048, 6144], P(('dp', 'ctx'))
- qkv_bias_grad: float32 [6144], P(('dp', 'ctx'))
- out_weight_grad: float32 [2048, 2048], P(('dp', 'ctx'))
- out_bias_grad: float32 [2048], P(('dp', 'ctx'))
- fc1_weight_grad: float32 [2048, 8192], P(('dp', 'ctx'))
- fc1_bias_grad: float32 [8192], P(('dp', 'ctx'))
- fc2_weight_grad: float32 [8192, 2048], P(('dp', 'ctx'))
- fc2_bias_grad: float32 [2048], P(('dp', 'ctx'))
The draws below stay inside these ranges and needn't reach their ends.
Inputs may be any that keep to these rules, and one draw needn't show every extreme that they name: `span_table`: row i names two spans c and 7 - c for some c, in either order; every span of 0 to 7 appears once.
All inputs are finite; a program needn't handle non-finite values.
Results may differ from the reference program's by a relative error of at most 0.013.
Values may be sent and summed in bfloat16 or wider, within the bound.
No kernel may reach another device: no remote copies, remote signals or barrier semaphores. Data moves between devices by JAX's collectives and lax.ppermute only.
A program may use at most 248 MiB of HBM per device.

```python
import math
from functools import partial
import jax
import jax.numpy as jnp
from jax import lax

D = 2048
HEADS = 32
HEAD = 64
ROT = 32
FF = 8192
SPAN = 128
SEQ_LEN = 1024
TOKENS = 8192
N_DP = 8
N_CTX = 4


def draw_span_table(key, part):
    key = jax.random.fold_in(key, 11)
    first, second = jax.random.split(key)
    lower = jax.random.permutation(first, N_CTX).astype(jnp.int32)
    upper = 2 * N_CTX - 1 - lower
    flips = jax.random.randint(second, (N_CTX,), 0, 2)
    front = jnp.where(flips == 1, upper, lower)
    back = jnp.where(flips == 1, lower, upper)
    return jnp.stack([front, back], 1).astype(jnp.int32)


def strengthened(values, stream_key, source, target, shards_of, factor):
    owner, partner = [(jnp.arange(values.shape[position]) // (values.shape[position] // shards_of)).reshape([-1 if axis == position else 1 for axis in range(values.ndim)]) for position in (source, target)]
    chosen = jax.random.permutation(stream_key, shards_of)[partner]
    strong = (owner == chosen) | (owner == (partner + shards_of // 2) % shards_of)
    return jnp.where(strong, factor * values, values)


def block_scale(own_key, shape, cuts, smallest, high):
    def one(axis_at, blocks):
        draws = jax.random.uniform(jax.random.fold_in(jax.random.fold_in(own_key, 6), axis_at), (blocks,), jnp.float32, smallest / len(cuts), high / len(cuts))
        return jnp.repeat(jnp.exp(draws), shape[axis_at] // blocks).reshape((-1,) + (1,) * (len(shape) - axis_at - 1))

    level = one(*cuts[0])
    for cut in cuts[1:]:
        level = level * one(*cut)
    return level


def gaussian(key, shape, width, reach, cuts=(), kind=jnp.bfloat16):
    array = jax.random.normal(key, shape, jnp.float32) * width
    if len(cuts) > 0:
        array = block_scale(key, shape, cuts, -0.22, 0.18) * array
    return jnp.clip(array, min=-reach, max=reach).astype(kind)


def heavy_noise(own_key, dims, scale, most, shards, heavy, held_as=jnp.bfloat16):
    values = scale * jax.random.normal(own_key, dims, jnp.float32)
    if shards:
        values = values * block_scale(own_key, dims, shards, -0.22, 0.18)
    return jnp.clip(strengthened(values, jax.random.fold_in(own_key, 3), *heavy), -most, most).astype(held_as)


def setup_inputs(seed: int = 0) -> dict:
    streams_of = jax.random.split(jax.random.key(seed), 14)
    inputs = heavy_noise(streams_of[0], (TOKENS, D), 1.0, 6.0, ((0, 32),), (0, 1, 32, 2.75))
    span_table = draw_span_table(jax.random.fold_in(streams_of[13], 71), 0)
    ln_gain = jnp.clip(1.0 + 0.1 * jax.random.normal(streams_of[2], (D,), jnp.float32), 0.5, 1.5).astype(jnp.bfloat16)
    ln_bias = gaussian(streams_of[3], (D,), 0.3, 2.0, ((0, 32),))
    qkv_weight = gaussian(streams_of[4], (D, 3 * D), D ** -0.5, 0.125, ((0, 32),))
    qkv_bias = gaussian(streams_of[5], (3 * D,), 0.03, 0.19921875, ((0, 32),))
    out_weight = gaussian(streams_of[6], (D, D), (max(D // 256, 8)) ** -0.5, 2.0, ((0, 32),))
    out_bias = gaussian(streams_of[7], (D,), 0.3, 2.0, ((0, 32),))
    fc1_weight = gaussian(streams_of[8], (D, FF), D ** -0.5, 0.125, ((0, 32),))
    fc1_bias = gaussian(streams_of[9], (FF,), 0.3, 2.0, ((0, 32),))
    fc2_weight = gaussian(streams_of[10], (FF, D), FF ** -0.5, 0.0625, ((0, 32),))
    fc2_bias = gaussian(streams_of[11], (D,), 0.3, 2.0, ((0, 32),))
    cotangent = heavy_noise(streams_of[12], (TOKENS, D), 1.0, 6.0, ((0, 32),), (0, 1, 32, 2.75))
    return dict(inputs=inputs, span_table=span_table, ln_gain=ln_gain, ln_bias=ln_bias, qkv_weight=qkv_weight, qkv_bias=qkv_bias, out_weight=out_weight, out_bias=out_bias, fc1_weight=fc1_weight, fc1_bias=fc1_bias, fc2_weight=fc2_weight, fc2_bias=fc2_bias, cotangent=cotangent)


EPS = 1e-05
NEG = -1e+30

@jax.custom_vjp
def low(v):
    return lax.optimization_barrier(v.astype(jnp.bfloat16)).astype(jnp.float32)

@jax.custom_vjp
def low_back(v):
    return v

def low_keep(v):
    return (low(v), None)

def low_pass(kept, grad):
    return (grad,)

def back_keep(v):
    return (v, None)

def back_low(kept, grad):
    return (low(grad),)
low.defvjp(low_keep, low_pass)
low_back.defvjp(back_keep, back_low)

def layer_norm(values, gain, bias):
    mean = lax.optimization_barrier(jnp.mean(values, axis=-1, keepdims=True))
    centred = values - mean
    spread = lax.optimization_barrier(jnp.mean(centred * centred, axis=-1, keepdims=True))
    return centred * lax.rsqrt(spread + EPS) * gain + bias

def span_positions(spans, span_len):
    starts = spans.reshape(-1).astype(jnp.int32)[:, None] * span_len
    return (starts + jnp.arange(span_len, dtype=jnp.int32)[None, :]).reshape(-1)

def rotary_tables(positions, rot_dims):
    half = rot_dims // 2
    freqs = jnp.exp(jnp.arange(half, dtype=jnp.float32) * (-2.0 * math.log(10000.0) / rot_dims))
    angles = positions.astype(jnp.float32)[:, None] * freqs[None, :]
    cosine = jnp.cos(angles)
    sine = jnp.sin(angles)
    return (jnp.concatenate([cosine, cosine], 1), jnp.concatenate([sine, sine], 1))

def rotate(values, cosine, sine):
    rot_dims = cosine.shape[1]
    half = rot_dims // 2
    front = values[..., :rot_dims]
    turned = jnp.concatenate([-front[..., half:], front[..., :half]], -1)
    moved = front * cosine[:, None, :] + turned * sine[:, None, :]
    return jnp.concatenate([moved, values[..., rot_dims:]], -1)

def matmul(left, right):
    return jnp.dot(left, right, precision=lax.Precision.HIGHEST, preferred_element_type=jnp.float32)

def attend(queries, keys, values, positions, scale):
    rows, heads, head_dim = queries.shape
    block = math.gcd(rows, 512)
    count = rows // block

    def one_block(item):
        query_block, pos_block = item
        scores = low_back(jnp.einsum('qhd,khd->hqk', query_block, keys, precision=lax.Precision.HIGHEST) * scale)
        allowed = positions[None, None, :] <= pos_block[None, :, None]
        probs = low(jax.nn.softmax(jnp.where(allowed, scores, NEG), axis=-1))
        return jnp.einsum('hqk,khd->qhd', probs, values, precision=lax.Precision.HIGHEST)
    blocks = lax.map(jax.checkpoint(one_block), (queries.reshape(count, block, heads, head_dim), positions.reshape(count, block)))
    return blocks.reshape(rows, heads * head_dim)

def layer_forward(x, gain, shift, w_qkv, b_qkv, w_out, b_out, w_up, b_up, w_down, b_down, positions):
    rows = x.shape[0]
    hidden = low(layer_norm(x, gain, shift))
    qkv = low_back(matmul(hidden, w_qkv) + b_qkv)
    q_raw = qkv[:, :D].reshape(rows, HEADS, HEAD)
    k_raw = qkv[:, D:2 * D].reshape(rows, HEADS, HEAD)
    cosine, sine = rotary_tables(positions, ROT)
    queries = low(rotate(q_raw, cosine, sine))
    keys = low(rotate(k_raw, cosine, sine))
    values = low(qkv[:, 2 * D:].reshape(rows, HEADS, HEAD))
    attended = attend(queries, keys, values, positions, HEAD ** (-0.5))
    attended_low = low(low_back(attended))
    pre = low_back(matmul(hidden, w_up) + b_up)
    act = low(jax.nn.gelu(pre, approximate=True))
    return x + (matmul(attended_low, w_out) + b_out) + (matmul(act, w_down) + b_down)

def reference(inputs, span_table, ln_gain, ln_bias, qkv_weight, qkv_bias, out_weight, out_bias, fc1_weight, fc1_bias, fc2_weight, fc2_bias, cotangent):
    positions = span_positions(span_table, SPAN)
    params = tuple((p.astype(jnp.float32) for p in (ln_gain, ln_bias, qkv_weight, qkv_bias, out_weight, out_bias, fc1_weight, fc1_bias, fc2_weight, fc2_bias)))
    xs = inputs.astype(jnp.float32).reshape(N_DP, SEQ_LEN, D)
    gs = cotangent.astype(jnp.float32).reshape(N_DP, SEQ_LEN, D)
    forward = partial(layer_forward, positions=positions)

    def step(sums, item):
        x, g = item
        y, back = jax.vjp(forward, x, *params)
        grads = back(g)
        return (tuple((a + b for a, b in zip(sums, grads[1:]))), (y, grads[0]))
    zero = tuple((jnp.zeros_like(p) for p in params))
    sums, (outs, dxs) = lax.scan(step, zero, (xs, gs))
    output = outs.reshape(TOKENS, D).astype(jnp.bfloat16)
    input_grad = dxs.reshape(TOKENS, D).astype(jnp.bfloat16)
    return (output, input_grad, sums[0], sums[1], sums[2], sums[3], sums[4], sums[5], sums[6], sums[7], sums[8], sums[9])
```

```python
from functools import partial
import math

import jax
import jax.numpy as jnp
from jax import lax
from jax.experimental import pallas as pl
from jax.experimental.pallas import tpu as pltpu
from jax.sharding import Mesh, PartitionSpec as P

HEADS = 32
ROT = 32
EPS = 1e-05
NEG = -1e30
BLOCK_Q = 256

BF = jnp.bfloat16
F32 = jnp.float32


def dot(a, b):
    return jnp.dot(a, b, preferred_element_type=F32)


def dot_t(a, b):
    return lax.dot_general(a, b, (((1,), (1,)), ((), ())), preferred_element_type=F32)


def t_dot(a, b):
    return lax.dot_general(a, b, (((0,), (0,)), ((), ())), preferred_element_type=F32)


def ring_pairs(order, step):
    n = len(order)
    return [(order[i], order[(i + step) % n]) for i in range(n)]


def ring_gather(own, axis, order):
    n = len(order)
    blocks = {0: own}
    up = down = own
    half = own.shape[0] // 2
    for step in range(1, n // 2 + 1):
        if 2 * step == n:
            first = lax.ppermute(up[:half], axis, ring_pairs(order, 1))
            second = lax.ppermute(down[half:], axis, ring_pairs(order, -1))
            blocks[step] = jnp.concatenate([first, second], 0)
        else:
            up = lax.ppermute(up, axis, ring_pairs(order, 1))
            down = lax.ppermute(down, axis, ring_pairs(order, -1))
            blocks[-step] = up
            blocks[step] = down
    return blocks


def ring_scatter(parts, axis, order):
    n = len(order)
    rows = parts[0].shape[0]
    half = rows // 2
    low = high = None
    for step in range(n // 2, 0, -1):
        if 2 * step == n:
            low = lax.ppermute(parts[step][:half].astype(BF), axis, ring_pairs(order, -1))
            high = lax.ppermute(parts[step][half:].astype(BF), axis, ring_pairs(order, 1))
        else:
            to_low = joined(parts[-step], low, True).astype(BF)
            to_high = joined(parts[step], high, False).astype(BF)
            low = lax.ppermute(to_low, axis, ring_pairs(order, -1))
            high = lax.ppermute(to_high, axis, ring_pairs(order, 1))
    return joined(joined(parts[0], low, True), high, False)


def joined(part, arrived, first):
    part = part.astype(F32)
    arrived = arrived.astype(F32)
    if arrived.shape[0] == part.shape[0]:
        return part + arrived
    half = arrived.shape[0]
    if first:
        return jnp.concatenate([part[:half] + arrived, part[half:]], 0)
    return jnp.concatenate([part[:half], part[half:] + arrived], 0)


def swap(value):
    return lax.ppermute(value, "core", [(0, 1), (1, 0)])


def turn(values, cosine, sine_a, sine_b):
    width = values.shape[1]
    return (
        values * cosine
        + pltpu.roll(values, width - ROT // 2, 1) * sine_a
        + pltpu.roll(values, ROT // 2, 1) * sine_b
    )


def head_mask(shape, head, head_dim):
    lane = lax.broadcasted_iota(jnp.int32, shape, 1)
    return (lane >= head * head_dim) & (lane < (head + 1) * head_dim)


def attend_kernel(heads, head_dim, span, order_ref, qkv_ref, cos_ref, sin_a_ref, sin_b_ref, att_ref, sorted_ref, out_scr):
    seq_len = qkv_ref.shape[1]
    width = heads * head_dim
    for slot in range(seq_len // span):
        rows = pl.ds(pl.multiple_of(order_ref[slot] * span, span), span)
        here = pl.ds(slot * span, span)
        tables = (cos_ref[here, :], sin_a_ref[here, :], sin_b_ref[here, :])
        query = turn(qkv_ref[0, rows, 0:width], *tables).astype(BF)
        sorted_ref[0, here, 0:width] = (query.astype(F32) * (head_dim**-0.5)).astype(BF)
        sorted_ref[0, here, width : 2 * width] = turn(qkv_ref[0, rows, width : 2 * width], *tables).astype(BF)
        sorted_ref[0, here, 2 * width :] = qkv_ref[0, rows, 2 * width :].astype(BF)
    block = min(BLOCK_Q, seq_len)
    for i in range(seq_len // block):
        extent = (i + 1) * block
        here = pl.ds(i * block, block)
        queries = sorted_ref[0, here, 0:width]
        keys = sorted_ref[0, 0:extent, width : 2 * width]
        values = sorted_ref[0, 0:extent, 2 * width :]
        row = lax.broadcasted_iota(jnp.int32, (block, extent), 0) + i * block
        col = lax.broadcasted_iota(jnp.int32, (block, extent), 1)
        total = jnp.zeros((block, width), F32)
        for head in range(heads):
            mask = head_mask((block, width), head, head_dim)
            scores = dot_t(jnp.where(mask, queries, jnp.zeros_like(queries)), keys)
            scores = jnp.where(col <= row, scores, NEG)
            top = jnp.max(scores, 1, keepdims=True)
            weights = jnp.exp(scores - top)
            norm = 1.0 / jnp.sum(weights, 1, keepdims=True)
            probs = (weights * norm).astype(BF)
            total = jnp.where(mask, dot(probs, values), total)
        out_scr[here, :] = total.astype(BF)
    for slot in range(seq_len // span):
        rows = pl.ds(pl.multiple_of(order_ref[slot] * span, span), span)
        att_ref[0, rows, :] = out_scr[slot * span : (slot + 1) * span, :]


def attend_back_kernel(
    heads, head_dim, span, order_ref, sorted_ref, grad_ref, cos_ref, sin_a_ref, sin_b_ref, out_ref, grad_scr, key_scr, value_scr
):
    seq_len = sorted_ref.shape[1]
    width = heads * head_dim
    for slot in range(seq_len // span):
        rows = pl.ds(pl.multiple_of(order_ref[slot] * span, span), span)
        grad_scr[slot * span : (slot + 1) * span, :] = grad_ref[0, rows, :]
    key_scr[...] = jnp.zeros_like(key_scr)
    value_scr[...] = jnp.zeros_like(value_scr)
    block = min(BLOCK_Q, seq_len)

    def put(slot, first, values):
        rows = pl.ds(pl.multiple_of(order_ref[slot] * span, span), span)
        out_ref[0, rows, first : first + width] = values.astype(BF)

    def tables(here):
        return (cos_ref[here, :], -sin_a_ref[here, :], -sin_b_ref[here, :])

    for i in range(seq_len // block):
        extent = (i + 1) * block
        here = pl.ds(i * block, block)
        queries = sorted_ref[0, here, 0:width]
        grads = grad_scr[here, :]
        keys = sorted_ref[0, 0:extent, width : 2 * width]
        values = sorted_ref[0, 0:extent, 2 * width :]
        key = lax.broadcasted_iota(jnp.int32, (extent, block), 0)
        query = lax.broadcasted_iota(jnp.int32, (extent, block), 1) + i * block
        query_grad = jnp.zeros((block, width), F32)
        for head in range(heads):
            mask = head_mask((block, width), head, head_dim)
            own_queries = jnp.where(mask, queries, jnp.zeros_like(queries))
            own_grads = jnp.where(mask, grads, jnp.zeros_like(grads))
            scores = jnp.where(key <= query, dot_t(keys, own_queries), NEG)
            weights = jnp.exp(scores - jnp.max(scores, 0, keepdims=True))
            probs = weights * (1.0 / jnp.sum(weights, 0, keepdims=True))
            probs_grad = dot_t(values, own_grads)
            delta = jnp.sum(probs * probs_grad, 0, keepdims=True)
            score_grad = (probs * (probs_grad - delta)).astype(BF)
            value_scr[0:extent, :] += dot(probs.astype(BF), own_grads)
            key_scr[0:extent, :] += dot(score_grad, own_queries)
            query_grad = jnp.where(mask, t_dot(score_grad, keys), query_grad)
        query_grad = turn(query_grad * (head_dim**-0.5), *tables(here))
        for j in range(block // span):
            put(i * (block // span) + j, 0, query_grad[j * span : (j + 1) * span])
    for slot in range(seq_len // span):
        here = pl.ds(slot * span, span)
        put(slot, width, turn(key_scr[here, :], *tables(here)))
        put(slot, 2 * width, value_scr[here, :])


def attend(order, qkv, tables, heads, head_dim, span):
    count, seq_len, wide = qkv.shape
    width = wide // 3
    whole = pl.BlockSpec((seq_len, width), lambda s, o: (0, 0))
    return pl.pallas_call(
        partial(attend_kernel, heads, head_dim, span),
        grid_spec=pltpu.PrefetchScalarGridSpec(
            num_scalar_prefetch=1,
            grid=(count,),
            in_specs=[pl.BlockSpec((1, seq_len, wide), lambda s, o: (s, 0, 0)), whole, whole, whole],
            out_specs=[
                pl.BlockSpec((1, seq_len, width), lambda s, o: (s, 0, 0)),
                pl.BlockSpec((1, seq_len, wide), lambda s, o: (s, 0, 0)),
            ],
            scratch_shapes=[pltpu.VMEM((seq_len, width), BF)],
        ),
        out_shape=[
            jax.ShapeDtypeStruct((count, seq_len, width), BF),
            jax.ShapeDtypeStruct((count, seq_len, wide), BF),
        ],
        compiler_params=pltpu.CompilerParams(vmem_limit_bytes=56 * 2**20),
        cost_estimate=pl.CostEstimate(
            flops=8 * count * heads * seq_len * seq_len * head_dim,
            bytes_accessed=count * seq_len * wide * 8,
            transcendentals=count * heads * seq_len * seq_len,
        ),
        name="attend",
    )(order, qkv, *tables)


def attend_back(order, kept, grads, tables, heads, head_dim, span):
    count, seq_len, wide = kept.shape
    width = wide // 3
    whole = pl.BlockSpec((seq_len, width), lambda s, o: (0, 0))
    return pl.pallas_call(
        partial(attend_back_kernel, heads, head_dim, span),
        grid_spec=pltpu.PrefetchScalarGridSpec(
            num_scalar_prefetch=1,
            grid=(count,),
            in_specs=[
                pl.BlockSpec((1, seq_len, wide), lambda s, o: (s, 0, 0)),
                pl.BlockSpec((1, seq_len, width), lambda s, o: (s, 0, 0)),
                whole,
                whole,
                whole,
            ],
            out_specs=pl.BlockSpec((1, seq_len, wide), lambda s, o: (s, 0, 0)),
            scratch_shapes=[
                pltpu.VMEM((seq_len, width), BF),
                pltpu.VMEM((seq_len, width), F32),
                pltpu.VMEM((seq_len, width), F32),
            ],
        ),
        out_shape=jax.ShapeDtypeStruct((count, seq_len, wide), BF),
        compiler_params=pltpu.CompilerParams(vmem_limit_bytes=56 * 2**20),
        cost_estimate=pl.CostEstimate(
            flops=20 * count * heads * seq_len * seq_len * head_dim,
            bytes_accessed=count * seq_len * wide * 6,
            transcendentals=count * heads * seq_len * seq_len,
        ),
        name="attend_back",
    )(order, kept, grads, *tables)


def norm_parts(rows):
    rows = rows.astype(F32)
    mean = jnp.mean(rows, -1, keepdims=True)
    centred = rows - mean
    scale = lax.rsqrt(jnp.mean(centred * centred, -1, keepdims=True) + EPS)
    return centred * scale, scale


def per_device(
    inputs,
    span_table,
    ln_gain,
    ln_bias,
    qkv_weight,
    qkv_bias,
    out_weight,
    out_bias,
    fc1_weight,
    fc1_bias,
    fc2_weight,
    fc2_bias,
    cotangent,
):
    rows, width = inputs.shape
    head_dim = width // HEADS
    n_q, n_z = lax.axis_size("q"), lax.axis_size("ctx")
    n_t = 2 * n_z
    n_all = n_q * n_t
    q, core, z = lax.axis_index("q"), lax.axis_index("core"), lax.axis_index("ctx")
    t = core * n_z + z
    span = rows // 2
    seq_len = rows * n_z
    heads = HEADS // n_t
    own_width = heads * head_dim
    hidden_all = fc2_weight.shape[0] * n_all
    units = fc2_weight.shape[0]
    own_units = units * n_q
    every = ("q", "core", "ctx")
    z_order = list(range(n_z))
    q_order = [0, 1, 3, 2] if n_q == 4 else list(range(n_q))
    places = jnp.array([q_order.index(i) for i in range(n_q)], jnp.int32)
    q_place = places[q]
    q_ring = jnp.array(q_order, jnp.int32)

    def q_at(offset):
        return q_ring[(q_place + offset) % n_q]

    small = jnp.concatenate([ln_gain, ln_bias, out_bias, fc2_bias, qkv_bias, fc1_bias])
    small = lax.all_gather(small, every, axis=0)
    cuts = [ln_gain.shape[0], ln_bias.shape[0], out_bias.shape[0], fc2_bias.shape[0], qkv_bias.shape[0], fc1_bias.shape[0]]
    starts = [sum(cuts[:i]) for i in range(len(cuts))]
    gain, shift, b_out, b_down, b_qkv, b_up = (
        small[:, s : s + c].astype(F32) for s, c in zip(starts, cuts)
    )
    gain, shift, b_out, b_down = (v.reshape(1, width) for v in (gain, shift, b_out, b_down))
    b_qkv = lax.dynamic_index_in_dim(b_qkv.reshape(3, heads, n_t, head_dim), t, 2, False).reshape(1, 3 * own_width)
    b_up = lax.dynamic_index_in_dim(b_up.reshape(n_q, n_t, units), t, 1, False).reshape(1, own_units)

    def q_gather(block):
        blocks = ring_gather(block, "q", q_order)
        whole = jnp.zeros((n_q,) + block.shape, block.dtype)
        for offset, value in blocks.items():
            whole = lax.dynamic_update_index_in_dim(whole, value, q_at(offset), 0)
        return whole.reshape((n_q * block.shape[0],) + block.shape[1:])

    def q_scatter(part):
        part = part.reshape((n_q, part.shape[0] // n_q) + part.shape[1:])
        offsets = [0] + [o for s in range(1, n_q // 2 + 1) for o in ((s,) if 2 * s == n_q else (-s, s))]
        parts = {o: lax.dynamic_index_in_dim(part, q_at(o), 0, False) for o in offsets}
        return ring_scatter(parts, "q", q_order)

    def rows_to_columns(blocks):
        _, r, c = blocks.shape
        blocks = blocks.reshape(2, n_z, r, c)
        mine = lax.dynamic_index_in_dim(blocks, core, 0, False)
        other = swap(lax.dynamic_index_in_dim(blocks, 1 - core, 0, False))
        both = jnp.stack([mine, other], 1)
        whole = jnp.zeros((2, n_z, r, c), blocks.dtype)
        for shift_by in range(n_z):
            piece = lax.dynamic_index_in_dim(both, (z + shift_by) % n_z, 0, False)
            if shift_by:
                piece = lax.ppermute(piece, "ctx", ring_pairs(z_order, shift_by))
            source = (z - shift_by) % n_z
            for rank, at in ((0, core), (1, 1 - core)):
                whole = lax.dynamic_update_slice(whole, piece[rank][None, None], (at, source, 0, 0))
        return whole.reshape(n_t * r, c)

    def columns_to_rows(part):
        c = part.shape[1]
        r = part.shape[0] // n_t
        part = part.reshape(2, n_z, r, c)
        mine = lax.dynamic_index_in_dim(part, core, 0, False)
        other = swap(lax.dynamic_index_in_dim(part, 1 - core, 0, False))
        both = jnp.stack([mine, other], 1)
        whole = jnp.zeros((2, n_z, r, c), part.dtype)
        for shift_by in range(n_z):
            piece = lax.dynamic_index_in_dim(both, (z + shift_by) % n_z, 0, False)
            if shift_by:
                piece = lax.ppermute(piece, "ctx", ring_pairs(z_order, shift_by))
            source = (z - shift_by) % n_z
            for rank, at in ((0, core), (1, 1 - core)):
                whole = lax.dynamic_update_slice(whole, piece[rank][None, None], (at, source, 0, 0))
        return whole.reshape(n_t, r, c)

    d_rows = qkv_weight.shape[0]
    qkv_blocks = qkv_weight.reshape(d_rows, 3, heads, n_t, head_dim).transpose(3, 0, 1, 2, 4).reshape(n_t, d_rows, 3 * own_width)
    up_blocks = fc1_weight.reshape(d_rows, n_q, n_t, units).transpose(2, 0, 1, 3).reshape(n_t, d_rows, own_units)
    w_qkv = q_gather(rows_to_columns(qkv_blocks))
    w_up = q_gather(rows_to_columns(up_blocks))
    whole_heads = out_weight.shape[0] == head_dim
    if whole_heads:
        w_out = q_gather(out_weight)
    else:
        w_out = lax.all_gather(out_weight, every, axis=0, tiled=True).reshape(heads, n_t, head_dim, width)
        w_out = lax.dynamic_index_in_dim(w_out, t, 1, False).reshape(own_width, width)
    w_down = q_gather(fc2_weight)

    offsets = [0] + [o for s in range(1, n_z // 2 + 1) for o in ((s,) if 2 * s == n_z else (-s, s))]

    def line_gather(block):
        blocks = ring_gather(block, "ctx", z_order)
        mine = [blocks[o] for o in offsets]
        return jnp.concatenate(mine + [swap(b) for b in mine], 0)

    def line_scatter(part):
        other = swap(part[seq_len:].astype(BF))
        mine = part[:seq_len].astype(F32) + other.astype(F32)
        parts = {o: mine[i * rows : (i + 1) * rows] for i, o in enumerate(offsets)}
        return ring_scatter(parts, "ctx", z_order)

    x_all = line_gather(inputs)
    g_all = line_gather(cotangent)

    spans = jnp.concatenate([lax.dynamic_index_in_dim(span_table, (z + o) % n_z, 0, False) for o in offsets])
    n_spans = 2 * n_z
    order = jnp.sum(
        jnp.where(spans[None, :] == jnp.arange(n_spans, dtype=jnp.int32)[:, None], jnp.arange(n_spans, dtype=jnp.int32)[None, :], 0),
        1,
        dtype=jnp.int32,
    )
    half = ROT // 2
    lane = jnp.arange(own_width, dtype=jnp.int32)[None, :] % head_dim
    position = jnp.arange(seq_len, dtype=jnp.int32).astype(F32)[:, None]
    freqs = jnp.where(lane < ROT, jnp.exp((lane % half).astype(F32) * (-2.0 * math.log(10000.0) / ROT)), 0.0)
    angles = position * freqs
    sine = jnp.sin(angles)
    tables = (jnp.cos(angles), jnp.where(lane < half, -sine, 0.0), jnp.where((lane >= half) & (lane < ROT), sine, 0.0))

    xhat, _ = norm_parts(x_all)
    hidden = (xhat * gain + shift).astype(BF)
    qkv = (dot(hidden, w_qkv) + b_qkv).reshape(2, seq_len, 3 * own_width)
    attended, kept = attend(order, qkv, tables, heads, head_dim, span)
    attended = attended.reshape(2 * seq_len, own_width)
    pre = dot(hidden, w_up) + b_up
    act, gelu_back = jax.vjp(partial(jax.nn.gelu, approximate=True), pre)
    act = act.astype(BF)
    out_part = dot(attended, w_out) + dot(act, w_down)
    x_own = inputs.astype(F32)
    output = (x_own + line_scatter(out_part.astype(BF)) + b_out + b_down).astype(BF)

    pre_grad = gelu_back(dot_t(g_all, w_down))[0].astype(BF)
    down_part = t_dot(act, g_all).astype(BF)
    up_part = t_dot(hidden, pre_grad).astype(BF)
    up_bias_part = jnp.sum(pre_grad.astype(F32), 0)

    attended_grad = dot_t(g_all, w_out).astype(BF).reshape(2, seq_len, own_width)
    out_w_part = t_dot(attended, g_all).astype(BF)
    qkv_grad = attend_back(order, kept, attended_grad, tables, heads, head_dim, span).reshape(2 * seq_len, 3 * own_width)
    normed_part = (dot_t(qkv_grad, w_qkv) + dot_t(pre_grad, w_up)).astype(BF)
    qkv_part = t_dot(hidden, qkv_grad).astype(BF)
    qkv_bias_part = jnp.sum(qkv_grad.astype(F32), 0)

    fc2_weight_grad = q_scatter(down_part)
    fc1_weight_grad = (
        columns_to_rows(q_scatter(up_part).astype(BF))
        .astype(F32)
        .reshape(n_t, d_rows, n_q, units)
        .transpose(1, 2, 0, 3)
        .reshape(d_rows, hidden_all)
    )
    qkv_weight_grad = (
        columns_to_rows(q_scatter(qkv_part).astype(BF))
        .astype(F32)
        .reshape(n_t, d_rows, 3, heads, head_dim)
        .transpose(1, 2, 3, 0, 4)
        .reshape(d_rows, 3 * width)
    )
    if whole_heads:
        out_weight_grad = q_scatter(out_w_part)
    else:
        spread = jnp.zeros((heads, n_t, head_dim, width), F32)
        spread = lax.dynamic_update_slice(spread, out_w_part.astype(F32).reshape(heads, 1, head_dim, width), (0, t, 0, 0))
        out_weight_grad = lax.psum_scatter(spread.reshape(width, width), every, scatter_dimension=0, tiled=True)

    normed_grad = line_scatter(normed_part)
    g_own = cotangent.astype(F32)
    xhat_own, scale_own = norm_parts(inputs)
    m = normed_grad * gain
    x_grad = (m - jnp.mean(m, -1, keepdims=True) - xhat_own * jnp.mean(m * xhat_own, -1, keepdims=True)) * scale_own
    input_grad = (g_own + x_grad).astype(BF)

    def by_owner(vector):
        return vector.reshape(n_all, vector.shape[0] // n_all)

    qkv_spread = lax.dynamic_update_slice(
        jnp.zeros((3, heads, n_t, head_dim), F32), qkv_bias_part.reshape(3, heads, 1, head_dim), (0, 0, t, 0)
    ).reshape(-1)
    up_spread = lax.dynamic_update_slice(jnp.zeros((n_q, n_t, units), F32), up_bias_part.reshape(n_q, 1, units), (0, t, 0)).reshape(-1)
    vectors = jnp.concatenate(
        [
            by_owner(jnp.sum(normed_grad * xhat_own, 0)),
            by_owner(jnp.sum(normed_grad, 0)),
            by_owner(jnp.sum(g_own, 0)),
            by_owner(qkv_spread),
            by_owner(up_spread),
        ],
        1,
    )
    wide = vectors.shape[1]
    cube = vectors.reshape(n_q, 2, n_z, wide)
    cube = lax.dynamic_index_in_dim(cube, core, 1, False) + swap(lax.dynamic_index_in_dim(cube, 1 - core, 1, False))
    line = sum_blocks(cube, "q", q, n_q)
    line = sum_blocks(line, "ctx", z, n_z)
    cuts = [ln_gain.shape[0], ln_bias.shape[0], out_bias.shape[0], qkv_bias.shape[0], fc1_bias.shape[0]]
    starts = [sum(cuts[:i]) for i in range(len(cuts))]
    gain_grad, shift_grad, bias_grad, qkv_bias_grad, fc1_bias_grad = (line[s : s + c] for s, c in zip(starts, cuts))
    return (
        output,
        input_grad,
        gain_grad,
        shift_grad,
        qkv_weight_grad,
        qkv_bias_grad,
        out_weight_grad,
        bias_grad,
        fc1_weight_grad,
        fc1_bias_grad,
        fc2_weight_grad,
        bias_grad,
    )


def sum_blocks(blocks, axis, index, n):
    total = lax.dynamic_index_in_dim(blocks, index, 0, False)
    for shift_by in range(1, n):
        piece = lax.dynamic_index_in_dim(blocks, (index + shift_by) % n, 0, False)
        total = total + lax.ppermute(piece, axis, ring_pairs(list(range(n)), shift_by))
    return total


def solution(mesh):
    n_dp, n_ctx = mesh.devices.shape
    inner = Mesh(mesh.devices.reshape(n_dp // 2, 2, n_ctx), ("q", "core", "ctx"))
    every = ("q", "core", "ctx")
    matrix, vector = P(every, None), P(every)
    return jax.shard_map(
        per_device,
        mesh=inner,
        in_specs=(
            matrix,
            P(),
            vector,
            vector,
            matrix,
            vector,
            matrix,
            vector,
            matrix,
            vector,
            matrix,
            vector,
            matrix,
        ),
        out_specs=(matrix, matrix, vector, vector, matrix, vector, matrix, vector, matrix, vector, matrix, vector),
        check_vma=False,
    )
```

```python
from functools import partial
import math

import jax
import jax.numpy as jnp
from jax import lax
from jax.experimental import pallas as pl
from jax.experimental.pallas import tpu as pltpu
from jax.sharding import Mesh, PartitionSpec as P

HEADS = 32
ROT = 32
EPS = 1e-05
NEG = -1e30
BLOCK_Q = 256

BF = jnp.bfloat16
F32 = jnp.float32


def dot(a, b):
    return jnp.dot(a, b, preferred_element_type=F32)


def dot_t(a, b):
    return lax.dot_general(a, b, (((1,), (1,)), ((), ())), preferred_element_type=F32)


def t_dot(a, b):
    return lax.dot_general(a, b, (((0,), (0,)), ((), ())), preferred_element_type=F32)


def ring_pairs(order, step):
    n = len(order)
    return [(order[i], order[(i + step) % n]) for i in range(n)]


def swap(value):
    return lax.ppermute(value, "core", [(0, 1), (1, 0)])


def turn(values, cosine, sine_a, sine_b):
    width = values.shape[1]
    return (
        values * cosine
        + pltpu.roll(values, width - ROT // 2, 1) * sine_a
        + pltpu.roll(values, ROT // 2, 1) * sine_b
    )


def head_mask(shape, head, head_dim):
    lane = lax.broadcasted_iota(jnp.int32, shape, 1)
    return (lane >= head * head_dim) & (lane < (head + 1) * head_dim)


def attend_kernel(heads, head_dim, span, order_ref, qkv_ref, cos_ref, sin_a_ref, sin_b_ref, att_ref, sorted_ref, out_scr):
    seq_len = qkv_ref.shape[1]
    width = heads * head_dim
    for slot in range(seq_len // span):
        rows = pl.ds(pl.multiple_of(order_ref[slot] * span, span), span)
        here = pl.ds(slot * span, span)
        tables = (cos_ref[here, :], sin_a_ref[here, :], sin_b_ref[here, :])
        query = turn(qkv_ref[0, rows, 0:width], *tables).astype(BF)
        sorted_ref[0, here, 0:width] = (query.astype(F32) * (head_dim**-0.5)).astype(BF)
        sorted_ref[0, here, width : 2 * width] = turn(qkv_ref[0, rows, width : 2 * width], *tables).astype(BF)
        sorted_ref[0, here, 2 * width :] = qkv_ref[0, rows, 2 * width :].astype(BF)
    block = min(BLOCK_Q, seq_len)
    for i in range(seq_len // block):
        extent = (i + 1) * block
        here = pl.ds(i * block, block)
        queries = sorted_ref[0, here, 0:width]
        keys = sorted_ref[0, 0:extent, width : 2 * width]
        values = sorted_ref[0, 0:extent, 2 * width :]
        row = lax.broadcasted_iota(jnp.int32, (block, extent), 0) + i * block
        col = lax.broadcasted_iota(jnp.int32, (block, extent), 1)
        total = jnp.zeros((block, width), F32)
        for head in range(heads):
            mask = head_mask((block, width), head, head_dim)
            scores = dot_t(jnp.where(mask, queries, jnp.zeros_like(queries)), keys)
            scores = jnp.where(col <= row, scores, NEG)
            top = jnp.max(scores, 1, keepdims=True)
            weights = jnp.exp(scores - top)
            norm = 1.0 / jnp.sum(weights, 1, keepdims=True)
            probs = (weights * norm).astype(BF)
            total = jnp.where(mask, dot(probs, values), total)
        out_scr[here, :] = total.astype(BF)
    for slot in range(seq_len // span):
        rows = pl.ds(pl.multiple_of(order_ref[slot] * span, span), span)
        att_ref[0, rows, :] = out_scr[slot * span : (slot + 1) * span, :]


def attend_back_kernel(
    heads, head_dim, span, order_ref, sorted_ref, grad_ref, cos_ref, sin_a_ref, sin_b_ref, out_ref, grad_scr, key_scr, value_scr
):
    seq_len = sorted_ref.shape[1]
    width = heads * head_dim
    for slot in range(seq_len // span):
        rows = pl.ds(pl.multiple_of(order_ref[slot] * span, span), span)
        grad_scr[slot * span : (slot + 1) * span, :] = grad_ref[0, rows, :]
    key_scr[...] = jnp.zeros_like(key_scr)
    value_scr[...] = jnp.zeros_like(value_scr)
    block = min(BLOCK_Q, seq_len)

    def put(slot, first, values):
        rows = pl.ds(pl.multiple_of(order_ref[slot] * span, span), span)
        out_ref[0, rows, first : first + width] = values.astype(BF)

    def tables(here):
        return (cos_ref[here, :], -sin_a_ref[here, :], -sin_b_ref[here, :])

    for i in range(seq_len // block):
        extent = (i + 1) * block
        here = pl.ds(i * block, block)
        queries = sorted_ref[0, here, 0:width]
        grads = grad_scr[here, :]
        keys = sorted_ref[0, 0:extent, width : 2 * width]
        values = sorted_ref[0, 0:extent, 2 * width :]
        key = lax.broadcasted_iota(jnp.int32, (extent, block), 0)
        query = lax.broadcasted_iota(jnp.int32, (extent, block), 1) + i * block
        query_grad = jnp.zeros((block, width), F32)
        for head in range(heads):
            mask = head_mask((block, width), head, head_dim)
            own_queries = jnp.where(mask, queries, jnp.zeros_like(queries))
            own_grads = jnp.where(mask, grads, jnp.zeros_like(grads))
            scores = jnp.where(key <= query, dot_t(keys, own_queries), NEG)
            weights = jnp.exp(scores - jnp.max(scores, 0, keepdims=True))
            probs = weights * (1.0 / jnp.sum(weights, 0, keepdims=True))
            probs_grad = dot_t(values, own_grads)
            delta = jnp.sum(probs * probs_grad, 0, keepdims=True)
            score_grad = (probs * (probs_grad - delta)).astype(BF)
            value_scr[0:extent, :] += dot(probs.astype(BF), own_grads)
            key_scr[0:extent, :] += dot(score_grad, own_queries)
            query_grad = jnp.where(mask, t_dot(score_grad, keys), query_grad)
        query_grad = turn(query_grad * (head_dim**-0.5), *tables(here))
        for j in range(block // span):
            put(i * (block // span) + j, 0, query_grad[j * span : (j + 1) * span])
    for slot in range(seq_len // span):
        here = pl.ds(slot * span, span)
        put(slot, width, turn(key_scr[here, :], *tables(here)))
        put(slot, 2 * width, value_scr[here, :])


def attend(order, qkv, tables, heads, head_dim, span):
    count, seq_len, wide = qkv.shape
    width = wide // 3
    whole = pl.BlockSpec((seq_len, width), lambda s, o: (0, 0))
    return pl.pallas_call(
        partial(attend_kernel, heads, head_dim, span),
        grid_spec=pltpu.PrefetchScalarGridSpec(
            num_scalar_prefetch=1,
            grid=(count,),
            in_specs=[pl.BlockSpec((1, seq_len, wide), lambda s, o: (s, 0, 0)), whole, whole, whole],
            out_specs=[
                pl.BlockSpec((1, seq_len, width), lambda s, o: (s, 0, 0)),
                pl.BlockSpec((1, seq_len, wide), lambda s, o: (s, 0, 0)),
            ],
            scratch_shapes=[pltpu.VMEM((seq_len, width), BF)],
        ),
        out_shape=[
            jax.ShapeDtypeStruct((count, seq_len, width), BF),
            jax.ShapeDtypeStruct((count, seq_len, wide), BF),
        ],
        compiler_params=pltpu.CompilerParams(vmem_limit_bytes=40 * 2**20),
        cost_estimate=pl.CostEstimate(
            flops=8 * count * heads * seq_len * seq_len * head_dim,
            bytes_accessed=count * seq_len * wide * 8,
            transcendentals=count * heads * seq_len * seq_len,
        ),
        name="attend",
    )(order, qkv, *tables)


def attend_back(order, kept, grads, tables, heads, head_dim, span):
    count, seq_len, wide = kept.shape
    width = wide // 3
    whole = pl.BlockSpec((seq_len, width), lambda s, o: (0, 0))
    return pl.pallas_call(
        partial(attend_back_kernel, heads, head_dim, span),
        grid_spec=pltpu.PrefetchScalarGridSpec(
            num_scalar_prefetch=1,
            grid=(count,),
            in_specs=[
                pl.BlockSpec((1, seq_len, wide), lambda s, o: (s, 0, 0)),
                pl.BlockSpec((1, seq_len, width), lambda s, o: (s, 0, 0)),
                whole,
                whole,
                whole,
            ],
            out_specs=pl.BlockSpec((1, seq_len, wide), lambda s, o: (s, 0, 0)),
            scratch_shapes=[
                pltpu.VMEM((seq_len, width), BF),
                pltpu.VMEM((seq_len, width), F32),
                pltpu.VMEM((seq_len, width), F32),
            ],
        ),
        out_shape=jax.ShapeDtypeStruct((count, seq_len, wide), BF),
        compiler_params=pltpu.CompilerParams(vmem_limit_bytes=40 * 2**20),
        cost_estimate=pl.CostEstimate(
            flops=20 * count * heads * seq_len * seq_len * head_dim,
            bytes_accessed=count * seq_len * wide * 6,
            transcendentals=count * heads * seq_len * seq_len,
        ),
        name="attend_back",
    )(order, kept, grads, *tables)


def after(value, *others):
    return lax.optimization_barrier((value,) + others)[0]


def whole_block(shape):
    return pl.BlockSpec(shape, lambda *_: (0,) * len(shape))


def params(limit):
    return pltpu.CompilerParams(vmem_limit_bytes=limit * 2**20)


def cost(flops, nbytes):
    return pl.CostEstimate(flops=flops, bytes_accessed=nbytes, transcendentals=0)


ANYWHERE = pl.BlockSpec(memory_space=pl.ANY)
SCALARS = pl.BlockSpec(memory_space=pltpu.SMEM)
VMEM = pl.BlockSpec(memory_space=pltpu.VMEM)
ROWS = 256


def gathered(own, axis, order):
    n = len(order)
    up_pairs, down_pairs = ring_pairs(order, 1), ring_pairs(order, -1)
    out = [(0, 0, own)]
    up = down = own
    half = own.shape[0] // 2
    for step in range(1, n // 2 + 1):
        if 2 * step == n:
            out.append((step, 0, lax.ppermute(up[:half], axis, up_pairs)))
            out.append((step, half, lax.ppermute(down[half:], axis, down_pairs)))
        else:
            up, down = lax.ppermute(up, axis, up_pairs), lax.ppermute(down, axis, down_pairs)
            out += [(-step, 0, up), (step, 0, down)]
    return out


def to_blocks_kernel(n_q, n_t, heads, head_dim, units, at_ref, qkv_ref, up_ref, *out_refs):
    n_z = n_t // 2
    width = heads * head_dim
    core, z = at_ref[0], at_ref[1]
    rows = qkv_ref.shape[0]
    low = lax.broadcasted_iota(jnp.int32, (rows, 128), 1) < head_dim
    per = 128 // head_dim
    for c in range(2):
        for s in range(n_z):
            out_ref = out_refs[c * n_z + s]
            t = lax.rem(core + c, 2) * n_z + lax.rem(z + s, n_z)
            odd = lax.rem(t, per)
            for which in range(3):
                for j in range(0, heads, per):
                    tiles = []
                    for i in range(per):
                        first = (which * heads + j + i) * n_t * head_dim + (t // per) * 128
                        tile = qkv_ref[:, pl.ds(pl.multiple_of(first, 128), 128)].astype(F32)
                        tiles.append(tile)
                    even = jnp.where(low, tiles[0], pltpu.roll(tiles[1], head_dim, 1))
                    uneven = jnp.where(low, pltpu.roll(tiles[0], head_dim, 1), tiles[1])
                    at = which * width + j * head_dim
                    out_ref[:, at : at + 128] = jnp.where(odd == 0, even, uneven).astype(BF)
            for q in range(n_q):
                at = 3 * width + q * units
                if units % 128 == 0:
                    first = pl.multiple_of((q * n_t + t) * units, 128)
                    out_ref[:, at : at + units] = up_ref[:, pl.ds(first, units)]
                else:
                    for k in range(n_t):

                        @pl.when(t == k)
                        def _(at=at, q=q, k=k):
                            first = (q * n_t + k) * units
                            out_ref[:, at : at + units] = up_ref[:, first : first + units]


def to_blocks(at, qkv, up, n_q, n_t, heads, head_dim, units):
    rows = qkv.shape[0]
    wide = 3 * heads * head_dim + n_q * units
    return pl.pallas_call(
        partial(to_blocks_kernel, n_q, n_t, heads, head_dim, units),
        in_specs=[SCALARS, VMEM, VMEM],
        out_specs=[VMEM] * n_t,
        out_shape=[jax.ShapeDtypeStruct((rows, wide), BF)] * n_t,
        compiler_params=params(16),
        cost_estimate=cost(0, 4 * rows * wide * n_t),
        name="to_blocks",
    )(at, qkv, up)


def stack_rows_kernel(n_z, at_ref, *refs):
    pieces, out_ref = refs[:-1], refs[-1]
    rows = pieces[0].shape[0]
    core, z = at_ref[0], at_ref[1]
    for c in range(2):
        for s in range(n_z):
            block = lax.rem(core + c, 2) * n_z + lax.rem(z - s + n_z, n_z)
            out_ref[pl.ds(pl.multiple_of(block * rows, 16), rows), :] = pieces[c * n_z + s][...]


def stack_rows(at, pieces):
    rows, columns = pieces[0].shape
    n_t = len(pieces)
    return pl.pallas_call(
        partial(stack_rows_kernel, n_t // 2),
        in_specs=[SCALARS] + [VMEM] * n_t,
        out_specs=VMEM,
        out_shape=jax.ShapeDtypeStruct((n_t * rows, columns), BF),
        compiler_params=params(16),
        cost_estimate=cost(0, 4 * n_t * rows * columns),
        name="stack_rows",
    )(at, *pieces)


def last_sum_kernel(n_z, at_ref, part_ref, low_ref, high_ref, *out_refs):
    rows = out_refs[0].shape[0]
    core, z = at_ref[0], at_ref[1]
    for c in range(2):
        for s in range(n_z):
            block = lax.rem(core + c, 2) * n_z + lax.rem(z + s, n_z)
            here = pl.ds(pl.multiple_of(block * rows, 16), rows)
            total = part_ref[here, :].astype(F32) + low_ref[here, :].astype(F32) + high_ref[here, :].astype(F32)
            out_refs[c * n_z + s][...] = total.astype(BF)


def last_sum(at, parts, low, high, n_t):
    count, columns = low.shape
    rows = count // n_t
    return pl.pallas_call(
        partial(last_sum_kernel, n_t // 2),
        grid=(1,),
        in_specs=[SCALARS] + [pl.BlockSpec((count, columns), lambda i: (0, 0))] * 3,
        out_specs=[pl.BlockSpec((rows, columns), lambda i: (0, 0))] * n_t,
        out_shape=[jax.ShapeDtypeStruct((rows, columns), BF)] * n_t,
        compiler_params=params(24),
        cost_estimate=cost(0, 8 * count * columns),
        name="last_sum",
    )(at, parts, low, high)


def from_blocks_kernel(groups, piece, n_t, at_ref, *refs):
    n_z = n_t // 2
    pieces, out_ref, held_ref = refs[:n_t], refs[n_t], refs[n_t + 1]
    core, z = at_ref[0], at_ref[1]
    for c in range(2):
        for s in range(n_z):
            block = lax.rem(core + c, 2) * n_z + lax.rem(z - s + n_z, n_z)
            held_ref[block] = pieces[c * n_z + s][...]
    for t in range(n_t):
        for j in range(groups):
            first = (j * n_t + t) * piece
            out_ref[:, first : first + piece] = held_ref[t, :, j * piece : (j + 1) * piece].astype(F32)


def from_blocks(at, pieces, groups, piece):
    n_t = len(pieces)
    rows = pieces[0].shape[0]
    return pl.pallas_call(
        partial(from_blocks_kernel, groups, piece, n_t),
        in_specs=[SCALARS] + [VMEM] * n_t,
        out_specs=VMEM,
        out_shape=jax.ShapeDtypeStruct((rows, groups * n_t * piece), F32),
        scratch_shapes=[pltpu.VMEM((n_t, rows, groups * piece), BF)],
        compiler_params=params(16),
        cost_estimate=cost(0, 8 * rows * groups * n_t * piece),
        name="from_blocks",
    )(at, *pieces)


def pass_on_kernel(half, low_part_ref, high_part_ref, low_ref, high_ref, to_low_ref, to_high_ref):
    rows = low_part_ref.shape[0]
    if half:
        cut = rows // 2
        to_low_ref[0:cut, :] = (low_part_ref[0:cut, :].astype(F32) + low_ref[...].astype(F32)).astype(BF)
        to_low_ref[cut:, :] = low_part_ref[cut:, :]
        to_high_ref[0:cut, :] = high_part_ref[0:cut, :]
        to_high_ref[cut:, :] = (high_part_ref[cut:, :].astype(F32) + high_ref[...].astype(F32)).astype(BF)
    else:
        to_low_ref[...] = (low_part_ref[...].astype(F32) + low_ref[...].astype(F32)).astype(BF)
        to_high_ref[...] = (high_part_ref[...].astype(F32) + high_ref[...].astype(F32)).astype(BF)


def pass_on(parts, low_slot, high_slot, low, high, rows):
    columns = parts.shape[1]
    half = low.shape[0] < rows
    wide = math.gcd(columns, 512)
    arrived = pl.BlockSpec((low.shape[0], wide), lambda i: (0, i))
    out = pl.BlockSpec((rows, wide), lambda i: (0, i))
    return pl.pallas_call(
        partial(pass_on_kernel, half),
        grid=(columns // wide,),
        in_specs=[
            pl.BlockSpec((rows, wide), lambda i: (low_slot, i)),
            pl.BlockSpec((rows, wide), lambda i: (high_slot, i)),
            arrived,
            arrived,
        ],
        out_specs=[out, out],
        out_shape=[jax.ShapeDtypeStruct((rows, columns), BF)] * 2,
        cost_estimate=pl.CostEstimate(flops=2 * rows * columns, bytes_accessed=12 * rows * columns, transcendentals=0),
        name="pass_on",
    )(parts, parts, low, high)


def ring_offsets(n):
    return [0] + [o for s in range(1, n // 2 + 1) for o in ((s,) if 2 * s == n else (-s, s))]


def ring_sum(parts, rows, axis, order):
    n = len(order)
    slots = {o: i for i, o in enumerate(ring_offsets(n))}
    down, up = ring_pairs(order, -1), ring_pairs(order, 1)
    low = high = None
    for step in range(n // 2, 0, -1):
        if 2 * step == n:
            first = slots[step] * rows
            to_low, to_high = parts[first : first + rows // 2], parts[first + rows // 2 : first + rows]
        else:
            to_low, to_high = pass_on(parts, slots[-step], slots[step], low, high, rows)
        low, high = lax.ppermute(to_low, axis, down), lax.ppermute(to_high, axis, up)
    return low, high, (to_low, to_high)


def load_pieces(plan, starts_ref, piece_refs, target, sem):
    copies = []
    for i, (piece, first, rows) in enumerate(plan):
        start = pl.multiple_of(starts_ref[i], 16)
        copies.append(pltpu.make_async_copy(piece_refs[piece].at[pl.ds(first, rows)], target.at[pl.ds(start, rows)], sem.at[i]))
    return copies


def slot_copies(plan, slot, piece_refs, target, sem):
    return [
        pltpu.make_async_copy(piece_refs[piece], target.at[pl.ds(first, rows)], sem)
        for piece, first, rows in plan[slot]
    ]


def fetch_slots(plan, piece_refs, buffers, sems):
    i = pl.program_id(0)
    for slot in range(len(plan)):

        @pl.when(i == slot)
        def _(slot=slot):
            if slot == 0:
                for copy in slot_copies(plan, 0, piece_refs, buffers.at[0], sems.at[0]):
                    copy.start()
            if slot + 1 < len(plan):
                for copy in slot_copies(plan, slot + 1, piece_refs, buffers.at[(slot + 1) % 2], sems.at[(slot + 1) % 2]):
                    copy.start()
            pltpu.make_async_copy(buffers.at[slot % 2], buffers.at[slot % 2], sems.at[slot % 2]).wait()


class Gathered:
    def __init__(self, arrays, plan, starts):
        self.arrays = arrays
        self.plan = tuple(plan)
        self.starts = jnp.stack([jnp.asarray(s, jnp.int32) for s in starts])
        self.rows = sum(rows for *_, rows in plan)
        self.columns = arrays[0].shape[1]

    def scratch(self):
        return [pltpu.VMEM((self.rows, self.columns), BF), pltpu.SemaphoreType.DMA((len(self.plan),))]

    def specs(self):
        return [ANYWHERE] * len(self.arrays)


def normed(rows):
    mean = jnp.mean(rows, -1, keepdims=True)
    centred = rows - mean
    scale = lax.rsqrt(jnp.mean(centred * centred, -1, keepdims=True) + EPS)
    return centred * scale, scale


def project_kernel(split, x_plan, n_x, w_plan, n_w, starts_ref, *refs):
    x_refs, refs = refs[:n_x], refs[n_x:]
    w_refs, refs = refs[:n_w], refs[n_w:]
    gain_ref, shift_ref, b_ref, x_out_ref, hidden_ref, qkv_ref, act_ref, slope_ref, w_ref, w_sem, x_buf, x_sem = refs

    @pl.when(pl.program_id(0) == 0)
    def _():
        for copy in load_pieces(w_plan, starts_ref, w_refs, w_ref, w_sem):
            copy.start()

    fetch_slots(x_plan, x_refs, x_buf, x_sem)
    x = x_buf[lax.rem(pl.program_id(0), 2)]
    x_out_ref[...] = x
    xhat, _ = normed(x.astype(F32))
    hidden = (xhat * gain_ref[...] + shift_ref[...]).astype(BF)
    hidden_ref[...] = hidden

    @pl.when(pl.program_id(0) == 0)
    def _():
        for copy in load_pieces(w_plan, starts_ref, w_refs, w_ref, w_sem):
            copy.wait()

    pre = dot(hidden, w_ref[:, split:]) + b_ref[:, split:]
    root = math.sqrt(2.0 / math.pi)
    square = pre * pre
    turned = jnp.tanh(root * pre * (1.0 + 0.044715 * square))
    act_ref[...] = (0.5 * pre * (1.0 + turned)).astype(BF)
    slope = 0.5 * (1.0 + turned) + 0.5 * pre * (1.0 - turned * turned) * (root * (1.0 + 3 * 0.044715 * square))
    slope_ref[...] = slope.astype(BF)
    qkv_ref[...] = dot(hidden, w_ref[:, :split]) + b_ref[:, :split]


def project(x_arrays, x_plan, gain, shift, w, b, split, rows):
    count, width = rows * len(x_plan), x_arrays[0].shape[1]
    wide = w.columns

    def block(columns):
        return pl.BlockSpec((rows, columns), lambda i, s: (i, 0))

    return pl.pallas_call(
        partial(project_kernel, split, x_plan, len(x_arrays), w.plan, len(w.arrays)),
        grid_spec=pltpu.PrefetchScalarGridSpec(
            num_scalar_prefetch=1,
            grid=(len(x_plan),),
            in_specs=[ANYWHERE] * len(x_arrays) + w.specs() + [whole_block((1, width))] * 2 + [whole_block(b.shape)],
            out_specs=[block(width), block(width), block(split), block(wide - split), block(wide - split)],
            scratch_shapes=w.scratch() + [pltpu.VMEM((2, rows, width), BF), pltpu.SemaphoreType.DMA((2,))],
        ),
        out_shape=[
            jax.ShapeDtypeStruct((count, width), BF),
            jax.ShapeDtypeStruct((count, width), BF),
            jax.ShapeDtypeStruct((count, split), F32),
            jax.ShapeDtypeStruct((count, wide - split), BF),
            jax.ShapeDtypeStruct((count, wide - split), BF),
        ],
        compiler_params=params(36),
        cost_estimate=cost(2 * count * width * wide, 8 * count * width + 2 * width * wide),
        name="project",
    )(w.starts, *x_arrays, *w.arrays, gain, shift, b)


def combine_kernel(split, w_plan, n_w, starts_ref, act_ref, att_ref, *refs):
    w_refs, refs = refs[:n_w], refs[n_w:]
    w_ref, w_sem = refs[-2:]

    @pl.when(pl.program_id(0) == 0)
    def _():
        copies = load_pieces(w_plan, starts_ref, w_refs, w_ref, w_sem)
        for copy in copies:
            copy.start()
        for copy in copies:
            copy.wait()

    total = dot(act_ref[...], w_ref[:split, :]) + dot(att_ref[...], w_ref[split:, :])
    if len(refs) == 4:
        total = total + refs[0][...].astype(F32)
    refs[-3][...] = total.astype(BF)


def combine(act, att, w, part, arrived=None):
    count, split = act.shape[0] // 2, act.shape[1]
    width = w.columns
    rows = math.gcd(count, ROWS)
    base = part * (count // rows)

    def block(columns):
        return pl.BlockSpec((rows, columns), lambda i, s: (i + base, 0))

    out = pl.BlockSpec((rows, width), lambda i, s: (i, 0))
    extra = [] if arrived is None else [arrived]
    return pl.pallas_call(
        partial(combine_kernel, split, w.plan, len(w.arrays)),
        grid_spec=pltpu.PrefetchScalarGridSpec(
            num_scalar_prefetch=1,
            grid=(count // rows,),
            in_specs=[block(split), block(att.shape[1])] + w.specs() + [out] * len(extra),
            out_specs=out,
            scratch_shapes=w.scratch(),
        ),
        out_shape=jax.ShapeDtypeStruct((count, width), BF),
        compiler_params=params(32),
        cost_estimate=cost(2 * count * width * w.rows, 4 * count * width + 2 * width * w.rows),
        name="combine",
    )(w.starts, act, att, *w.arrays, *extra)


def combine_back_kernel(split, g_plan, n_g, w_plan, n_w, starts_ref, *refs):
    g_refs, refs = refs[:n_g], refs[n_g:]
    w_refs, refs = refs[:n_w], refs[n_w:]
    slope_ref, g_out_ref, pre_grad_ref, att_grad_ref, w_ref, w_sem, g_buf, g_sem = refs

    @pl.when(pl.program_id(0) == 0)
    def _():
        for copy in load_pieces(w_plan, starts_ref, w_refs, w_ref, w_sem):
            copy.start()

    fetch_slots(g_plan, g_refs, g_buf, g_sem)

    @pl.when(pl.program_id(0) == 0)
    def _():
        for copy in load_pieces(w_plan, starts_ref, w_refs, w_ref, w_sem):
            copy.wait()

    grad = g_buf[lax.rem(pl.program_id(0), 2)]
    g_out_ref[...] = grad
    pre_grad_ref[...] = (dot_t(grad, w_ref[:split, :]) * slope_ref[...].astype(F32)).astype(BF)
    att_grad_ref[...] = dot_t(grad, w_ref[split:, :]).astype(BF)


def combine_back(g_arrays, g_plan, w, slope, rows):
    count, width = rows * len(g_plan), g_arrays[0].shape[1]
    split = slope.shape[1]
    rest = w.rows - split

    def block(columns):
        return pl.BlockSpec((rows, columns), lambda i, s: (i, 0))

    return pl.pallas_call(
        partial(combine_back_kernel, split, g_plan, len(g_arrays), w.plan, len(w.arrays)),
        grid_spec=pltpu.PrefetchScalarGridSpec(
            num_scalar_prefetch=1,
            grid=(len(g_plan),),
            in_specs=[ANYWHERE] * len(g_arrays) + w.specs() + [block(split)],
            out_specs=[block(width), block(split), block(rest)],
            scratch_shapes=w.scratch() + [pltpu.VMEM((2, rows, width), BF), pltpu.SemaphoreType.DMA((2,))],
        ),
        out_shape=[
            jax.ShapeDtypeStruct((count, width), BF),
            jax.ShapeDtypeStruct((count, split), BF),
            jax.ShapeDtypeStruct((count, rest), BF),
        ],
        compiler_params=params(32),
        cost_estimate=cost(2 * count * width * w.rows, 6 * count * width + 2 * width * w.rows),
        name="combine_back",
    )(w.starts, *g_arrays, *w.arrays, slope)


def project_back_kernel(split, w_plan, n_w, starts_ref, qkv_grad_ref, pre_grad_ref, x_ref, *refs):
    w_refs, refs = refs[:n_w], refs[n_w:]
    out_ref, sums_ref, w_ref, w_sem = refs[-4:]

    @pl.when(pl.program_id(0) == 0)
    def _():
        copies = load_pieces(w_plan, starts_ref, w_refs, w_ref, w_sem)
        for copy in copies:
            copy.start()
        sums_ref[...] = jnp.zeros_like(sums_ref)
        for copy in copies:
            copy.wait()

    grad = dot_t(qkv_grad_ref[...], w_ref[:, :split]) + dot_t(pre_grad_ref[...], w_ref[:, split:])
    xhat, _ = normed(x_ref[...].astype(F32))
    sums_ref[0:1, :] += jnp.sum(grad * xhat, 0, keepdims=True)
    sums_ref[1:2, :] += jnp.sum(grad, 0, keepdims=True)
    if len(refs) == 5:
        grad = grad + refs[0][...].astype(F32)
    out_ref[...] = grad.astype(BF)


def project_back(qkv_grad, pre_grad, w, x, part, arrived=None):
    count, width = x.shape[0] // 2, x.shape[1]
    split = qkv_grad.shape[1]
    rows = math.gcd(count, ROWS)
    base = part * (count // rows)

    def block(columns):
        return pl.BlockSpec((rows, columns), lambda i, s: (i + base, 0))

    out = pl.BlockSpec((rows, width), lambda i, s: (i, 0))
    extra = [] if arrived is None else [arrived]
    return pl.pallas_call(
        partial(project_back_kernel, split, w.plan, len(w.arrays)),
        grid_spec=pltpu.PrefetchScalarGridSpec(
            num_scalar_prefetch=1,
            grid=(count // rows,),
            in_specs=[block(split), block(pre_grad.shape[1]), block(width)] + w.specs() + [out] * len(extra),
            out_specs=[out, whole_block((8, width))],
            scratch_shapes=w.scratch(),
        ),
        out_shape=[jax.ShapeDtypeStruct((count, width), BF), jax.ShapeDtypeStruct((8, width), F32)],
        compiler_params=params(36),
        cost_estimate=cost(2 * count * width * w.columns, 6 * count * width + 2 * width * w.columns),
        name="project_back",
    )(w.starts, qkv_grad, pre_grad, x, *w.arrays, *extra)


def weight_grad_kernel(turns_ref, left_ref, right_ref, out_ref, sums_ref):
    out_ref[...] = t_dot(left_ref[...], right_ref[...]).astype(BF)

    @pl.when(pl.program_id(0) == 0)
    def _():
        sums_ref[...] = jnp.zeros_like(sums_ref)
        sums_ref[0:1, :] = jnp.sum(right_ref[...].astype(F32), 0, keepdims=True)


def weight_grad(turns, left, right):
    n_q = turns.shape[0]
    count, wide = left.shape
    columns = right.shape[1]
    part = wide // n_q
    return pl.pallas_call(
        weight_grad_kernel,
        grid_spec=pltpu.PrefetchScalarGridSpec(
            num_scalar_prefetch=1,
            grid=(n_q,),
            in_specs=[pl.BlockSpec((count, part), lambda k, s: (0, s[k])), whole_block(right.shape)],
            out_specs=[pl.BlockSpec((part, columns), lambda k, s: (k, 0)), whole_block((8, columns))],
        ),
        out_shape=[jax.ShapeDtypeStruct((wide, columns), BF), jax.ShapeDtypeStruct((8, columns), F32)],
        compiler_params=params(40),
        cost_estimate=cost(2 * count * wide * columns, 2 * count * (wide + columns) + 2 * wide * columns),
        name="weight_grad",
    )(turns, left, right)


def down_grad_kernel(head_rows, turns_ref, act_ref, att_ref, g_ref, out_ref, held_ref):
    units = act_ref.shape[1]
    k = pl.program_id(0)

    @pl.when(k == 0)
    def _():
        held_ref[...] = t_dot(att_ref[...], g_ref[...]).astype(BF)

    out_ref[0:units, :] = t_dot(act_ref[...], g_ref[...]).astype(BF)
    rows = pl.ds(pl.multiple_of(turns_ref[k] * head_rows, head_rows), head_rows)
    out_ref[units:, :] = held_ref[rows, :]


def down_grad(turns, act, att, g, head_rows):
    n_q = turns.shape[0]
    count, wide = act.shape
    own_width = att.shape[1]
    width = g.shape[1]
    units = wide // n_q
    if not head_rows:
        whole = t_dot(act, g).astype(BF).reshape(n_q, units, width)[turns]
        return whole.reshape(wide, width), t_dot(att, g)
    return pl.pallas_call(
        partial(down_grad_kernel, head_rows),
        grid_spec=pltpu.PrefetchScalarGridSpec(
            num_scalar_prefetch=1,
            grid=(n_q,),
            in_specs=[pl.BlockSpec((count, units), lambda k, s: (0, s[k])), whole_block(att.shape), whole_block(g.shape)],
            out_specs=pl.BlockSpec((units + head_rows, width), lambda k, s: (k, 0)),
            scratch_shapes=[pltpu.VMEM((own_width, width), BF)],
        ),
        out_shape=jax.ShapeDtypeStruct((n_q * (units + head_rows), width), BF),
        compiler_params=params(40),
        cost_estimate=cost(2 * count * (wide + own_width) * width, 2 * count * (wide + width) + 2 * wide * width),
        name="down_grad",
    )(turns, act, att, g), None


def finish_kernel(part_ref, low_ref, high_ref, x_ref, g_ref, gain_ref, out_ref):
    grad = part_ref[...].astype(F32) + low_ref[...].astype(F32) + high_ref[...].astype(F32)
    xhat, scale = normed(x_ref[...].astype(F32))
    m = grad * gain_ref[...]
    x_grad = (m - jnp.mean(m, -1, keepdims=True) - xhat * jnp.mean(m * xhat, -1, keepdims=True)) * scale
    out_ref[...] = (g_ref[...].astype(F32) + x_grad).astype(BF)


def finish(parts, low, high, x, g, gain):
    count, width = x.shape
    rows = math.gcd(count, 64)
    block = pl.BlockSpec((rows, width), lambda i: (i, 0))
    return pl.pallas_call(
        finish_kernel,
        grid=(count // rows,),
        in_specs=[block] * 5 + [whole_block((1, width))],
        out_specs=block,
        out_shape=jax.ShapeDtypeStruct((count, width), BF),
        cost_estimate=cost(20 * count * width, 12 * count * width),
        name="finish",
    )(parts, low, high, x, g, gain)


def per_device(
    inputs,
    span_table,
    ln_gain,
    ln_bias,
    qkv_weight,
    qkv_bias,
    out_weight,
    out_bias,
    fc1_weight,
    fc1_bias,
    fc2_weight,
    fc2_bias,
    cotangent,
):
    rows, width = inputs.shape
    head_dim = width // HEADS
    n_q, n_z = lax.axis_size("q"), lax.axis_size("ctx")
    n_t = 2 * n_z
    n_all = n_q * n_t
    q, core, z = lax.axis_index("q"), lax.axis_index("core"), lax.axis_index("ctx")
    t = core * n_z + z
    at = jnp.stack([core, z]).astype(jnp.int32)
    span = rows // 2
    seq_len = rows * n_z
    heads = HEADS // n_t
    own_width = heads * head_dim
    split = 3 * own_width
    units = fc2_weight.shape[0]
    own_units = units * n_q
    d_rows = qkv_weight.shape[0]
    every = ("q", "core", "ctx")
    z_order = list(range(n_z))
    q_order = [0, 1, 3, 2] if n_q == 4 else list(range(n_q))
    places = jnp.array([q_order.index(i) for i in range(n_q)], jnp.int32)
    q_ring = jnp.array(q_order, jnp.int32)
    q_offsets, z_offsets = ring_offsets(n_q), ring_offsets(n_z)
    turns = jnp.stack([q_ring[(places[q] + o) % n_q] for o in q_offsets])
    q_at = dict(zip(q_offsets, turns))
    whole_heads = out_weight.shape[0] == head_dim

    small = jnp.concatenate([ln_gain, ln_bias, out_bias, fc2_bias, qkv_bias, fc1_bias])
    small = jnp.pad(small, (0, 256 * 128 - small.shape[0])).reshape(256, 128)
    small = lax.all_gather(small, every, axis=0, tiled=True).reshape(n_all, 256 * 128)
    cuts = [ln_gain.shape[0], ln_bias.shape[0], out_bias.shape[0], fc2_bias.shape[0], qkv_bias.shape[0], fc1_bias.shape[0]]
    starts = [sum(cuts[:i]) for i in range(len(cuts))]
    gain, shift, b_out, b_down, b_qkv, b_up = (small[:, s : s + c].astype(F32) for s, c in zip(starts, cuts))
    gain, shift, b_out, b_down = (v.reshape(1, width) for v in (gain, shift, b_out, b_down))
    b_qkv = lax.dynamic_index_in_dim(b_qkv.reshape(3, heads, n_t, head_dim), t, 2, False).reshape(1, split)
    b_up = lax.dynamic_index_in_dim(b_up.reshape(n_q, n_t, units), t, 1, False).reshape(1, own_units)
    b_project = jnp.concatenate([b_qkv, b_up], 1)

    spans = jnp.concatenate([lax.dynamic_index_in_dim(span_table, (z + o) % n_z, 0, False) for o in z_offsets])
    n_spans = 2 * n_z
    slots = jnp.arange(n_spans, dtype=jnp.int32)
    order = jnp.sum(jnp.where(spans[None, :] == slots[:, None], slots[None, :], 0), 1, dtype=jnp.int32)
    half = ROT // 2
    lane = jnp.arange(own_width, dtype=jnp.int32)[None, :] % head_dim
    position = jnp.arange(seq_len, dtype=jnp.int32).astype(F32)[:, None]
    freqs = jnp.where(lane < ROT, jnp.exp((lane % half).astype(F32) * (-2.0 * math.log(10000.0) / ROT)), 0.0)
    angles = position * freqs
    sine = jnp.sin(angles)
    tables = (jnp.cos(angles), jnp.where(lane < half, -sine, 0.0), jnp.where((lane >= half) & (lane < ROT), sine, 0.0))

    def line_exchange(pieces):
        mine = pieces[:n_z]
        theirs = list(swap(jnp.concatenate(pieces[n_z:], 0)).reshape(n_z, *pieces[0].shape))
        return [
            lax.ppermute(p, "ctx", ring_pairs(z_order, s)) if s else p for c in (mine, theirs) for s, p in enumerate(c)
        ]

    w2_block = jnp.concatenate([fc2_weight, out_weight], 0) if whole_heads else fc2_weight
    w2_pieces = gathered(w2_block, "q", q_order)
    blocks = line_exchange(to_blocks(at, qkv_weight, fc1_weight, n_q, n_t, heads, head_dim, units))
    w1_block = stack_rows(at, [after(blocks[0], w2_pieces[1][2], w2_pieces[2][2])] + blocks[1:])
    plan, places_of = [], []
    for i, (offset, first, piece) in enumerate(w2_pieces):
        last = first + piece.shape[0]
        if first < units:
            plan.append((i, 0, min(last, units) - first))
            places_of.append(q_at[offset] * units + first)
        if last > units:
            begin = max(first, units)
            plan.append((i, begin - first, last - begin))
            places_of.append(own_units + q_at[offset] * head_dim + begin - units)
    w2_arrays = [piece for *_, piece in w2_pieces]
    if not whole_heads:
        w_out = lax.all_gather(out_weight, every, axis=0, tiled=True).reshape(heads, n_t, head_dim, width)
        w2_arrays.append(lax.dynamic_index_in_dim(w_out, t, 1, False).reshape(own_width, width))
        plan.append((len(w2_arrays) - 1, 0, own_width))
        places_of.append(own_units)
    w2 = Gathered(w2_arrays, plan, places_of)

    w1_pieces = gathered(w1_block, "q", q_order)
    block_rows = n_t * d_rows
    w1 = Gathered(
        [piece for *_, piece in w1_pieces],
        [(i, 0, piece.shape[0]) for i, (*_, piece) in enumerate(w1_pieces)],
        [q_at[offset] * block_rows + first for offset, first, _ in w1_pieces],
    )

    slot_of = {o: i for i, o in enumerate(z_offsets)}

    def line(block):
        pieces = gathered(block, "ctx", z_order)
        token_plan = [[] for _ in range(2 * n_z)]
        for i, (offset, first, piece) in enumerate(pieces):
            for c in range(2):
                token_plan[slot_of[offset] + c * n_z].append((i + c * len(pieces), first, piece.shape[0]))
        arrays = [piece for *_, piece in pieces]
        return arrays, arrays + [swap(piece) for piece in arrays], tuple(tuple(p) for p in token_plan)

    x_line, x_arrays, token_plan = line(after(inputs, *blocks[1:n_z], *blocks[n_z + 1 :]))
    g_line, g_arrays, _ = line(after(cotangent, *x_line[-2:]))

    x_all, hidden, qkv, act, slope = project(x_arrays, token_plan, gain, shift, w1, b_project, split, rows)
    att, kept = attend(order, qkv.reshape(2, seq_len, split), tables, heads, head_dim, span)
    att = after(att, *g_line[1:3]).reshape(2 * seq_len, own_width)
    out_other = combine(act, att, w2, 1)
    out_own = combine(act, after(att, out_other), w2, 0, swap(out_other))

    low, high, sent = ring_sum(after(out_own, *g_line[-2:]), rows, "ctx", z_order)
    x_here = inputs.astype(F32)
    output = (x_here + (out_own[:rows].astype(F32) + low.astype(F32) + high.astype(F32)) + (b_out + b_down)).astype(BF)

    def q_sum(part):
        return ring_sum(part, part.shape[0] // n_q, "q", q_order)

    g_all, pre_grad, att_grad = combine_back(g_arrays, token_plan, w2, after(slope, out_own), rows)
    up_part, up_sums = weight_grad(turns, hidden, pre_grad)
    up_low, up_high, up_sent = q_sum(up_part)
    att_grad = after(att_grad, up_part, *sent).reshape(2, seq_len, own_width)
    qkv_grad = attend_back(order, kept, att_grad, tables, heads, head_dim, span).reshape(2 * seq_len, split)
    part_other, sums_other = project_back(after(qkv_grad, *up_sent), pre_grad, w1, x_all, 1)
    qkv_part, qkv_sums = weight_grad(turns, after(hidden, part_other), qkv_grad)
    part_own, sums_own = project_back(after(qkv_grad, qkv_part, low, high), pre_grad, w1, x_all, 0, swap(part_other))
    qkv_low, qkv_high, qkv_sent = q_sum(qkv_part)
    n_low, n_high, n_sent = ring_sum(part_own, rows, "ctx", z_order)
    up_rows = last_sum(at, up_part, up_low, up_high, n_t)
    down, out_apart = down_grad(turns, after(act, part_own, *qkv_sent, *up_rows), att, g_all, head_dim if whole_heads else 0)

    fc1_weight_grad = from_blocks(at, line_exchange(up_rows), n_q, units)
    qkv_rows = last_sum(at, qkv_part, qkv_low, qkv_high, n_t)
    qkv_weight_grad = from_blocks(at, line_exchange(qkv_rows), 3 * heads, head_dim)
    down_low, down_high, _ = q_sum(down)
    down_rows = down_low.shape[0]
    down_sum = down[:down_rows].astype(F32) + down_low.astype(F32) + down_high.astype(F32)
    fc2_weight_grad = down_sum[:units]
    if whole_heads:
        out_weight_grad = down_sum[units:]
    else:
        spread = jnp.zeros((heads, n_t, head_dim, width), F32)
        spread = lax.dynamic_update_slice(spread, out_apart.reshape(heads, 1, head_dim, width), (0, t, 0, 0))
        out_weight_grad = lax.psum_scatter(spread.reshape(width, width), every, scatter_dimension=0, tiled=True)

    input_grad = finish(part_own, n_low, n_high, inputs, cotangent, gain)

    def by_owner(vector):
        return vector.reshape(n_all, vector.shape[0] // n_all)

    qkv_spread = lax.dynamic_update_slice(
        jnp.zeros((3, heads, n_t, head_dim), F32), qkv_sums[0].reshape(3, heads, 1, head_dim), (0, 0, t, 0)
    ).reshape(-1)
    up_spread = lax.dynamic_update_slice(jnp.zeros((n_q, n_t, units), F32), up_sums[0].reshape(n_q, 1, units), (0, t, 0)).reshape(-1)
    vectors = jnp.concatenate(
        [
            by_owner(sums_own[0] + sums_other[0]),
            by_owner(sums_own[1] + sums_other[1]),
            by_owner(jnp.sum(cotangent.astype(F32), 0)),
            by_owner(qkv_spread),
            by_owner(up_spread),
        ],
        1,
    )
    cube = vectors.reshape(n_q, 2, n_z, vectors.shape[1])
    cube = lax.dynamic_index_in_dim(cube, core, 1, False) + swap(lax.dynamic_index_in_dim(cube, 1 - core, 1, False))
    total = sum_blocks(cube, "q", q, n_q)
    total = sum_blocks(total, "ctx", z, n_z)
    cuts = [ln_gain.shape[0], ln_bias.shape[0], out_bias.shape[0], qkv_bias.shape[0], fc1_bias.shape[0]]
    starts = [sum(cuts[:i]) for i in range(len(cuts))]
    gain_grad, shift_grad, bias_grad, qkv_bias_grad, fc1_bias_grad = (total[s : s + c] for s, c in zip(starts, cuts))
    return (
        output,
        input_grad,
        gain_grad,
        shift_grad,
        qkv_weight_grad,
        qkv_bias_grad,
        out_weight_grad,
        bias_grad,
        fc1_weight_grad,
        fc1_bias_grad,
        fc2_weight_grad,
        bias_grad,
    )


def sum_blocks(blocks, axis, index, n):
    total = lax.dynamic_index_in_dim(blocks, index, 0, False)
    for shift_by in range(1, n):
        piece = lax.dynamic_index_in_dim(blocks, (index + shift_by) % n, 0, False)
        total = total + lax.ppermute(piece, axis, ring_pairs(list(range(n)), shift_by))
    return total


def solution(mesh):
    n_dp, n_ctx = mesh.devices.shape
    inner = Mesh(mesh.devices.reshape(n_dp // 2, 2, n_ctx), ("q", "core", "ctx"))
    every = ("q", "core", "ctx")
    matrix, vector = P(every, None), P(every)
    return jax.shard_map(
        per_device,
        mesh=inner,
        in_specs=(
            matrix,
            P(),
            vector,
            vector,
            matrix,
            vector,
            matrix,
            vector,
            matrix,
            vector,
            matrix,
            vector,
            matrix,
        ),
        out_specs=(matrix, matrix, vector, vector, matrix, vector, matrix, vector, matrix, vector, matrix, vector),
        check_vma=False,
    )
```

```python
from functools import partial
import math

import jax
import jax.numpy as jnp
from jax import lax
from jax.experimental import pallas as pl
from jax.experimental.pallas import tpu as pltpu
from jax.sharding import Mesh, PartitionSpec as P

HEADS = 32
ROT = 32
EPS = 1e-05
NEG = -1e30
BLOCK_Q = 256

BF = jnp.bfloat16
F32 = jnp.float32


def dot(a, b):
    return jnp.dot(a, b, preferred_element_type=F32)


def dot_t(a, b):
    return lax.dot_general(a, b, (((1,), (1,)), ((), ())), preferred_element_type=F32)


def t_dot(a, b):
    return lax.dot_general(a, b, (((0,), (0,)), ((), ())), preferred_element_type=F32)


def cost(flops, nbytes):
    return pl.CostEstimate(flops=flops // 1000, bytes_accessed=nbytes // 1000, transcendentals=0)


def across(value, axis, e):
    n = math.prod(lax.axis_size(a) for a in axis) if isinstance(axis, tuple) else lax.axis_size(axis)
    return lax.ppermute(value, axis, [(i, i ^ e) for i in range(n)])


def scattered(parts, axis):
    return [parts[0]] + [across(part, axis, e) for e, part in enumerate(parts) if e]


def ring_pairs(order, step):
    n = len(order)
    return [(order[i], order[(i + step) % n]) for i in range(n)]


def ring_offsets(n):
    return [0] + [o for s in range(1, n // 2) for o in (-s, s)] + [n // 2]


def half_of(rows):
    return rows // 32 * 16


def slot_plan(n, rows, first=0):
    plan = [((first + k, 0, rows),) for k in range(n - 1)]
    return plan + [((first + n - 1, 0, half_of(rows)), (first + n, half_of(rows), rows - half_of(rows)))]


def ring_gathered(own, axis, order, hold=()):
    n = len(order)
    up_pairs, down_pairs = ring_pairs(order, 1), ring_pairs(order, -1)
    out = [own]
    up = down = own
    half = half_of(own.shape[0])
    for _ in range(1, n // 2):
        up, down = lax.ppermute(up, axis, up_pairs), lax.ppermute(down, axis, down_pairs)
        out += [up, down]
    up, down = after(up[:half], *hold), after(down[half:], *hold)
    return out + [lax.ppermute(up, axis, up_pairs), lax.ppermute(down, axis, down_pairs)]


def ring_sum(parts, axis, order, hold=(), tail=0):
    n = len(order)
    up_pairs, down_pairs = ring_pairs(order, 1), ring_pairs(order, -1)
    low, high = lax.ppermute(parts[n - 1], axis, down_pairs), lax.ppermute(parts[n], axis, up_pairs)
    sent = ()
    for step in range(n // 2 - 1, 0, -1):
        sent = pass_on(parts[2 * step - 1], parts[2 * step], after(low, *hold), high, tail)
        low, high = lax.ppermute(sent[0], axis, down_pairs), lax.ppermute(sent[1], axis, up_pairs)
    return [parts[0], low, high], sent


def in_two(values):
    first = values.astype(BF)
    return first, (values - first.astype(F32)).astype(BF)


def add_rows(part, arrived, tail):
    total = part.astype(F32) + arrived.astype(F32)
    if not tail:
        return total.astype(BF)
    cut, half = total.shape[0] - tail, tail // 2
    values = total[cut : cut + half, :] + total[cut + half :, :]
    return jnp.concatenate([total[:cut, :].astype(BF), *in_two(values)], 0)


def pass_on_kernel(tail, low_part_ref, high_part_ref, low_ref, high_ref, to_low_ref, to_high_ref):
    rows = low_part_ref.shape[0]
    cut = low_ref.shape[0]
    if cut < rows:
        to_low_ref[0:cut, :] = add_rows(low_part_ref[0:cut, :], low_ref[...], 0)
        to_low_ref[cut:, :] = low_part_ref[cut:, :]
        to_high_ref[0:cut, :] = high_part_ref[0:cut, :]
        to_high_ref[cut:, :] = add_rows(high_part_ref[cut:, :], high_ref[...], tail)
    else:
        to_low_ref[...] = add_rows(low_part_ref[...], low_ref[...], tail)
        to_high_ref[...] = add_rows(high_part_ref[...], high_ref[...], tail)


def pass_on(low_part, high_part, low, high, tail):
    rows, columns = low_part.shape
    wide = math.gcd(columns, 512)

    def block(array):
        return pl.BlockSpec((array.shape[0], wide), lambda i: (0, i))

    arrays = [low_part, high_part, low, high]
    return pl.pallas_call(
        partial(pass_on_kernel, tail),
        grid=(columns // wide,),
        in_specs=[block(array) for array in arrays],
        out_specs=[block(low_part)] * 2,
        out_shape=[jax.ShapeDtypeStruct((rows, columns), BF)] * 2,
        cost_estimate=cost(2 * rows * columns, 12 * rows * columns),
        name="pass_on",
    )(*arrays)


def swap(value):
    return lax.ppermute(value, "core", [(0, 1), (1, 0)])


def turn(values, cosine, sine_a, sine_b):
    width = values.shape[1]
    cosine, sine_a, sine_b = (jnp.concatenate([v] * (width // 128), 1) for v in (cosine, sine_a, sine_b))
    return (
        values * cosine
        + pltpu.roll(values, width - ROT // 2, 1) * sine_a
        + pltpu.roll(values, ROT // 2, 1) * sine_b
    )


def head_mask(shape, head, head_dim):
    lane = lax.broadcasted_iota(jnp.int32, shape, 1)
    return (lane >= head * head_dim) & (lane < (head + 1) * head_dim)


def attend_kernel(heads, head_dim, span, order_ref, qkv_ref, cos_ref, sin_a_ref, sin_b_ref, att_ref, sorted_ref, out_scr):
    seq_len = qkv_ref.shape[1]
    width = heads * head_dim
    for slot in range(seq_len // span):
        rows = pl.ds(pl.multiple_of(order_ref[slot] * span, span), span)
        here = pl.ds(slot * span, span)
        tables = (cos_ref[here, :], sin_a_ref[here, :], sin_b_ref[here, :])
        query = turn(qkv_ref[0, rows, 0:width], *tables).astype(BF)
        sorted_ref[0, here, 0:width] = (query.astype(F32) * (head_dim**-0.5)).astype(BF)
        sorted_ref[0, here, width : 2 * width] = turn(qkv_ref[0, rows, width : 2 * width], *tables).astype(BF)
        sorted_ref[0, here, 2 * width :] = qkv_ref[0, rows, 2 * width :].astype(BF)
    block = min(BLOCK_Q, seq_len)
    for i in range(seq_len // block):
        extent = (i + 1) * block
        here = pl.ds(i * block, block)
        queries = sorted_ref[0, here, 0:width]
        keys = sorted_ref[0, 0:extent, width : 2 * width]
        values = sorted_ref[0, 0:extent, 2 * width :]
        row = lax.broadcasted_iota(jnp.int32, (block, extent), 0) + i * block
        col = lax.broadcasted_iota(jnp.int32, (block, extent), 1)
        total = jnp.zeros((block, width), F32)
        for head in range(heads):
            mask = head_mask((block, width), head, head_dim)
            scores = dot_t(jnp.where(mask, queries, jnp.zeros_like(queries)), keys)
            scores = jnp.where(col <= row, scores, NEG)
            top = jnp.max(scores, 1, keepdims=True)
            weights = jnp.exp(scores - top)
            norm = 1.0 / jnp.sum(weights, 1, keepdims=True)
            probs = (weights * norm).astype(BF)
            total = jnp.where(mask, dot(probs, values), total)
        out_scr[here, :] = total.astype(BF)
    for slot in range(seq_len // span):
        rows = pl.ds(pl.multiple_of(order_ref[slot] * span, span), span)
        att_ref[0, rows, :] = out_scr[slot * span : (slot + 1) * span, :]


def attend_back_kernel(
    heads, head_dim, span, order_ref, kept_a_ref, kept_b_ref, grad_ref, cos_ref, sin_a_ref, sin_b_ref, out_ref, grad_scr, key_scr, value_scr, sorted_ref
):
    seq_len = sorted_ref.shape[1]

    @pl.when(pl.program_id(0) == 0)
    def _():
        sorted_ref[...] = kept_a_ref[...]

    @pl.when(pl.program_id(0) == 1)
    def _():
        sorted_ref[...] = kept_b_ref[...]

    width = heads * head_dim
    for slot in range(seq_len // span):
        rows = pl.ds(pl.multiple_of(order_ref[slot] * span, span), span)
        grad_scr[slot * span : (slot + 1) * span, :] = grad_ref[0, rows, :]
    key_scr[...] = jnp.zeros_like(key_scr)
    value_scr[...] = jnp.zeros_like(value_scr)
    block = min(BLOCK_Q, seq_len)

    def put(slot, first, values):
        rows = pl.ds(pl.multiple_of(order_ref[slot] * span, span), span)
        out_ref[0, rows, first : first + width] = values.astype(BF)

    def tables(here):
        return (cos_ref[here, :], -sin_a_ref[here, :], -sin_b_ref[here, :])

    for i in range(seq_len // block):
        extent = (i + 1) * block
        here = pl.ds(i * block, block)
        queries = sorted_ref[0, here, 0:width]
        grads = grad_scr[here, :]
        keys = sorted_ref[0, 0:extent, width : 2 * width]
        values = sorted_ref[0, 0:extent, 2 * width :]
        key = lax.broadcasted_iota(jnp.int32, (extent, block), 0)
        query = lax.broadcasted_iota(jnp.int32, (extent, block), 1) + i * block
        query_grad = jnp.zeros((block, width), F32)
        for head in range(heads):
            mask = head_mask((block, width), head, head_dim)
            own_queries = jnp.where(mask, queries, jnp.zeros_like(queries))
            own_grads = jnp.where(mask, grads, jnp.zeros_like(grads))
            scores = jnp.where(key <= query, dot_t(keys, own_queries), NEG)
            weights = jnp.exp(scores - jnp.max(scores, 0, keepdims=True))
            probs = weights * (1.0 / jnp.sum(weights, 0, keepdims=True))
            probs_grad = dot_t(values, own_grads)
            delta = jnp.sum(probs * probs_grad, 0, keepdims=True)
            score_grad = (probs * (probs_grad - delta)).astype(BF)
            value_scr[0:extent, :] += dot(probs.astype(BF), own_grads)
            key_scr[0:extent, :] += dot(score_grad, own_queries)
            query_grad = jnp.where(mask, t_dot(score_grad, keys), query_grad)
        query_grad = turn(query_grad * (head_dim**-0.5), *tables(here))
        for j in range(block // span):
            put(i * (block // span) + j, 0, query_grad[j * span : (j + 1) * span])
    for slot in range(seq_len // span):
        here = pl.ds(slot * span, span)
        put(slot, width, turn(key_scr[here, :], *tables(here)))
        put(slot, 2 * width, value_scr[here, :])


def attend(order, qkv, tables, heads, head_dim, span, part):
    seq_len, wide = qkv.shape[0] // 2, qkv.shape[1]
    width = wide // 3
    whole = pl.BlockSpec((seq_len, 128), lambda s, o: (0, 0))
    return pl.pallas_call(
        partial(attend_kernel, heads, head_dim, span),
        grid_spec=pltpu.PrefetchScalarGridSpec(
            num_scalar_prefetch=1,
            grid=(1,),
            in_specs=[pl.BlockSpec((1, seq_len, wide), lambda s, o: (part, 0, 0)), whole, whole, whole],
            out_specs=[
                pl.BlockSpec((1, seq_len, width), lambda s, o: (0, 0, 0)),
                pl.BlockSpec((1, seq_len, wide), lambda s, o: (0, 0, 0)),
            ],
            scratch_shapes=[pltpu.VMEM((seq_len, width), BF)],
        ),
        out_shape=[
            jax.ShapeDtypeStruct((1, seq_len, width), BF),
            jax.ShapeDtypeStruct((1, seq_len, wide), BF),
        ],
        compiler_params=pltpu.CompilerParams(vmem_limit_bytes=40 * 2**20),
        cost_estimate=cost(8 * heads * seq_len * seq_len * head_dim, 8 * seq_len * wide),
        name="attend",
    )(order, qkv.reshape(2, seq_len, wide), *tables)


def attend_back(order, kept, grads, tables, heads, head_dim, span):
    count, (_, seq_len, wide) = len(kept), kept[0].shape
    width = wide // 3
    whole = pl.BlockSpec((seq_len, 128), lambda s, o: (0, 0))
    return pl.pallas_call(
        partial(attend_back_kernel, heads, head_dim, span),
        grid_spec=pltpu.PrefetchScalarGridSpec(
            num_scalar_prefetch=1,
            grid=(count,),
            in_specs=[
                pl.BlockSpec((1, seq_len, wide), lambda s, o: (0, 0, 0)),
                pl.BlockSpec((1, seq_len, wide), lambda s, o: (0, 0, 0)),
                pl.BlockSpec((1, seq_len, width), lambda s, o: (s, 0, 0)),
                whole,
                whole,
                whole,
            ],
            out_specs=pl.BlockSpec((1, seq_len, wide), lambda s, o: (s, 0, 0)),
            scratch_shapes=[
                pltpu.VMEM((seq_len, width), BF),
                pltpu.VMEM((seq_len, width), F32),
                pltpu.VMEM((seq_len, width), F32),
                pltpu.VMEM((1, seq_len, wide), BF),
            ],
        ),
        out_shape=jax.ShapeDtypeStruct((count, seq_len, wide), BF),
        compiler_params=pltpu.CompilerParams(vmem_limit_bytes=40 * 2**20),
        cost_estimate=cost(20 * count * heads * seq_len * seq_len * head_dim, 6 * count * seq_len * wide),
        name="attend_back",
    )(order, *kept, grads, *tables)


def after(value, *others):
    return lax.optimization_barrier((value,) + others)[0]


def whole_block(shape):
    return pl.BlockSpec(shape, lambda *_: (0,) * len(shape))


def params(limit):
    return pltpu.CompilerParams(vmem_limit_bytes=limit * 2**20)


ANYWHERE = pl.BlockSpec(memory_space=pl.ANY)
SCALARS = pl.BlockSpec(memory_space=pltpu.SMEM)
VMEM = pl.BlockSpec(memory_space=pltpu.VMEM)
ROWS = 256


def to_blocks_kernel(n_q, n_t, heads, head_dim, units, at_ref, qkv_ref, up_ref, *out_refs):
    n_z = n_t // 2
    width = heads * head_dim
    core, z = at_ref[0], at_ref[1]
    rows = qkv_ref.shape[0]
    low = lax.broadcasted_iota(jnp.int32, (rows, 128), 1) < head_dim
    per = 128 // head_dim
    for c in range(2):
        for s in range(n_z):
            out_ref = out_refs[s].at[pl.ds(c * rows, rows)]
            t = lax.rem(core + c, 2) * n_z + (z ^ s)
            odd = lax.rem(t, per)
            for which in range(3):
                for j in range(0, heads, per):
                    tiles = []
                    for i in range(per):
                        first = (which * heads + j + i) * n_t * head_dim + (t // per) * 128
                        tile = qkv_ref[:, pl.ds(pl.multiple_of(first, 128), 128)].astype(F32)
                        tiles.append(tile)
                    even = jnp.where(low, tiles[0], pltpu.roll(tiles[1], head_dim, 1))
                    uneven = jnp.where(low, pltpu.roll(tiles[0], head_dim, 1), tiles[1])
                    at = which * width + j * head_dim
                    out_ref[:, at : at + 128] = jnp.where(odd == 0, even, uneven).astype(BF)
            for q in range(n_q):
                at = 3 * width + q * units
                if units % 128 == 0:
                    first = pl.multiple_of((q * n_t + t) * units, 128)
                    out_ref[:, at : at + units] = up_ref[:, pl.ds(first, units)]
                else:
                    for k in range(n_t):

                        @pl.when(t == k)
                        def _(at=at, q=q, k=k):
                            first = (q * n_t + k) * units
                            out_ref[:, at : at + units] = up_ref[:, first : first + units]


def to_blocks(at, qkv, up, n_q, n_t, heads, head_dim, units):
    rows = qkv.shape[0]
    wide = 3 * heads * head_dim + n_q * units
    return pl.pallas_call(
        partial(to_blocks_kernel, n_q, n_t, heads, head_dim, units),
        in_specs=[SCALARS, VMEM, VMEM],
        out_specs=[VMEM] * (n_t // 2),
        out_shape=[jax.ShapeDtypeStruct((2 * rows, wide), BF)] * (n_t // 2),
        compiler_params=params(16),
        cost_estimate=cost(0, 4 * rows * wide * n_t),
        name="to_blocks",
    )(at, qkv, up)


def theirs_kernel(*refs):
    pieces, out_ref = refs[:-1], refs[-1]
    rows = pieces[0].shape[0] // 2
    for s, piece in enumerate(pieces):
        out_ref[s * rows : (s + 1) * rows, :] = piece[rows:, :]


def theirs(pieces):
    rows, columns = pieces[0].shape
    return pl.pallas_call(
        theirs_kernel,
        in_specs=[VMEM] * len(pieces),
        out_specs=VMEM,
        out_shape=jax.ShapeDtypeStruct((len(pieces) * rows // 2, columns), BF),
        compiler_params=params(16),
        cost_estimate=cost(0, 2 * len(pieces) * rows * columns),
        name="theirs",
    )(*pieces)


def piece_rows(came_refs, got_ref, at_ref):
    n_z = len(came_refs)
    rows = came_refs[0].shape[0] // 2
    core, z = at_ref[0], at_ref[1]
    for s in range(n_z):
        yield core * n_z + (z ^ s), came_refs[s][0:rows, :]
        yield (1 - core) * n_z + (z ^ s), got_ref[s * rows : (s + 1) * rows, :]


def stack_rows_kernel(at_ref, *refs):
    out_ref = refs[-1]
    for block, values in piece_rows(refs[:-2], refs[-2], at_ref):
        rows = values.shape[0]
        out_ref[pl.ds(pl.multiple_of(block * rows, 16), rows), :] = values


def stack_rows(at, came, got):
    rows, columns = came[0].shape
    return pl.pallas_call(
        stack_rows_kernel,
        in_specs=[SCALARS] + [VMEM] * (len(came) + 1),
        out_specs=VMEM,
        out_shape=jax.ShapeDtypeStruct((len(came) * rows, columns), BF),
        compiler_params=params(16),
        cost_estimate=cost(0, 4 * len(came) * rows * columns),
        name="stack_rows",
    )(at, *came, got)


def last_sum_kernel(n_z, n_parts, tail, at_ref, *refs):
    part_refs, out_refs = refs[:n_parts], refs[n_parts:]
    n_t = 2 * n_z
    below = 16 if tail else 0
    count = part_refs[0].shape[0] - tail
    rows = count // n_t
    core, z = at_ref[0], at_ref[1]
    if tail:
        total = part_refs[0][count:, :].astype(F32)
        for part_ref in part_refs[1:]:
            total = total + part_ref[count:, :].astype(F32)
        values = total[: tail // 2, :] + total[tail // 2 :, :]
        index = lax.broadcasted_iota(jnp.int32, values.shape, 0)
    for c in range(2):
        for s in range(n_z):
            block = lax.rem(core + c, 2) * n_z + (z ^ s)
            here = pl.ds(pl.multiple_of(block * rows, 16), rows)
            total = part_refs[0][here, :].astype(F32)
            for part_ref in part_refs[1:]:
                total = total + part_ref[here, :].astype(F32)
            first = c * (rows + below)
            out_refs[s][first : first + rows, :] = total.astype(BF)
            if tail:
                own = jnp.sum(jnp.where(index == block, values, 0.0), 0, keepdims=True)
                high, low = in_two(own)
                row = lax.broadcasted_iota(jnp.int32, (below, own.shape[1]), 0)
                both = jnp.where(row == 0, high.astype(F32), jnp.where(row == 1, low.astype(F32), 0.0))
                out_refs[s][first + rows : first + rows + below, :] = both.astype(BF)


def last_sum(at, parts, n_t, tail=0):
    columns = parts[0].shape[1]
    rows = 2 * ((parts[0].shape[0] - tail) // n_t + (16 if tail else 0))
    return pl.pallas_call(
        partial(last_sum_kernel, n_t // 2, len(parts), tail),
        in_specs=[SCALARS] + [VMEM] * len(parts),
        out_specs=[VMEM] * (n_t // 2),
        out_shape=[jax.ShapeDtypeStruct((rows, columns), BF)] * (n_t // 2),
        compiler_params=params(24),
        cost_estimate=cost(0, 8 * rows * n_t * columns),
        name="last_sum",
    )(at, *parts)


def from_blocks_kernel(groups, piece, below, at_ref, *refs):
    came_refs, got_ref, refs = refs[: -3 - (below > 0)], refs[-3 - (below > 0)], refs[-2 - (below > 0) :]
    out_ref, held_ref = refs[0], refs[-1]
    n_t = held_ref.shape[0]
    rows = out_ref.shape[0]
    total = 0.0
    for block, values in piece_rows(came_refs, got_ref, at_ref):
        held_ref[block] = values[0:rows, :]
        if below:
            under = values[rows:, :].astype(F32)
            total = total + under[0:1, :] + under[1:2, :]
    for t in range(n_t):
        for j in range(groups):
            first = (j * n_t + t) * piece
            out_ref[:, first : first + piece] = held_ref[t, :, j * piece : (j + 1) * piece].astype(F32)
    if below:
        refs[1][...] = jnp.broadcast_to(total, refs[1].shape)


def from_blocks(at, came, got, groups, piece, below=0):
    n_t = 2 * len(came)
    rows = came[0].shape[0] // 2 - below
    columns = groups * piece
    return pl.pallas_call(
        partial(from_blocks_kernel, groups, piece, below),
        in_specs=[SCALARS] + [VMEM] * (len(came) + 1),
        out_specs=[VMEM] * (1 + (below > 0)),
        out_shape=[jax.ShapeDtypeStruct((rows, columns * n_t), F32)]
        + [jax.ShapeDtypeStruct((8, columns), F32)] * (below > 0),
        scratch_shapes=[pltpu.VMEM((n_t, rows, columns), BF)],
        compiler_params=params(16),
        cost_estimate=cost(0, 8 * rows * columns * n_t),
        name="from_blocks",
    )(at, *came, got)


def places_kernel(n_q, n_z, q_order, at_ref, table_ref, turns_ref, order_ref):
    q, z = at_ref[2], at_ref[1]
    place = 0
    for i, index in enumerate(q_order):
        place = place + jnp.where(q == index, i, 0)
    for k, offset in enumerate(ring_offsets(n_q)):
        at = lax.rem(place + offset + n_q, n_q)
        turn_of = 0
        for i, index in enumerate(q_order):
            turn_of = turn_of + jnp.where(at == i, index, 0)
        turns_ref[k] = turn_of
    for k, offset in enumerate(ring_offsets(n_z)):
        row = lax.rem(z + offset + n_z, n_z)
        for j in range(2):
            order_ref[table_ref[row, j]] = 2 * k + j


def find_places(at, span_table, n_q, n_z, q_order):
    return pl.pallas_call(
        partial(places_kernel, n_q, n_z, q_order),
        in_specs=[SCALARS, SCALARS],
        out_specs=[SCALARS, SCALARS],
        out_shape=[jax.ShapeDtypeStruct((n_q,), jnp.int32), jax.ShapeDtypeStruct((2 * n_z,), jnp.int32)],
        cost_estimate=cost(0, 1000),
        name="places",
    )(at, span_table)


def pack_small_kernel(*refs):
    out_ref = refs[-1]
    row = 0
    for ref in refs[:-1]:
        size = ref.shape[1]
        for first in range(0, size, 128):
            count = min(128, size - first)
            out_ref[row : row + 1, 0:count] = ref[:, first : first + count].astype(F32).astype(BF)
            row += 1


def pack_small(vectors):
    return pl.pallas_call(
        pack_small_kernel,
        in_specs=[VMEM] * len(vectors),
        out_specs=VMEM,
        out_shape=jax.ShapeDtypeStruct((256, 128), BF),
        cost_estimate=cost(0, 65536),
        name="pack_small",
    )(*[v.reshape(1, -1) for v in vectors])


def pack_vectors_kernel(shape, widths, at_ref, norm_a_ref, norm_b_ref, g_ref, up_ref, out_ref):
    n_q, n_t, heads, head_dim, units = shape
    part, biases = widths
    t_here = at_ref[0] * (n_t // 2) + at_ref[1]
    gain = norm_a_ref[0:1, :] + norm_b_ref[0:1, :]
    shift = norm_a_ref[1:2, :] + norm_b_ref[1:2, :]
    qkv = norm_a_ref[2:3, :] + norm_b_ref[2:3, :]
    g = g_ref[0:1, :]
    up = up_ref[0:1, :]
    columns = out_ref.shape[2]
    for q in range(n_q):
        lines = []
        for t in range(n_t):
            owner = q * n_t + t
            here = slice(owner * part, (owner + 1) * part)
            cells = [gain[:, here], shift[:, here], g[:, here]]
            first, end = owner * biases, (owner + 1) * biases
            while first < end:
                which, head = first // (HEADS * head_dim), first // head_dim % HEADS
                stop = min(end, (first // head_dim + 1) * head_dim)
                source = (which * heads + head // n_t) * head_dim + first % head_dim
                cells.append(jnp.where(t_here == head % n_t, qkv[:, source : source + stop - first], 0.0))
                first = stop
            cells.append(jnp.where(t_here == t, up[:, q * units : (q + 1) * units], 0.0))
            used = 3 * part + biases + units
            cells.append(jnp.zeros((1, columns - used), F32))
            lines.append(jnp.concatenate(cells, 1))
        high, low = in_two(jnp.concatenate(lines, 0))
        out_ref[q, 0:n_t, :] = high
        out_ref[q, n_t:, :] = low


def pack_vectors(at, norm_a, norm_b, g, up, shape, widths, columns):
    n_q, n_t = shape[:2]
    return pl.pallas_call(
        partial(pack_vectors_kernel, shape, widths),
        in_specs=[SCALARS] + [VMEM] * 4,
        out_specs=VMEM,
        out_shape=jax.ShapeDtypeStruct((n_q, 2 * n_t, columns), BF),
        cost_estimate=cost(0, 4 * n_q * n_t * columns),
        name="pack_vectors",
    )(at, norm_a, norm_b, g, up)


def load_pieces(plan, turns_ref, piece_refs, target, sem):
    copies = []
    for i, (piece, first, rows, slot, scale, base) in enumerate(plan):
        start = pl.multiple_of(turns_ref[slot] * scale + base, 16)
        copies.append(pltpu.make_async_copy(piece_refs[piece].at[pl.ds(first, rows)], target.at[pl.ds(start, rows)], sem.at[i]))
    return copies


def fetch_slots(plan, slot_refs, buffers, sems):
    i = pl.program_id(0)

    def copies(k):
        return [
            pltpu.make_async_copy(slot_refs[which], buffers.at[k % 2, pl.ds(first, rows)], sems.at[k % 2, part])
            for part, (which, first, rows) in enumerate(plan[k])
        ]

    for k in range(len(plan)):

        @pl.when(i == k)
        def _(k=k):
            for copy in (copies(0) if k == 0 else []) + (copies(k + 1) if k + 1 < len(plan) else []):
                copy.start()
            for copy in copies(k):
                copy.wait()


class Gathered:
    def __init__(self, arrays, plan, turns):
        self.arrays = arrays
        self.plan = tuple(plan)
        self.starts = turns
        self.rows = sum(piece[2] for piece in plan)
        self.columns = arrays[0].shape[1]

    def scratch(self):
        return [pltpu.VMEM((self.rows, self.columns), BF), pltpu.SemaphoreType.DMA((len(self.plan),))]

    def specs(self):
        return [ANYWHERE] * len(self.arrays)


def put_block(plan, block, held_ref, out_refs, sem):
    i = pl.program_id(0)
    held_ref[i] = block

    def copies(k):
        return [
            pltpu.make_async_copy(held_ref.at[k, pl.ds(first, rows)], out_refs[which], sem.at[which])
            for which, first, rows in plan[k]
        ]

    for k in range(len(plan)):

        @pl.when(i == k)
        def _(k=k):
            for copy in copies(k):
                copy.start()

    @pl.when(i == len(plan) - 1)
    def _():
        for k in range(len(plan)):
            for copy in copies(k):
                copy.wait()


def normed(rows):
    mean = jnp.mean(rows, -1, keepdims=True)
    centred = rows - mean
    scale = lax.rsqrt(jnp.mean(centred * centred, -1, keepdims=True) + EPS)
    return centred * scale, scale


def project_kernel(split, x_plan, n_x, w_plan, n_w, starts_ref, *refs):
    x_refs, refs = refs[:n_x], refs[n_x:]
    w_refs, refs = refs[:n_w], refs[n_w:]
    gain_ref, shift_ref, b_ref, x_out_ref, hidden_ref, qkv_ref, act_ref, slope_ref, w_ref, w_sem, x_buf, x_sem = refs

    @pl.when(pl.program_id(0) == 0)
    def _():
        for copy in load_pieces(w_plan, starts_ref, w_refs, w_ref, w_sem):
            copy.start()

    fetch_slots(x_plan, x_refs, x_buf, x_sem)
    x = x_buf[lax.rem(pl.program_id(0), 2)]
    x_out_ref[...] = x
    xhat, _ = normed(x.astype(F32))
    hidden = (xhat * gain_ref[...] + shift_ref[...]).astype(BF)
    hidden_ref[...] = hidden

    @pl.when(pl.program_id(0) == 0)
    def _():
        for copy in load_pieces(w_plan, starts_ref, w_refs, w_ref, w_sem):
            copy.wait()

    pre = dot(hidden, w_ref[:, split:]) + b_ref[:, split:]
    root = math.sqrt(2.0 / math.pi)
    square = pre * pre
    turned = jnp.tanh(root * pre * (1.0 + 0.044715 * square))
    act_ref[...] = (0.5 * pre * (1.0 + turned)).astype(BF)
    slope = 0.5 * (1.0 + turned) + 0.5 * pre * (1.0 - turned * turned) * (root * (1.0 + 3 * 0.044715 * square))
    slope_ref[...] = slope.astype(BF)
    qkv_ref[...] = dot(hidden, w_ref[:, :split]) + b_ref[:, :split]


def project(x_arrays, x_plan, gain, shift, w, b, split):
    rows, width = x_arrays[0].shape
    count = rows * len(x_plan)
    wide = w.columns

    def block(columns):
        return pl.BlockSpec((rows, columns), lambda i, s: (i, 0))

    return pl.pallas_call(
        partial(project_kernel, split, x_plan, len(x_arrays), w.plan, len(w.arrays)),
        grid_spec=pltpu.PrefetchScalarGridSpec(
            num_scalar_prefetch=1,
            grid=(len(x_plan),),
            in_specs=[ANYWHERE] * len(x_arrays) + w.specs() + [whole_block((1, width))] * 2 + [whole_block(b.shape)],
            out_specs=[block(width), block(width), block(split), block(wide - split), block(wide - split)],
            scratch_shapes=w.scratch() + [pltpu.VMEM((2, rows, width), BF), pltpu.SemaphoreType.DMA((2, 2))],
        ),
        out_shape=[
            jax.ShapeDtypeStruct((count, width), BF),
            jax.ShapeDtypeStruct((count, width), BF),
            jax.ShapeDtypeStruct((count, split), F32),
            jax.ShapeDtypeStruct((count, wide - split), BF),
            jax.ShapeDtypeStruct((count, wide - split), BF),
        ],
        compiler_params=params(36),
        cost_estimate=cost(2 * count * width * wide, 8 * count * width + 2 * width * wide),
        name="project",
    )(w.starts, *x_arrays, *w.arrays, gain, shift, b)


def combine_kernel(split, w_plan, n_w, plan, n_arrived, starts_ref, act_ref, att_ref, *refs):
    w_refs, refs = refs[:n_w], refs[n_w:]
    arrived_refs, refs = refs[:n_arrived], refs[n_arrived:]
    out_refs, (w_ref, w_sem, held, held_sem, buf, buf_sem) = refs[:-6], refs[-6:]

    @pl.when(pl.program_id(0) == 0)
    def _():
        copies = load_pieces(w_plan, starts_ref, w_refs, w_ref, w_sem)
        for copy in copies:
            copy.start()
        for copy in copies:
            copy.wait()

    total = dot(act_ref[...], w_ref[:split, :]) + dot(att_ref[...], w_ref[split:, :])
    if n_arrived:
        fetch_slots([((k, 0, total.shape[0]),) for k in range(n_arrived)], arrived_refs, buf, buf_sem)
        total = total + buf[lax.rem(pl.program_id(0), 2)].astype(F32)
    put_block(plan, total.astype(BF), held, out_refs, held_sem)


def held_blocks(steps, rows, width):
    return [pltpu.VMEM((steps, rows, width), BF), pltpu.SemaphoreType.DMA((steps + 1,))]


def combine(act, att, w, part, rows, arrived=()):
    count, split = act.shape[0] // 2, act.shape[1]
    own_width = att.shape[-1]
    att = att.reshape(count, own_width)
    width = w.columns
    steps = count // rows
    base = part * steps
    plan = slot_plan(steps, rows) if arrived else [((k, 0, rows),) for k in range(steps)]
    shapes = [jax.ShapeDtypeStruct((r, width), BF) for slot in plan for _, _, r in slot]
    return pl.pallas_call(
        partial(combine_kernel, split, w.plan, len(w.arrays), plan, len(arrived)),
        grid_spec=pltpu.PrefetchScalarGridSpec(
            num_scalar_prefetch=1,
            grid=(steps,),
            in_specs=[
                pl.BlockSpec((rows, split), lambda i, s: (i + base, 0)),
                pl.BlockSpec((rows, own_width), lambda i, s: (i, 0)),
            ]
            + w.specs()
            + [ANYWHERE] * len(arrived),
            out_specs=[ANYWHERE] * len(shapes),
            scratch_shapes=w.scratch()
            + held_blocks(steps, rows, width)
            + [pltpu.VMEM((2, rows, width), BF), pltpu.SemaphoreType.DMA((2, 2))],
        ),
        out_shape=shapes,
        compiler_params=params(32),
        cost_estimate=cost(2 * count * width * w.rows, 4 * count * width + 2 * width * w.rows),
        name="combine",
    )(w.starts, act, att, *w.arrays, *arrived)


def combine_back_kernel(split, g_plan, n_g, w_plan, n_w, starts_ref, *refs):
    g_refs, refs = refs[:n_g], refs[n_g:]
    w_refs, refs = refs[:n_w], refs[n_w:]
    slope_ref, g_out_ref, pre_grad_ref, att_grad_ref, sums_ref, w_ref, w_sem, g_buf, g_sem = refs

    @pl.when(pl.program_id(0) == 0)
    def _():
        for copy in load_pieces(w_plan, starts_ref, w_refs, w_ref, w_sem):
            copy.start()

    fetch_slots(g_plan, g_refs, g_buf, g_sem)

    @pl.when(pl.program_id(0) == 0)
    def _():
        for copy in load_pieces(w_plan, starts_ref, w_refs, w_ref, w_sem):
            copy.wait()

    grad = g_buf[lax.rem(pl.program_id(0), 2)]
    g_out_ref[...] = grad

    @pl.when(pl.program_id(0) == 0)
    def _():
        sums_ref[...] = jnp.zeros_like(sums_ref)
        sums_ref[0:1, :] = jnp.sum(grad.astype(F32), 0, keepdims=True)

    pre_grad_ref[...] = (dot_t(grad, w_ref[:split, :]) * slope_ref[...].astype(F32)).astype(BF)
    att_grad_ref[...] = dot_t(grad, w_ref[split:, :]).astype(BF)


def combine_back(g_arrays, g_plan, w, slope):
    rows, width = g_arrays[0].shape
    count = rows * len(g_plan)
    split = slope.shape[1]
    rest = w.rows - split

    def block(columns):
        return pl.BlockSpec((rows, columns), lambda i, s: (i, 0))

    return pl.pallas_call(
        partial(combine_back_kernel, split, g_plan, len(g_arrays), w.plan, len(w.arrays)),
        grid_spec=pltpu.PrefetchScalarGridSpec(
            num_scalar_prefetch=1,
            grid=(len(g_plan),),
            in_specs=[ANYWHERE] * len(g_arrays) + w.specs() + [block(split)],
            out_specs=[block(width), block(split), block(rest), whole_block((8, width))],
            scratch_shapes=w.scratch() + [pltpu.VMEM((2, rows, width), BF), pltpu.SemaphoreType.DMA((2, 2))],
        ),
        out_shape=[
            jax.ShapeDtypeStruct((count, width), BF),
            jax.ShapeDtypeStruct((count, split), BF),
            jax.ShapeDtypeStruct((count, rest), BF),
            jax.ShapeDtypeStruct((8, width), F32),
        ],
        compiler_params=params(32),
        cost_estimate=cost(2 * count * width * w.rows, 6 * count * width + 2 * width * w.rows),
        name="combine_back",
    )(w.starts, *g_arrays, *w.arrays, slope)


def project_back_kernel(split, w_plan, n_w, plan, n_arrived, starts_ref, qkv_grad_ref, pre_grad_ref, x_ref, *refs):
    w_refs, refs = refs[:n_w], refs[n_w:]
    arrived_refs, refs = refs[:n_arrived], refs[n_arrived:]
    out_refs, (sums_ref, w_ref, w_sem, held, held_sem, buf, buf_sem) = refs[:-7], refs[-7:]

    @pl.when(pl.program_id(0) == 0)
    def _():
        copies = load_pieces(w_plan, starts_ref, w_refs, w_ref, w_sem)
        for copy in copies:
            copy.start()
        sums_ref[...] = jnp.zeros_like(sums_ref)
        for copy in copies:
            copy.wait()

    grad = dot_t(qkv_grad_ref[...], w_ref[:, :split]) + dot_t(pre_grad_ref[...], w_ref[:, split:])
    xhat, _ = normed(x_ref[...].astype(F32))
    sums_ref[0:1, :] += jnp.sum(grad * xhat, 0, keepdims=True)
    sums_ref[1:2, :] += jnp.sum(grad, 0, keepdims=True)
    sums_ref[2:3, 0:split] += jnp.sum(qkv_grad_ref[...].astype(F32), 0, keepdims=True)
    if n_arrived:
        fetch_slots([((k, 0, grad.shape[0]),) for k in range(n_arrived)], arrived_refs, buf, buf_sem)
        grad = grad + buf[lax.rem(pl.program_id(0), 2)].astype(F32)
    put_block(plan, grad.astype(BF), held, out_refs, held_sem)


def project_back(qkv_grad, pre_grad, w, x, part, rows, arrived=()):
    count, width = x.shape[0] // 2, x.shape[1]
    split = qkv_grad.shape[1]
    steps = count // rows
    base = part * steps
    plan = slot_plan(steps, rows) if arrived else [((k, 0, rows),) for k in range(steps)]
    shapes = [jax.ShapeDtypeStruct((r, width), BF) for slot in plan for _, _, r in slot]

    def block(columns):
        return pl.BlockSpec((rows, columns), lambda i, s: (i + base, 0))

    *out, sums = pl.pallas_call(
        partial(project_back_kernel, split, w.plan, len(w.arrays), plan, len(arrived)),
        grid_spec=pltpu.PrefetchScalarGridSpec(
            num_scalar_prefetch=1,
            grid=(steps,),
            in_specs=[block(split), block(pre_grad.shape[1]), block(width)] + w.specs() + [ANYWHERE] * len(arrived),
            out_specs=[ANYWHERE] * len(shapes) + [whole_block((8, width))],
            scratch_shapes=w.scratch()
            + held_blocks(steps, rows, width)
            + [pltpu.VMEM((2, rows, width), BF), pltpu.SemaphoreType.DMA((2, 2))],
        ),
        out_shape=shapes + [jax.ShapeDtypeStruct((8, width), F32)],
        compiler_params=params(36),
        cost_estimate=cost(2 * count * width * w.columns, 6 * count * width + 2 * width * w.columns),
        name="project_back",
    )(w.starts, qkv_grad, pre_grad, x, *w.arrays, *arrived)
    return out, sums


def weight_grad_kernel(with_tail, turns_ref, left_ref, right_ref, *refs):
    tail_refs, refs = refs[:with_tail], refs[with_tail:]
    out_refs, (sums_ref, held, sem) = refs[:-3], refs[-3:]

    @pl.when(pl.program_id(0) == 0)
    def _():
        sums_ref[...] = jnp.zeros_like(sums_ref)
        sums_ref[0:1, :] = jnp.sum(right_ref[...].astype(F32), 0, keepdims=True)

    block = t_dot(left_ref[...], right_ref[...]).astype(BF)
    if with_tail:
        block = jnp.concatenate([block, tail_refs[0][0]], 0)
    put_block(slot_plan(held.shape[0], held.shape[1]), block, held, out_refs, sem)


def slot_shapes(n, rows, columns):
    return [jax.ShapeDtypeStruct((r, columns), BF) for slot in slot_plan(n, rows) for _, _, r in slot]


def weight_grad(turns, left, right, tail=None):
    n_q = turns.shape[0]
    count, wide = left.shape
    columns = right.shape[1]
    part = wide // n_q
    rows = part + (0 if tail is None else tail.shape[1])
    extra = [] if tail is None else [tail]
    shapes = slot_shapes(n_q, rows, columns)
    *out, sums = pl.pallas_call(
        partial(weight_grad_kernel, len(extra)),
        grid_spec=pltpu.PrefetchScalarGridSpec(
            num_scalar_prefetch=1,
            grid=(n_q,),
            in_specs=[pl.BlockSpec((count, part), lambda k, s: (0, s[k])), whole_block(right.shape)]
            + [pl.BlockSpec((1,) + v.shape[1:], lambda k, s: (s[k], 0, 0)) for v in extra],
            out_specs=[ANYWHERE] * len(shapes) + [whole_block((8, columns))],
            scratch_shapes=held_blocks(n_q, rows, columns),
        ),
        out_shape=shapes + [jax.ShapeDtypeStruct((8, columns), F32)],
        compiler_params=params(40),
        cost_estimate=cost(2 * count * wide * columns, 2 * count * (wide + columns) + 2 * wide * columns),
        name="weight_grad",
    )(turns, left, right, *extra)
    return out, sums


def down_grad_kernel(head_rows, turns_ref, act_ref, att_a_ref, att_b_ref, g_ref, *refs):
    out_refs, (heads_ref, held, sem) = refs[:-3], refs[-3:]
    units = act_ref.shape[1]
    k = pl.program_id(0)

    @pl.when(k == 0)
    def _():
        half = att_a_ref.shape[0]
        heads_ref[...] = (t_dot(att_a_ref[...], g_ref[0:half, :]) + t_dot(att_b_ref[...], g_ref[half:, :])).astype(BF)

    rows = pl.ds(pl.multiple_of(turns_ref[k] * head_rows, head_rows), head_rows)
    block = jnp.concatenate([t_dot(act_ref[...], g_ref[...]).astype(BF), heads_ref[rows, :]], 0)
    put_block(slot_plan(held.shape[0], held.shape[1]), block, held, out_refs, sem)


def down_grad(turns, act, att, g, head_rows):
    n_q = turns.shape[0]
    count, wide = act.shape
    own_width = att[0].shape[-1]
    att = [a.reshape(count // 2, own_width) for a in att]
    width = g.shape[1]
    units = wide // n_q
    if not head_rows:
        whole = t_dot(act, g).astype(BF).reshape(n_q, units, width)[turns]
        blocks = [whole[k][first : first + r] for k, slot in enumerate(slot_plan(n_q, units)) for _, first, r in slot]
        return blocks, t_dot(jnp.concatenate(att, 0), g)
    out = pl.pallas_call(
        partial(down_grad_kernel, head_rows),
        grid_spec=pltpu.PrefetchScalarGridSpec(
            num_scalar_prefetch=1,
            grid=(n_q,),
            in_specs=[pl.BlockSpec((count, units), lambda k, s: (0, s[k]))] + [whole_block(v.shape) for v in (*att, g)],
            out_specs=[ANYWHERE] * (n_q + 1),
            scratch_shapes=[pltpu.VMEM((own_width, width), BF)] + held_blocks(n_q, units + head_rows, width),
        ),
        out_shape=slot_shapes(n_q, units + head_rows, width),
        compiler_params=params(40),
        cost_estimate=cost(2 * count * (wide + own_width) * width, 2 * count * (wide + width) + 2 * wide * width),
        name="down_grad",
    )(turns, act, *att, g)
    return list(out), None


def finish_kernel(x_ref, g_ref, gain_ref, *refs):
    part_refs, out_ref = refs[:-1], refs[-1]
    grad = part_refs[0][...].astype(F32)
    for part_ref in part_refs[1:]:
        grad = grad + part_ref[...].astype(F32)
    xhat, scale = normed(x_ref[...].astype(F32))
    m = grad * gain_ref[...]
    x_grad = (m - jnp.mean(m, -1, keepdims=True) - xhat * jnp.mean(m * xhat, -1, keepdims=True)) * scale
    out_ref[...] = (g_ref[...].astype(F32) + x_grad).astype(BF)


def finish(parts, x, g, gain):
    count, width = x.shape
    rows = math.gcd(count, 64)
    block = pl.BlockSpec((rows, width), lambda i: (i, 0))
    return pl.pallas_call(
        finish_kernel,
        grid=(count // rows,),
        in_specs=[block] * 2 + [whole_block((1, width))] + [block] * len(parts),
        out_specs=block,
        out_shape=jax.ShapeDtypeStruct((count, width), BF),
        cost_estimate=cost(20 * count * width, 12 * count * width),
        name="finish",
    )(x, g, gain, *parts)


def output_kernel(x_ref, bias_ref, *refs):
    part_refs, out_ref = refs[:-1], refs[-1]
    total = x_ref[...].astype(F32) + bias_ref[...]
    for part_ref in part_refs:
        total = total + part_ref[...].astype(F32)
    out_ref[...] = total.astype(BF)


def output_sum(x, bias, parts):
    count, width = x.shape
    rows = math.gcd(count, 64)
    block = pl.BlockSpec((rows, width), lambda i: (i, 0))
    return pl.pallas_call(
        output_kernel,
        grid=(count // rows,),
        in_specs=[block, whole_block((1, width))] + [block] * len(parts),
        out_specs=block,
        out_shape=jax.ShapeDtypeStruct((count, width), BF),
        cost_estimate=cost(4 * count * width, 10 * count * width),
        name="output_sum",
    )(x, bias, *parts)


def split_sum(parts, cuts):
    count, width = parts[0].shape
    wide = math.gcd(width, 512)
    ends = [sum(cuts[: i + 1]) for i in range(len(cuts))]

    def kernel(*refs):
        part_refs, out_refs = refs[: len(parts)], refs[len(parts) :]
        total = part_refs[0][...].astype(F32)
        for part_ref in part_refs[1:]:
            total = total + part_ref[...].astype(F32)
        for end, rows, out_ref in zip(ends, cuts, out_refs):
            out_ref[...] = total[end - rows : end, :]

    return pl.pallas_call(
        kernel,
        grid=(width // wide,),
        in_specs=[pl.BlockSpec((count, wide), lambda i: (0, i))] * len(parts),
        out_specs=[pl.BlockSpec((rows, wide), lambda i: (0, i)) for rows in cuts],
        out_shape=[jax.ShapeDtypeStruct((rows, width), F32) for rows in cuts],
        cost_estimate=cost(4 * count * width, 12 * count * width),
        name="split_sum",
    )(*parts)


def tables_kernel(head_dim, cos_ref, sin_a_ref, sin_b_ref):
    rows = cos_ref.shape[0]
    half = ROT // 2
    lane = lax.broadcasted_iota(jnp.int32, (1, 128), 1) % head_dim
    step = (lane % half).astype(F32) * (-2.0 * math.log(10000.0) / ROT)
    freqs = jnp.where(lane < ROT, jnp.exp(step), 0.0)
    position = lax.broadcasted_iota(jnp.int32, (rows, 128), 0) + pl.program_id(0) * rows
    angles = position.astype(F32) * freqs
    cosine, sine = jnp.cos(angles), jnp.sin(angles)
    cos_ref[...] = cosine
    sin_a_ref[...] = jnp.where(lane < half, -sine, 0.0)
    sin_b_ref[...] = jnp.where((lane >= half) & (lane < ROT), sine, 0.0)


def rotary_tables(seq_len, head_dim):
    width = 128
    block = pl.BlockSpec((128, width), lambda i: (i, 0))
    return pl.pallas_call(
        partial(tables_kernel, head_dim),
        grid=(seq_len // 128,),
        out_specs=[block] * 3,
        out_shape=[jax.ShapeDtypeStruct((seq_len, width), F32)] * 3,
        cost_estimate=cost(100 * seq_len * width, 12 * seq_len * width),
        name="rotary_tables",
    )()


def per_device(
    inputs,
    span_table,
    ln_gain,
    ln_bias,
    qkv_weight,
    qkv_bias,
    out_weight,
    out_bias,
    fc1_weight,
    fc1_bias,
    fc2_weight,
    fc2_bias,
    cotangent,
):
    rows, width = inputs.shape
    head_dim = width // HEADS
    n_q, n_z = lax.axis_size("q"), lax.axis_size("ctx")
    n_t = 2 * n_z
    n_all = n_q * n_t
    q, core, z = lax.axis_index("q"), lax.axis_index("core"), lax.axis_index("ctx")
    t = core * n_z + z
    at = jnp.stack([core, z, q]).astype(jnp.int32)
    span = rows // 2
    seq_len = rows * n_z
    heads = HEADS // n_t
    own_width = heads * head_dim
    split = 3 * own_width
    units = fc2_weight.shape[0]
    own_units = units * n_q
    d_rows = qkv_weight.shape[0]
    every = ("q", "core", "ctx")
    z_order = list(range(n_z))
    q_order = [0, 1, 3, 2] if n_q == 4 else list(range(n_q))
    turns, order = find_places(at, span_table, n_q, n_z, q_order)
    whole_heads = out_weight.shape[0] == head_dim

    tables = rotary_tables(seq_len, head_dim)

    owned = [ln_gain, ln_bias, out_bias, fc2_bias, qkv_bias, fc1_bias]
    small = lax.all_gather(pack_small(owned), every, axis=0, tiled=True)

    came = scattered(to_blocks(at, qkv_weight, fc1_weight, n_q, n_t, heads, head_dim, units), "ctx")
    w2_block = jnp.concatenate([fc2_weight, out_weight], 0) if whole_heads else fc2_weight
    w2_arrays = ring_gathered(w2_block, "q", q_order)
    plan = []
    for slot, pieces in enumerate(slot_plan(n_q, w2_block.shape[0])):
        for which, first, count in pieces:
            if first < units:
                plan.append((which, 0, min(first + count, units) - first, slot, units, first))
            if first + count > units:
                begin = max(first, units)
                plan.append((which, begin - first, first + count - begin, slot, head_dim, own_units + begin - units))
    w2_sent = w2_arrays[1:]
    if not whole_heads:
        w_out = lax.all_gather(out_weight, every, axis=0, tiled=True).reshape(heads, n_t, head_dim, width)
        w2_arrays = w2_arrays + [lax.dynamic_index_in_dim(w_out, t, 1, False).reshape(own_width, width)]
        plan.append((len(w2_arrays) - 1, 0, own_width, 0, 0, own_units))
    w2 = Gathered(w2_arrays, plan, turns)

    got = swap(theirs([after(came[0], *w2_sent[:-2], turns, order)] + came[1:]))
    w1_block = stack_rows(at, came, got)
    w1_arrays = ring_gathered(w1_block, "q", q_order)
    block_rows = n_t * d_rows
    w1_plan = [
        (which, 0, count, slot, block_rows, first)
        for slot, pieces in enumerate(slot_plan(n_q, block_rows))
        for which, first, count in pieces
    ]
    w1 = Gathered(w1_arrays, w1_plan, turns)

    token_plan = slot_plan(n_z, rows) + slot_plan(n_z, rows, n_z + 1)
    x_line = ring_gathered(after(inputs, *w2_sent[:-2]), "ctx", z_order, w1_arrays[1:-2])
    x_arrays = x_line + [swap(p) for p in x_line[:-2]] + [swap(after(p, *w1_arrays[-2:])) for p in x_line[-2:]]

    small = after(small, *x_line[-2:])
    small = small.reshape(n_all, 256, 128)[:, :16]
    lists, row = [], 0
    for vector in owned:
        used = -(-vector.shape[0] // 128)
        lists.append(small[:, row : row + used].reshape(n_all, used * 128)[:, : vector.shape[0]].astype(F32))
        row += used
    gain, shift, b_out, b_down = (v.reshape(1, width) for v in lists[:4])
    b_qkv = lax.dynamic_index_in_dim(lists[4].reshape(3, heads, n_t, head_dim), t, 2, False).reshape(1, split)
    b_up = lax.dynamic_index_in_dim(lists[5].reshape(n_q, n_t, units), t, 1, False).reshape(1, own_units)
    b_project = jnp.concatenate([b_qkv, b_up], 1)

    x_all, hidden, qkv, act, slope = project(x_arrays, token_plan, gain, shift, w1, b_project, split)
    att_other, kept_other = attend(order, qkv, tables, heads, head_dim, span, 1)
    out_other = combine(act, att_other, w2, 1, rows)
    g_line = ring_gathered(after(cotangent, *x_line[-2:]), "ctx", z_order, out_other)
    att_own, kept_own = attend(order, after(qkv, *out_other, *g_line[1:-2]), tables, heads, head_dim, span, 0)
    out_own = combine(act, att_own, w2, 0, rows, [swap(p) for p in out_other])
    g_arrays = g_line + [swap(p) for p in g_line[:-2]] + [swap(after(p, *out_own)) for p in g_line[-2:]]

    g_all, pre_grad, att_grad, g_sums = combine_back(g_arrays, token_plan, w2, after(slope, *out_own))
    up_own, up_sums = weight_grad(turns, hidden, pre_grad)
    out_parts, out_sent = ring_sum(out_own, "ctx", z_order, up_own)
    att_grad = after(att_grad, *up_own, *out_sent).reshape(2, seq_len, own_width)
    qkv_grad = attend_back(order, (kept_own, kept_other), att_grad, tables, heads, head_dim, span).reshape(2 * seq_len, split)
    up_parts, up_sent = ring_sum(up_own, "q", q_order, [qkv_grad])
    normed_other, sums_other = project_back(after(qkv_grad, *up_sent), pre_grad, w1, x_all, 1, rows)
    down, out_apart = down_grad(turns, after(act, *normed_other, *out_parts[1:]), (att_own, att_other), g_all, head_dim if whole_heads else 0)
    up_came = scattered(last_sum(at, [after(up_parts[0], *down)] + up_parts[1:], n_t), "ctx")
    normed_own, sums_own = project_back(
        after(qkv_grad, *down), pre_grad, w1, x_all, 0, rows, [swap(p) for p in normed_other]
    )
    down_parts, _ = ring_sum(down, "q", q_order, normed_own)
    vectors = pack_vectors(
        at, sums_own, sums_other, g_sums, up_sums, (n_q, n_t, heads, head_dim, units), (d_rows, qkv_bias.shape[0]), split
    )
    qkv_own, _ = weight_grad(turns, after(hidden, *normed_own), qkv_grad, vectors)
    normed_parts, normed_sent = ring_sum([after(p, *up_came[1:]) for p in normed_own], "ctx", z_order, qkv_own)
    qkv_parts, qkv_sent = ring_sum(qkv_own, "q", q_order, normed_sent, 2 * n_t)
    output = output_sum(inputs, b_out + b_down, [after(out_parts[0], *normed_sent)] + out_parts[1:])

    qkv_came = scattered(last_sum(at, qkv_parts, n_t, 2 * n_t), "ctx")
    up_got = swap(theirs([after(up_came[0], *normed_parts[1:], output)] + up_came[1:]))
    (fc1_weight_grad,) = from_blocks(at, up_came, up_got, n_q, units)
    qkv_got = swap(theirs([after(qkv_came[0], up_got)] + qkv_came[1:]))
    qkv_weight_grad, total = from_blocks(at, qkv_came, qkv_got, 3 * heads, head_dim, 16)
    total = total[0]
    if whole_heads:
        fc2_weight_grad, out_weight_grad = split_sum(down_parts, [units, head_dim])
    else:
        (fc2_weight_grad,) = split_sum(down_parts, [units])
        spread = jnp.zeros((heads, n_t, head_dim, width), F32)
        spread = lax.dynamic_update_slice(spread, out_apart.reshape(heads, 1, head_dim, width), (0, t, 0, 0))
        out_weight_grad = lax.psum_scatter(spread.reshape(width, width), every, scatter_dimension=0, tiled=True)

    input_grad = finish(normed_parts, inputs, cotangent, gain)

    cuts = [ln_gain.shape[0], ln_bias.shape[0], out_bias.shape[0], qkv_bias.shape[0], fc1_bias.shape[0]]
    starts = [sum(cuts[:i]) for i in range(len(cuts))]
    gain_grad, shift_grad, bias_grad, qkv_bias_grad, fc1_bias_grad = (total[s : s + c] for s, c in zip(starts, cuts))
    return (
        output,
        input_grad,
        gain_grad,
        shift_grad,
        qkv_weight_grad,
        qkv_bias_grad,
        out_weight_grad,
        bias_grad,
        fc1_weight_grad,
        fc1_bias_grad,
        fc2_weight_grad,
        bias_grad,
    )


def solution(mesh):
    n_dp, n_ctx = mesh.devices.shape
    inner = Mesh(mesh.devices.reshape(n_dp // 2, 2, n_ctx), ("q", "core", "ctx"))
    every = ("q", "core", "ctx")
    matrix, vector = P(every, None), P(every)
    return jax.shard_map(
        per_device,
        mesh=inner,
        in_specs=(
            matrix,
            P(),
            vector,
            vector,
            matrix,
            vector,
            matrix,
            vector,
            matrix,
            vector,
            matrix,
            vector,
            matrix,
        ),
        out_specs=(matrix, matrix, vector, vector, matrix, vector, matrix, vector, matrix, vector, matrix, vector),
        check_vma=False,
    )
```

```python
from functools import partial
import math

import jax
import jax.numpy as jnp
from jax import lax
from jax.experimental import pallas as pl
from jax.experimental.pallas import tpu as pltpu
from jax.sharding import Mesh, PartitionSpec as P

HEADS = 32
ROT = 32
EPS = 1e-05
NEG = -1e30
BLOCK_Q = 256

BF = jnp.bfloat16
F32 = jnp.float32


def dot(a, b):
    return jnp.dot(a, b, preferred_element_type=F32)


def dot_t(a, b):
    return lax.dot_general(a, b, (((1,), (1,)), ((), ())), preferred_element_type=F32)


def t_dot(a, b):
    return lax.dot_general(a, b, (((0,), (0,)), ((), ())), preferred_element_type=F32)


def cost(flops, nbytes):
    return pl.CostEstimate(flops=flops // 1000, bytes_accessed=nbytes // 1000, transcendentals=0)


def across(value, axis, e):
    n = math.prod(lax.axis_size(a) for a in axis) if isinstance(axis, tuple) else lax.axis_size(axis)
    return lax.ppermute(value, axis, [(i, i ^ e) for i in range(n)])


def scattered(parts, axis):
    return [parts[0]] + [across(part, axis, e) for e, part in enumerate(parts) if e]


def ring_pairs(order, step):
    n = len(order)
    return [(order[i], order[(i + step) % n]) for i in range(n)]


def ring_offsets(n):
    return [0] + [o for s in range(1, n // 2) for o in (-s, s)] + [n // 2]


def half_of(rows):
    return rows // 32 * 16


def slot_plan(n, rows, first=0):
    plan = [((first + k, 0, rows),) for k in range(n - 1)]
    return plan + [((first + n - 1, 0, half_of(rows)), (first + n, half_of(rows), rows - half_of(rows)))]


def ring_halves(own, axis, order):
    n = len(order)
    up_pairs, down_pairs = ring_pairs(order, 1), ring_pairs(order, -1)
    out = [own]
    up = down = own
    half = half_of(own.shape[0])
    for _ in range(1, n // 2):
        up, down = lax.ppermute(up, axis, up_pairs), lax.ppermute(down, axis, down_pairs)
        out += [up, down]
    return out, (up[:half], down[half:])


def ring_gathered(own, axis, order, hold=()):
    out, (up, down) = ring_halves(own, axis, order)
    up, down = after(up, *hold), after(down, *hold)
    return out + [lax.ppermute(up, axis, ring_pairs(order, 1)), lax.ppermute(down, axis, ring_pairs(order, -1))]


def ring_first(parts, axis, order):
    n = len(order)
    return [
        lax.ppermute(parts[n - 1], axis, ring_pairs(order, -1)),
        lax.ppermute(parts[n], axis, ring_pairs(order, 1)),
    ]


def ring_rest(parts, arrived, axis, order, hold=(), tail=0):
    n = len(order)
    low, high = arrived
    sent = ()
    for step in range(n // 2 - 1, 0, -1):
        sent = pass_on(parts[2 * step - 1], parts[2 * step], after(low, *hold), high, tail)
        low = lax.ppermute(sent[0], axis, ring_pairs(order, -1))
        high = lax.ppermute(sent[1], axis, ring_pairs(order, 1))
    return [parts[0], low, high], sent


def ring_sum(parts, axis, order, hold=()):
    return ring_rest(parts, ring_first(parts, axis, order), axis, order, hold)


def in_two(values):
    first = values.astype(BF)
    return first, (values - first.astype(F32)).astype(BF)


def add_rows(part, arrived, tail):
    total = part.astype(F32) + arrived.astype(F32)
    if not tail:
        return total.astype(BF)
    cut, half = total.shape[0] - tail, tail // 2
    values = total[cut : cut + half, :] + total[cut + half :, :]
    return jnp.concatenate([total[:cut, :].astype(BF), *in_two(values)], 0)


def pass_on_kernel(tail, low_part_ref, high_part_ref, low_ref, high_ref, to_low_ref, to_high_ref):
    rows = low_part_ref.shape[0]
    cut = low_ref.shape[0]
    if cut < rows:
        to_low_ref[0:cut, :] = add_rows(low_part_ref[0:cut, :], low_ref[...], 0)
        to_low_ref[cut:, :] = low_part_ref[cut:, :]
        to_high_ref[0:cut, :] = high_part_ref[0:cut, :]
        to_high_ref[cut:, :] = add_rows(high_part_ref[cut:, :], high_ref[...], tail)
    else:
        to_low_ref[...] = add_rows(low_part_ref[...], low_ref[...], tail)
        to_high_ref[...] = add_rows(high_part_ref[...], high_ref[...], tail)


def pass_on(low_part, high_part, low, high, tail):
    rows, columns = low_part.shape
    wide = math.gcd(columns, 1024)

    def block(array):
        return pl.BlockSpec((array.shape[0], wide), lambda i: (0, i))

    arrays = [low_part, high_part, low, high]
    return pl.pallas_call(
        partial(pass_on_kernel, tail),
        grid=(columns // wide,),
        in_specs=[block(array) for array in arrays],
        out_specs=[block(low_part)] * 2,
        out_shape=[jax.ShapeDtypeStruct((rows, columns), BF)] * 2,
        cost_estimate=cost(2 * rows * columns, 12 * rows * columns),
        name="pass_on",
    )(*arrays)


def swap(value):
    return lax.ppermute(value, "core", [(0, 1), (1, 0)])


def turn(values, cosine, sine_a, sine_b):
    width = values.shape[1]
    cosine, sine_a, sine_b = (jnp.concatenate([v] * (width // 128), 1) for v in (cosine, sine_a, sine_b))
    return (
        values * cosine
        + pltpu.roll(values, width - ROT // 2, 1) * sine_a
        + pltpu.roll(values, ROT // 2, 1) * sine_b
    )


def head_mask(shape, head, head_dim):
    lane = lax.broadcasted_iota(jnp.int32, shape, 1)
    return (lane >= head * head_dim) & (lane < (head + 1) * head_dim)


def attend_kernel(heads, head_dim, span, order_ref, qkv_ref, cos_ref, sin_a_ref, sin_b_ref, att_ref, sorted_ref, out_scr):
    seq_len = qkv_ref.shape[1]
    width = heads * head_dim
    for slot in range(seq_len // span):
        rows = pl.ds(pl.multiple_of(order_ref[slot] * span, span), span)
        here = pl.ds(slot * span, span)
        tables = (cos_ref[here, :], sin_a_ref[here, :], sin_b_ref[here, :])
        query = turn(qkv_ref[0, rows, 0:width], *tables).astype(BF)
        sorted_ref[0, here, 0:width] = (query.astype(F32) * (head_dim**-0.5)).astype(BF)
        sorted_ref[0, here, width : 2 * width] = turn(qkv_ref[0, rows, width : 2 * width], *tables).astype(BF)
        sorted_ref[0, here, 2 * width :] = qkv_ref[0, rows, 2 * width :].astype(BF)
    block = min(BLOCK_Q, seq_len)
    for i in range(seq_len // block):
        extent = (i + 1) * block
        here = pl.ds(i * block, block)
        queries = sorted_ref[0, here, 0:width]
        keys = sorted_ref[0, 0:extent, width : 2 * width]
        values = sorted_ref[0, 0:extent, 2 * width :]
        row = lax.broadcasted_iota(jnp.int32, (block, extent), 0) + i * block
        col = lax.broadcasted_iota(jnp.int32, (block, extent), 1)
        total = jnp.zeros((block, width), F32)
        for head in range(heads):
            mask = head_mask((block, width), head, head_dim)
            scores = dot_t(jnp.where(mask, queries, jnp.zeros_like(queries)), keys)
            scores = jnp.where(col <= row, scores, NEG)
            top = jnp.max(scores, 1, keepdims=True)
            weights = jnp.exp(scores - top)
            norm = 1.0 / jnp.sum(weights, 1, keepdims=True)
            probs = (weights * norm).astype(BF)
            total = jnp.where(mask, dot(probs, values), total)
        out_scr[here, :] = total.astype(BF)
    for slot in range(seq_len // span):
        rows = pl.ds(pl.multiple_of(order_ref[slot] * span, span), span)
        att_ref[0, rows, :] = out_scr[slot * span : (slot + 1) * span, :]


def attend_back_kernel(
    heads, head_dim, span, order_ref, kept_a_ref, kept_b_ref, grad_ref, cos_ref, sin_a_ref, sin_b_ref, out_ref, grad_scr, key_scr, value_scr, sorted_ref
):
    seq_len = sorted_ref.shape[1]

    @pl.when(pl.program_id(0) == 0)
    def _():
        sorted_ref[...] = kept_a_ref[...]

    @pl.when(pl.program_id(0) == 1)
    def _():
        sorted_ref[...] = kept_b_ref[...]

    width = heads * head_dim
    for slot in range(seq_len // span):
        rows = pl.ds(pl.multiple_of(order_ref[slot] * span, span), span)
        grad_scr[slot * span : (slot + 1) * span, :] = grad_ref[0, rows, :]
    key_scr[...] = jnp.zeros_like(key_scr)
    value_scr[...] = jnp.zeros_like(value_scr)
    block = min(BLOCK_Q, seq_len)

    def put(slot, first, values):
        rows = pl.ds(pl.multiple_of(order_ref[slot] * span, span), span)
        out_ref[0, rows, first : first + width] = values.astype(BF)

    def tables(here):
        return (cos_ref[here, :], -sin_a_ref[here, :], -sin_b_ref[here, :])

    for i in range(seq_len // block):
        extent = (i + 1) * block
        here = pl.ds(i * block, block)
        queries = sorted_ref[0, here, 0:width]
        grads = grad_scr[here, :]
        keys = sorted_ref[0, 0:extent, width : 2 * width]
        values = sorted_ref[0, 0:extent, 2 * width :]
        key = lax.broadcasted_iota(jnp.int32, (extent, block), 0)
        query = lax.broadcasted_iota(jnp.int32, (extent, block), 1) + i * block
        query_grad = jnp.zeros((block, width), F32)
        for head in range(heads):
            mask = head_mask((block, width), head, head_dim)
            own_queries = jnp.where(mask, queries, jnp.zeros_like(queries))
            own_grads = jnp.where(mask, grads, jnp.zeros_like(grads))
            scores = jnp.where(key <= query, dot_t(keys, own_queries), NEG)
            weights = jnp.exp(scores - jnp.max(scores, 0, keepdims=True))
            probs = weights * (1.0 / jnp.sum(weights, 0, keepdims=True))
            probs_grad = dot_t(values, own_grads)
            delta = jnp.sum(probs * probs_grad, 0, keepdims=True)
            score_grad = (probs * (probs_grad - delta)).astype(BF)
            value_scr[0:extent, :] += dot(probs.astype(BF), own_grads)
            key_scr[0:extent, :] += dot(score_grad, own_queries)
            query_grad = jnp.where(mask, t_dot(score_grad, keys), query_grad)
        query_grad = turn(query_grad * (head_dim**-0.5), *tables(here))
        for j in range(block // span):
            put(i * (block // span) + j, 0, query_grad[j * span : (j + 1) * span])
    for slot in range(seq_len // span):
        here = pl.ds(slot * span, span)
        put(slot, width, turn(key_scr[here, :], *tables(here)))
        put(slot, 2 * width, value_scr[here, :])


def attend(order, qkv, tables, heads, head_dim, span, part):
    seq_len, wide = qkv.shape[0] // 2, qkv.shape[1]
    width = wide // 3
    whole = pl.BlockSpec((seq_len, 128), lambda s, o: (0, 0))
    return pl.pallas_call(
        partial(attend_kernel, heads, head_dim, span),
        grid_spec=pltpu.PrefetchScalarGridSpec(
            num_scalar_prefetch=1,
            grid=(1,),
            in_specs=[pl.BlockSpec((1, seq_len, wide), lambda s, o: (part, 0, 0)), whole, whole, whole],
            out_specs=[
                pl.BlockSpec((1, seq_len, width), lambda s, o: (0, 0, 0)),
                pl.BlockSpec((1, seq_len, wide), lambda s, o: (0, 0, 0)),
            ],
            scratch_shapes=[pltpu.VMEM((seq_len, width), BF)],
        ),
        out_shape=[
            jax.ShapeDtypeStruct((1, seq_len, width), BF),
            jax.ShapeDtypeStruct((1, seq_len, wide), BF),
        ],
        compiler_params=pltpu.CompilerParams(vmem_limit_bytes=40 * 2**20),
        cost_estimate=cost(8 * heads * seq_len * seq_len * head_dim, 8 * seq_len * wide),
        name="attend",
    )(order, qkv.reshape(2, seq_len, wide), *tables)


def attend_back(order, kept, grads, tables, heads, head_dim, span):
    count, (_, seq_len, wide) = len(kept), kept[0].shape
    width = wide // 3
    whole = pl.BlockSpec((seq_len, 128), lambda s, o: (0, 0))
    return pl.pallas_call(
        partial(attend_back_kernel, heads, head_dim, span),
        grid_spec=pltpu.PrefetchScalarGridSpec(
            num_scalar_prefetch=1,
            grid=(count,),
            in_specs=[
                pl.BlockSpec((1, seq_len, wide), lambda s, o: (0, 0, 0)),
                pl.BlockSpec((1, seq_len, wide), lambda s, o: (0, 0, 0)),
                pl.BlockSpec((1, seq_len, width), lambda s, o: (s, 0, 0)),
                whole,
                whole,
                whole,
            ],
            out_specs=pl.BlockSpec((1, seq_len, wide), lambda s, o: (s, 0, 0)),
            scratch_shapes=[
                pltpu.VMEM((seq_len, width), BF),
                pltpu.VMEM((seq_len, width), F32),
                pltpu.VMEM((seq_len, width), F32),
                pltpu.VMEM((1, seq_len, wide), BF),
            ],
        ),
        out_shape=jax.ShapeDtypeStruct((count, seq_len, wide), BF),
        compiler_params=params(58),
        cost_estimate=cost(20 * count * heads * seq_len * seq_len * head_dim, 6 * count * seq_len * wide),
        name="attend_back",
    )(order, *kept, grads, *tables)


def after(value, *others):
    return lax.optimization_barrier((value,) + others)[0]


def whole_block(shape):
    return pl.BlockSpec(shape, lambda *_: (0,) * len(shape))


def params(limit):
    return pltpu.CompilerParams(vmem_limit_bytes=limit * 2**20)


ANYWHERE = pl.BlockSpec(memory_space=pl.ANY)
SCALARS = pl.BlockSpec(memory_space=pltpu.SMEM)
VMEM = pl.BlockSpec(memory_space=pltpu.VMEM)
ROWS = 256


def to_blocks_kernel(n_q, n_t, heads, head_dim, units, at_ref, qkv_ref, up_ref, *out_refs):
    n_z = n_t // 2
    width = heads * head_dim
    core, z = at_ref[0], at_ref[1]
    rows = qkv_ref.shape[0]
    low = lax.broadcasted_iota(jnp.int32, (rows, 128), 1) < head_dim
    per = 128 // head_dim
    for c in range(2):
        for s in range(n_z):
            out_ref = out_refs[s].at[pl.ds(c * rows, rows)]
            t = lax.rem(core + c, 2) * n_z + (z ^ s)
            odd = lax.rem(t, per)
            for which in range(3):
                for j in range(0, heads, per):
                    tiles = []
                    for i in range(per):
                        first = (which * heads + j + i) * n_t * head_dim + (t // per) * 128
                        tile = qkv_ref[:, pl.ds(pl.multiple_of(first, 128), 128)].astype(F32)
                        tiles.append(tile)
                    even = jnp.where(low, tiles[0], pltpu.roll(tiles[1], head_dim, 1))
                    uneven = jnp.where(low, pltpu.roll(tiles[0], head_dim, 1), tiles[1])
                    at = which * width + j * head_dim
                    out_ref[:, at : at + 128] = jnp.where(odd == 0, even, uneven).astype(BF)
            for q in range(n_q):
                at = 3 * width + q * units
                if units % 128 == 0:
                    first = pl.multiple_of((q * n_t + t) * units, 128)
                    out_ref[:, at : at + units] = up_ref[:, pl.ds(first, units)]
                else:
                    for k in range(n_t):

                        @pl.when(t == k)
                        def _(at=at, q=q, k=k):
                            first = (q * n_t + k) * units
                            out_ref[:, at : at + units] = up_ref[:, first : first + units]


def to_blocks(at, qkv, up, n_q, n_t, heads, head_dim, units):
    rows = qkv.shape[0]
    wide = 3 * heads * head_dim + n_q * units
    return pl.pallas_call(
        partial(to_blocks_kernel, n_q, n_t, heads, head_dim, units),
        in_specs=[SCALARS, VMEM, VMEM],
        out_specs=[VMEM] * (n_t // 2),
        out_shape=[jax.ShapeDtypeStruct((2 * rows, wide), BF)] * (n_t // 2),
        compiler_params=params(16),
        cost_estimate=cost(0, 4 * rows * wide * n_t),
        name="to_blocks",
    )(at, qkv, up)


def theirs_kernel(*refs):
    pieces, out_ref = refs[:-1], refs[-1]
    rows = pieces[0].shape[0] // 2
    for s, piece in enumerate(pieces):
        out_ref[s * rows : (s + 1) * rows, :] = piece[rows:, :]


def theirs(pieces):
    rows, columns = pieces[0].shape
    return pl.pallas_call(
        theirs_kernel,
        in_specs=[VMEM] * len(pieces),
        out_specs=VMEM,
        out_shape=jax.ShapeDtypeStruct((len(pieces) * rows // 2, columns), BF),
        compiler_params=params(16),
        cost_estimate=cost(0, 2 * len(pieces) * rows * columns),
        name="theirs",
    )(*pieces)


def piece_rows(came_refs, got_ref, at_ref):
    n_z = len(came_refs)
    rows = came_refs[0].shape[0] // 2
    core, z = at_ref[0], at_ref[1]
    for s in range(n_z):
        yield core * n_z + (z ^ s), came_refs[s][0:rows, :]
        yield (1 - core) * n_z + (z ^ s), got_ref[s * rows : (s + 1) * rows, :]


def stack_rows_kernel(at_ref, *refs):
    out_ref = refs[-1]
    for block, values in piece_rows(refs[:-2], refs[-2], at_ref):
        rows = values.shape[0]
        out_ref[pl.ds(pl.multiple_of(block * rows, 16), rows), :] = values


def stack_rows(at, came, got):
    rows, columns = came[0].shape
    return pl.pallas_call(
        stack_rows_kernel,
        in_specs=[SCALARS] + [VMEM] * (len(came) + 1),
        out_specs=VMEM,
        out_shape=jax.ShapeDtypeStruct((len(came) * rows, columns), BF),
        compiler_params=params(16),
        cost_estimate=cost(0, 4 * len(came) * rows * columns),
        name="stack_rows",
    )(at, *came, got)


def last_sum_kernel(n_z, n_parts, tail, at_ref, *refs):
    part_refs, out_refs = refs[:n_parts], refs[n_parts:]
    n_t = 2 * n_z
    below = 16 if tail else 0
    count = part_refs[0].shape[0] - tail
    rows = count // n_t
    core, z = at_ref[0], at_ref[1]
    if tail:
        total = part_refs[0][count:, :].astype(F32)
        for part_ref in part_refs[1:]:
            total = total + part_ref[count:, :].astype(F32)
        values = total[: tail // 2, :] + total[tail // 2 :, :]
        index = lax.broadcasted_iota(jnp.int32, values.shape, 0)
    for c in range(2):
        for s in range(n_z):
            block = lax.rem(core + c, 2) * n_z + (z ^ s)
            here = pl.ds(pl.multiple_of(block * rows, 16), rows)
            total = part_refs[0][here, :].astype(F32)
            for part_ref in part_refs[1:]:
                total = total + part_ref[here, :].astype(F32)
            first = c * (rows + below)
            out_refs[s][first : first + rows, :] = total.astype(BF)
            if tail:
                own = jnp.sum(jnp.where(index == block, values, 0.0), 0, keepdims=True)
                high, low = in_two(own)
                row = lax.broadcasted_iota(jnp.int32, (below, own.shape[1]), 0)
                both = jnp.where(row == 0, high.astype(F32), jnp.where(row == 1, low.astype(F32), 0.0))
                out_refs[s][first + rows : first + rows + below, :] = both.astype(BF)


def last_sum(at, parts, n_t, tail=0):
    columns = parts[0].shape[1]
    rows = 2 * ((parts[0].shape[0] - tail) // n_t + (16 if tail else 0))
    return pl.pallas_call(
        partial(last_sum_kernel, n_t // 2, len(parts), tail),
        in_specs=[SCALARS] + [VMEM] * len(parts),
        out_specs=[VMEM] * (n_t // 2),
        out_shape=[jax.ShapeDtypeStruct((rows, columns), BF)] * (n_t // 2),
        compiler_params=params(24),
        cost_estimate=cost(0, 8 * rows * n_t * columns),
        name="last_sum",
    )(at, *parts)


def from_blocks_kernel(groups, piece, below, at_ref, *refs):
    came_refs, got_ref, refs = refs[: -3 - (below > 0)], refs[-3 - (below > 0)], refs[-2 - (below > 0) :]
    out_ref, held_ref = refs[0], refs[-1]
    n_t = held_ref.shape[0]
    rows = out_ref.shape[0]
    total = 0.0
    for block, values in piece_rows(came_refs, got_ref, at_ref):
        held_ref[block] = values[0:rows, :]
        if below:
            under = values[rows:, :].astype(F32)
            total = total + under[0:1, :] + under[1:2, :]
    for t in range(n_t):
        for j in range(groups):
            first = (j * n_t + t) * piece
            out_ref[:, first : first + piece] = held_ref[t, :, j * piece : (j + 1) * piece].astype(F32)
    if below:
        refs[1][...] = jnp.broadcast_to(total, refs[1].shape)


def from_blocks(at, came, got, groups, piece, below=0):
    n_t = 2 * len(came)
    rows = came[0].shape[0] // 2 - below
    columns = groups * piece
    return pl.pallas_call(
        partial(from_blocks_kernel, groups, piece, below),
        in_specs=[SCALARS] + [VMEM] * (len(came) + 1),
        out_specs=[VMEM] * (1 + (below > 0)),
        out_shape=[jax.ShapeDtypeStruct((rows, columns * n_t), F32)]
        + [jax.ShapeDtypeStruct((8, columns), F32)] * (below > 0),
        scratch_shapes=[pltpu.VMEM((n_t, rows, columns), BF)],
        compiler_params=params(16),
        cost_estimate=cost(0, 8 * rows * columns * n_t),
        name="from_blocks",
    )(at, *came, got)


def places_kernel(n_q, n_z, q_order, at_ref, table_ref, turns_ref, order_ref):
    q, z = at_ref[2], at_ref[1]
    place = 0
    for i, index in enumerate(q_order):
        place = place + jnp.where(q == index, i, 0)
    for k, offset in enumerate(ring_offsets(n_q)):
        at = lax.rem(place + offset + n_q, n_q)
        turn_of = 0
        for i, index in enumerate(q_order):
            turn_of = turn_of + jnp.where(at == i, index, 0)
        turns_ref[k] = turn_of
    for k, offset in enumerate(ring_offsets(n_z)):
        row = lax.rem(z + offset + n_z, n_z)
        for j in range(2):
            order_ref[table_ref[row, j]] = 2 * k + j


def find_places(at, span_table, n_q, n_z, q_order):
    return pl.pallas_call(
        partial(places_kernel, n_q, n_z, q_order),
        in_specs=[SCALARS, SCALARS],
        out_specs=[SCALARS, SCALARS],
        out_shape=[jax.ShapeDtypeStruct((n_q,), jnp.int32), jax.ShapeDtypeStruct((2 * n_z,), jnp.int32)],
        cost_estimate=cost(0, 1000),
        name="places",
    )(at, span_table)


def pack_small_kernel(*refs):
    out_ref = refs[-1]
    row = 0
    for ref in refs[:-1]:
        size = ref.shape[1]
        for first in range(0, size, 128):
            count = min(128, size - first)
            out_ref[row : row + 1, 0:count] = ref[:, first : first + count].astype(F32).astype(BF)
            row += 1


def pack_small(vectors):
    return pl.pallas_call(
        pack_small_kernel,
        in_specs=[VMEM] * len(vectors),
        out_specs=VMEM,
        out_shape=jax.ShapeDtypeStruct((256, 128), BF),
        cost_estimate=cost(0, 65536),
        name="pack_small",
    )(*[v.reshape(1, -1) for v in vectors])


def pack_vectors_kernel(shape, widths, at_ref, norm_a_ref, norm_b_ref, g_ref, up_ref, out_ref):
    n_q, n_t, heads, head_dim, units = shape
    part, biases = widths
    t_here = at_ref[0] * (n_t // 2) + at_ref[1]
    gain = norm_a_ref[0:1, :] + norm_b_ref[0:1, :]
    shift = norm_a_ref[1:2, :] + norm_b_ref[1:2, :]
    qkv = norm_a_ref[2:3, :] + norm_b_ref[2:3, :]
    g = g_ref[0:1, :]
    up = up_ref[0:1, :]
    columns = out_ref.shape[2]
    for q in range(n_q):
        lines = []
        for t in range(n_t):
            owner = q * n_t + t
            here = slice(owner * part, (owner + 1) * part)
            cells = [gain[:, here], shift[:, here], g[:, here]]
            first, end = owner * biases, (owner + 1) * biases
            while first < end:
                which, head = first // (HEADS * head_dim), first // head_dim % HEADS
                stop = min(end, (first // head_dim + 1) * head_dim)
                source = (which * heads + head // n_t) * head_dim + first % head_dim
                cells.append(jnp.where(t_here == head % n_t, qkv[:, source : source + stop - first], 0.0))
                first = stop
            cells.append(jnp.where(t_here == t, up[:, q * units : (q + 1) * units], 0.0))
            used = 3 * part + biases + units
            cells.append(jnp.zeros((1, columns - used), F32))
            lines.append(jnp.concatenate(cells, 1))
        high, low = in_two(jnp.concatenate(lines, 0))
        out_ref[q, 0:n_t, :] = high
        out_ref[q, n_t:, :] = low


def pack_vectors(at, norm_a, norm_b, g, up, shape, widths, columns):
    n_q, n_t = shape[:2]
    return pl.pallas_call(
        partial(pack_vectors_kernel, shape, widths),
        in_specs=[SCALARS] + [VMEM] * 4,
        out_specs=VMEM,
        out_shape=jax.ShapeDtypeStruct((n_q, 2 * n_t, columns), BF),
        cost_estimate=cost(0, 4 * n_q * n_t * columns),
        name="pack_vectors",
    )(at, norm_a, norm_b, g, up)


def load_pieces(plan, turns_ref, piece_refs, target, sem):
    copies = []
    for i, (piece, first, rows, slot, scale, base) in enumerate(plan):
        start = pl.multiple_of(turns_ref[slot] * scale + base, 16)
        copies.append(pltpu.make_async_copy(piece_refs[piece].at[pl.ds(first, rows)], target.at[pl.ds(start, rows)], sem.at[i]))
    return copies


def fetch_slots(plan, slot_refs, buffers, sems):
    i = pl.program_id(0)

    def copies(k):
        return [
            pltpu.make_async_copy(slot_refs[which], buffers.at[k % 2, pl.ds(first, rows)], sems.at[k % 2, part])
            for part, (which, first, rows) in enumerate(plan[k])
        ]

    for k in range(len(plan)):

        @pl.when(i == k)
        def _(k=k):
            for copy in (copies(0) if k == 0 else []) + (copies(k + 1) if k + 1 < len(plan) else []):
                copy.start()
            for copy in copies(k):
                copy.wait()


class Gathered:
    def __init__(self, arrays, plan, turns):
        self.arrays = arrays
        self.plan = tuple(plan)
        self.starts = turns
        self.rows = sum(piece[2] for piece in plan)
        self.columns = arrays[0].shape[1]

    def scratch(self):
        return [pltpu.VMEM((self.rows, self.columns), BF), pltpu.SemaphoreType.DMA((len(self.plan),))]

    def specs(self):
        return [ANYWHERE] * len(self.arrays)


def put_block(plan, block, held_ref, out_refs, sem):
    i = pl.program_id(0)
    held_ref[i] = block

    def copies(k):
        return [
            pltpu.make_async_copy(held_ref.at[k, pl.ds(first, rows)], out_refs[which], sem.at[which])
            for which, first, rows in plan[k]
        ]

    for k in range(len(plan)):

        @pl.when(i == k)
        def _(k=k):
            for copy in copies(k):
                copy.start()

    @pl.when(i == len(plan) - 1)
    def _():
        for k in range(len(plan)):
            for copy in copies(k):
                copy.wait()


def normed(rows):
    mean = jnp.mean(rows, -1, keepdims=True)
    centred = rows - mean
    scale = lax.rsqrt(jnp.mean(centred * centred, -1, keepdims=True) + EPS)
    return centred * scale, scale


def project_kernel(split, x_plan, n_x, w_plan, n_w, starts_ref, *refs):
    x_refs, refs = refs[:n_x], refs[n_x:]
    w_refs, refs = refs[:n_w], refs[n_w:]
    gain_ref, shift_ref, b_ref, x_out_ref, hidden_ref, qkv_ref, act_ref, slope_ref, w_ref, w_sem, x_buf, x_sem = refs

    @pl.when(pl.program_id(0) == 0)
    def _():
        for copy in load_pieces(w_plan, starts_ref, w_refs, w_ref, w_sem):
            copy.start()

    fetch_slots(x_plan, x_refs, x_buf, x_sem)
    x = x_buf[lax.rem(pl.program_id(0), 2)]
    x_out_ref[...] = x
    xhat, _ = normed(x.astype(F32))
    hidden = (xhat * gain_ref[...] + shift_ref[...]).astype(BF)
    hidden_ref[...] = hidden

    @pl.when(pl.program_id(0) == 0)
    def _():
        for copy in load_pieces(w_plan, starts_ref, w_refs, w_ref, w_sem):
            copy.wait()

    pre = dot(hidden, w_ref[:, split:]) + b_ref[:, split:]
    root = math.sqrt(2.0 / math.pi)
    square = pre * pre
    turned = jnp.tanh(root * pre * (1.0 + 0.044715 * square))
    act_ref[...] = (0.5 * pre * (1.0 + turned)).astype(BF)
    slope = 0.5 * (1.0 + turned) + 0.5 * pre * (1.0 - turned * turned) * (root * (1.0 + 3 * 0.044715 * square))
    slope_ref[...] = slope.astype(BF)
    qkv_ref[...] = dot(hidden, w_ref[:, :split]) + b_ref[:, :split]


def project(x_arrays, x_plan, gain, shift, w, b, split):
    rows, width = x_arrays[0].shape
    count = rows * len(x_plan)
    wide = w.columns

    def block(columns):
        return pl.BlockSpec((rows, columns), lambda i, s: (i, 0))

    return pl.pallas_call(
        partial(project_kernel, split, x_plan, len(x_arrays), w.plan, len(w.arrays)),
        grid_spec=pltpu.PrefetchScalarGridSpec(
            num_scalar_prefetch=1,
            grid=(len(x_plan),),
            in_specs=[ANYWHERE] * len(x_arrays) + w.specs() + [whole_block((1, width))] * 2 + [whole_block(b.shape)],
            out_specs=[block(width), block(width), block(split), block(wide - split), block(wide - split)],
            scratch_shapes=w.scratch() + [pltpu.VMEM((2, rows, width), BF), pltpu.SemaphoreType.DMA((2, 2))],
        ),
        out_shape=[
            jax.ShapeDtypeStruct((count, width), BF),
            jax.ShapeDtypeStruct((count, width), BF),
            jax.ShapeDtypeStruct((count, split), F32),
            jax.ShapeDtypeStruct((count, wide - split), BF),
            jax.ShapeDtypeStruct((count, wide - split), BF),
        ],
        compiler_params=params(58),
        cost_estimate=cost(2 * count * width * wide, 8 * count * width + 2 * width * wide),
        name="project",
    )(w.starts, *x_arrays, *w.arrays, gain, shift, b)


def combine_kernel(split, w_plan, n_w, plan, n_arrived, starts_ref, act_ref, att_ref, *refs):
    w_refs, refs = refs[:n_w], refs[n_w:]
    arrived_refs, refs = refs[:n_arrived], refs[n_arrived:]
    out_refs, (w_ref, w_sem, held, held_sem, buf, buf_sem) = refs[:-6], refs[-6:]

    @pl.when(pl.program_id(0) == 0)
    def _():
        copies = load_pieces(w_plan, starts_ref, w_refs, w_ref, w_sem)
        for copy in copies:
            copy.start()
        for copy in copies:
            copy.wait()

    total = dot(act_ref[...], w_ref[:split, :]) + dot(att_ref[...], w_ref[split:, :])
    if n_arrived:
        fetch_slots([((k, 0, total.shape[0]),) for k in range(n_arrived)], arrived_refs, buf, buf_sem)
        total = total + buf[lax.rem(pl.program_id(0), 2)].astype(F32)
    put_block(plan, total.astype(BF), held, out_refs, held_sem)


def held_blocks(steps, rows, width):
    return [pltpu.VMEM((steps, rows, width), BF), pltpu.SemaphoreType.DMA((steps + 1,))]


def combine(act, att, w, part, rows, arrived=()):
    count, split = act.shape[0] // 2, act.shape[1]
    own_width = att.shape[-1]
    att = att.reshape(count, own_width)
    width = w.columns
    steps = count // rows
    base = part * steps
    plan = slot_plan(steps, rows) if arrived else [((k, 0, rows),) for k in range(steps)]
    shapes = [jax.ShapeDtypeStruct((r, width), BF) for slot in plan for _, _, r in slot]
    return pl.pallas_call(
        partial(combine_kernel, split, w.plan, len(w.arrays), plan, len(arrived)),
        grid_spec=pltpu.PrefetchScalarGridSpec(
            num_scalar_prefetch=1,
            grid=(steps,),
            in_specs=[
                pl.BlockSpec((rows, split), lambda i, s: (i + base, 0)),
                pl.BlockSpec((rows, own_width), lambda i, s: (i, 0)),
            ]
            + w.specs()
            + [ANYWHERE] * len(arrived),
            out_specs=[ANYWHERE] * len(shapes),
            scratch_shapes=w.scratch()
            + held_blocks(steps, rows, width)
            + [pltpu.VMEM((2, rows, width), BF), pltpu.SemaphoreType.DMA((2, 2))],
        ),
        out_shape=shapes,
        compiler_params=params(32),
        cost_estimate=cost(2 * count * width * w.rows, 4 * count * width + 2 * width * w.rows),
        name="combine",
    )(w.starts, act, att, *w.arrays, *arrived)


def combine_back_kernel(split, g_plan, n_g, w_plan, n_w, starts_ref, *refs):
    g_refs, refs = refs[:n_g], refs[n_g:]
    w_refs, refs = refs[:n_w], refs[n_w:]
    slope_ref, g_out_ref, pre_grad_ref, att_grad_ref, sums_ref, w_ref, w_sem, g_buf, g_sem = refs

    @pl.when(pl.program_id(0) == 0)
    def _():
        for copy in load_pieces(w_plan, starts_ref, w_refs, w_ref, w_sem):
            copy.start()

    fetch_slots(g_plan, g_refs, g_buf, g_sem)

    @pl.when(pl.program_id(0) == 0)
    def _():
        for copy in load_pieces(w_plan, starts_ref, w_refs, w_ref, w_sem):
            copy.wait()

    grad = g_buf[lax.rem(pl.program_id(0), 2)]
    g_out_ref[...] = grad

    @pl.when(pl.program_id(0) == 0)
    def _():
        sums_ref[...] = jnp.zeros_like(sums_ref)
        sums_ref[0:1, :] = jnp.sum(grad.astype(F32), 0, keepdims=True)

    pre_grad_ref[...] = (dot_t(grad, w_ref[:split, :]) * slope_ref[...].astype(F32)).astype(BF)
    att_grad_ref[...] = dot_t(grad, w_ref[split:, :]).astype(BF)


def combine_back(g_arrays, g_plan, w, slope):
    rows, width = g_arrays[0].shape
    count = rows * len(g_plan)
    split = slope.shape[1]
    rest = w.rows - split

    def block(columns):
        return pl.BlockSpec((rows, columns), lambda i, s: (i, 0))

    return pl.pallas_call(
        partial(combine_back_kernel, split, g_plan, len(g_arrays), w.plan, len(w.arrays)),
        grid_spec=pltpu.PrefetchScalarGridSpec(
            num_scalar_prefetch=1,
            grid=(len(g_plan),),
            in_specs=[ANYWHERE] * len(g_arrays) + w.specs() + [block(split)],
            out_specs=[block(width), block(split), block(rest), whole_block((8, width))],
            scratch_shapes=w.scratch() + [pltpu.VMEM((2, rows, width), BF), pltpu.SemaphoreType.DMA((2, 2))],
        ),
        out_shape=[
            jax.ShapeDtypeStruct((count, width), BF),
            jax.ShapeDtypeStruct((count, split), BF),
            jax.ShapeDtypeStruct((count, rest), BF),
            jax.ShapeDtypeStruct((8, width), F32),
        ],
        compiler_params=params(58),
        cost_estimate=cost(2 * count * width * w.rows, 6 * count * width + 2 * width * w.rows),
        name="combine_back",
    )(w.starts, *g_arrays, *w.arrays, slope)


def project_back_kernel(split, w_plan, n_w, plan, n_arrived, starts_ref, qkv_grad_ref, pre_grad_ref, x_ref, *refs):
    w_refs, refs = refs[:n_w], refs[n_w:]
    arrived_refs, refs = refs[:n_arrived], refs[n_arrived:]
    out_refs, (sums_ref, w_ref, w_sem, held, held_sem, buf, buf_sem) = refs[:-7], refs[-7:]

    @pl.when(pl.program_id(0) == 0)
    def _():
        copies = load_pieces(w_plan, starts_ref, w_refs, w_ref, w_sem)
        for copy in copies:
            copy.start()
        sums_ref[...] = jnp.zeros_like(sums_ref)
        for copy in copies:
            copy.wait()

    grad = dot_t(qkv_grad_ref[...], w_ref[:, :split]) + dot_t(pre_grad_ref[...], w_ref[:, split:])
    xhat, _ = normed(x_ref[...].astype(F32))
    sums_ref[0:1, :] += jnp.sum(grad * xhat, 0, keepdims=True)
    sums_ref[1:2, :] += jnp.sum(grad, 0, keepdims=True)
    sums_ref[2:3, 0:split] += jnp.sum(qkv_grad_ref[...].astype(F32), 0, keepdims=True)
    if n_arrived:
        fetch_slots([((k, 0, grad.shape[0]),) for k in range(n_arrived)], arrived_refs, buf, buf_sem)
        grad = grad + buf[lax.rem(pl.program_id(0), 2)].astype(F32)
    put_block(plan, grad.astype(BF), held, out_refs, held_sem)


def project_back(qkv_grad, pre_grad, w, x, part, rows, arrived=()):
    count, width = x.shape[0] // 2, x.shape[1]
    split = qkv_grad.shape[1]
    steps = count // rows
    base = part * steps
    plan = slot_plan(steps, rows) if arrived else [((k, 0, rows),) for k in range(steps)]
    shapes = [jax.ShapeDtypeStruct((r, width), BF) for slot in plan for _, _, r in slot]

    def block(columns):
        return pl.BlockSpec((rows, columns), lambda i, s: (i + base, 0))

    *out, sums = pl.pallas_call(
        partial(project_back_kernel, split, w.plan, len(w.arrays), plan, len(arrived)),
        grid_spec=pltpu.PrefetchScalarGridSpec(
            num_scalar_prefetch=1,
            grid=(steps,),
            in_specs=[block(split), block(pre_grad.shape[1]), block(width)] + w.specs() + [ANYWHERE] * len(arrived),
            out_specs=[ANYWHERE] * len(shapes) + [whole_block((8, width))],
            scratch_shapes=w.scratch()
            + held_blocks(steps, rows, width)
            + [pltpu.VMEM((2, rows, width), BF), pltpu.SemaphoreType.DMA((2, 2))],
        ),
        out_shape=shapes + [jax.ShapeDtypeStruct((8, width), F32)],
        compiler_params=params(58),
        cost_estimate=cost(2 * count * width * w.columns, 6 * count * width + 2 * width * w.columns),
        name="project_back",
    )(w.starts, qkv_grad, pre_grad, x, *w.arrays, *arrived)
    return out, sums


def weight_grad_kernel(with_tail, turns_ref, left_ref, right_ref, *refs):
    tail_refs, refs = refs[:with_tail], refs[with_tail:]
    out_refs, (sums_ref, held, sem) = refs[:-3], refs[-3:]

    @pl.when(pl.program_id(0) == 0)
    def _():
        sums_ref[...] = jnp.zeros_like(sums_ref)
        sums_ref[0:1, :] = jnp.sum(right_ref[...].astype(F32), 0, keepdims=True)

    block = t_dot(left_ref[...], right_ref[...]).astype(BF)
    if with_tail:
        block = jnp.concatenate([block, tail_refs[0][0]], 0)
    put_block(slot_plan(held.shape[0], held.shape[1]), block, held, out_refs, sem)


def slot_shapes(n, rows, columns):
    return [jax.ShapeDtypeStruct((r, columns), BF) for slot in slot_plan(n, rows) for _, _, r in slot]


def weight_grad(turns, left, right, tail=None):
    n_q = turns.shape[0]
    count, wide = left.shape
    columns = right.shape[1]
    part = wide // n_q
    rows = part + (0 if tail is None else tail.shape[1])
    extra = [] if tail is None else [tail]
    shapes = slot_shapes(n_q, rows, columns)
    *out, sums = pl.pallas_call(
        partial(weight_grad_kernel, len(extra)),
        grid_spec=pltpu.PrefetchScalarGridSpec(
            num_scalar_prefetch=1,
            grid=(n_q,),
            in_specs=[pl.BlockSpec((count, part), lambda k, s: (0, s[k])), whole_block(right.shape)]
            + [pl.BlockSpec((1,) + v.shape[1:], lambda k, s: (s[k], 0, 0)) for v in extra],
            out_specs=[ANYWHERE] * len(shapes) + [whole_block((8, columns))],
            scratch_shapes=held_blocks(n_q, rows, columns),
        ),
        out_shape=shapes + [jax.ShapeDtypeStruct((8, columns), F32)],
        compiler_params=params(58),
        cost_estimate=cost(2 * count * wide * columns, 2 * count * (wide + columns) + 2 * wide * columns),
        name="weight_grad",
    )(turns, left, right, *extra)
    return out, sums


def down_grad_kernel(head_rows, turns_ref, act_ref, att_a_ref, att_b_ref, g_ref, *refs):
    out_refs, (heads_ref, held, sem) = refs[:-3], refs[-3:]
    units = act_ref.shape[1]
    k = pl.program_id(0)

    @pl.when(k == 0)
    def _():
        half = att_a_ref.shape[0]
        heads_ref[...] = (t_dot(att_a_ref[...], g_ref[0:half, :]) + t_dot(att_b_ref[...], g_ref[half:, :])).astype(BF)

    rows = pl.ds(pl.multiple_of(turns_ref[k] * head_rows, head_rows), head_rows)
    block = jnp.concatenate([t_dot(act_ref[...], g_ref[...]).astype(BF), heads_ref[rows, :]], 0)
    put_block(slot_plan(held.shape[0], held.shape[1]), block, held, out_refs, sem)


def down_grad(turns, act, att, g, head_rows):
    n_q = turns.shape[0]
    count, wide = act.shape
    own_width = att[0].shape[-1]
    att = [a.reshape(count // 2, own_width) for a in att]
    width = g.shape[1]
    units = wide // n_q
    if not head_rows:
        whole = t_dot(act, g).astype(BF).reshape(n_q, units, width)[turns]
        blocks = [whole[k][first : first + r] for k, slot in enumerate(slot_plan(n_q, units)) for _, first, r in slot]
        return blocks, t_dot(jnp.concatenate(att, 0), g)
    out = pl.pallas_call(
        partial(down_grad_kernel, head_rows),
        grid_spec=pltpu.PrefetchScalarGridSpec(
            num_scalar_prefetch=1,
            grid=(n_q,),
            in_specs=[pl.BlockSpec((count, units), lambda k, s: (0, s[k]))] + [whole_block(v.shape) for v in (*att, g)],
            out_specs=[ANYWHERE] * (n_q + 1),
            scratch_shapes=[pltpu.VMEM((own_width, width), BF)] + held_blocks(n_q, units + head_rows, width),
        ),
        out_shape=slot_shapes(n_q, units + head_rows, width),
        compiler_params=params(58),
        cost_estimate=cost(2 * count * (wide + own_width) * width, 2 * count * (wide + width) + 2 * wide * width),
        name="down_grad",
    )(turns, act, *att, g)
    return list(out), None


def finish_kernel(x_ref, g_ref, gain_ref, *refs):
    part_refs, out_ref = refs[:-1], refs[-1]
    grad = part_refs[0][...].astype(F32)
    for part_ref in part_refs[1:]:
        grad = grad + part_ref[...].astype(F32)
    xhat, scale = normed(x_ref[...].astype(F32))
    m = grad * gain_ref[...]
    x_grad = (m - jnp.mean(m, -1, keepdims=True) - xhat * jnp.mean(m * xhat, -1, keepdims=True)) * scale
    out_ref[...] = (g_ref[...].astype(F32) + x_grad).astype(BF)


def finish(parts, x, g, gain):
    count, width = x.shape
    rows = math.gcd(count, 128)
    block = pl.BlockSpec((rows, width), lambda i: (i, 0))
    return pl.pallas_call(
        finish_kernel,
        grid=(count // rows,),
        in_specs=[block] * 2 + [whole_block((1, width))] + [block] * len(parts),
        out_specs=block,
        out_shape=jax.ShapeDtypeStruct((count, width), BF),
        cost_estimate=cost(20 * count * width, 12 * count * width),
        name="finish",
    )(x, g, gain, *parts)


def output_kernel(x_ref, bias_ref, *refs):
    part_refs, out_ref = refs[:-1], refs[-1]
    total = x_ref[...].astype(F32) + bias_ref[...]
    for part_ref in part_refs:
        total = total + part_ref[...].astype(F32)
    out_ref[...] = total.astype(BF)


def output_sum(x, bias, parts):
    count, width = x.shape
    rows = math.gcd(count, 128)
    block = pl.BlockSpec((rows, width), lambda i: (i, 0))
    return pl.pallas_call(
        output_kernel,
        grid=(count // rows,),
        in_specs=[block, whole_block((1, width))] + [block] * len(parts),
        out_specs=block,
        out_shape=jax.ShapeDtypeStruct((count, width), BF),
        cost_estimate=cost(4 * count * width, 10 * count * width),
        name="output_sum",
    )(x, bias, *parts)


def split_sum(parts, cuts):
    count, width = parts[0].shape
    wide = math.gcd(width, 1024)
    ends = [sum(cuts[: i + 1]) for i in range(len(cuts))]

    def kernel(*refs):
        part_refs, out_refs = refs[: len(parts)], refs[len(parts) :]
        total = part_refs[0][...].astype(F32)
        for part_ref in part_refs[1:]:
            total = total + part_ref[...].astype(F32)
        for end, rows, out_ref in zip(ends, cuts, out_refs):
            out_ref[...] = total[end - rows : end, :]

    return pl.pallas_call(
        kernel,
        grid=(width // wide,),
        in_specs=[pl.BlockSpec((count, wide), lambda i: (0, i))] * len(parts),
        out_specs=[pl.BlockSpec((rows, wide), lambda i: (0, i)) for rows in cuts],
        out_shape=[jax.ShapeDtypeStruct((rows, width), F32) for rows in cuts],
        cost_estimate=cost(4 * count * width, 12 * count * width),
        name="split_sum",
    )(*parts)


def tables_kernel(head_dim, cos_ref, sin_a_ref, sin_b_ref):
    rows = cos_ref.shape[0]
    half = ROT // 2
    lane = lax.broadcasted_iota(jnp.int32, (1, 128), 1) % head_dim
    step = (lane % half).astype(F32) * (-2.0 * math.log(10000.0) / ROT)
    freqs = jnp.where(lane < ROT, jnp.exp(step), 0.0)
    position = lax.broadcasted_iota(jnp.int32, (rows, 128), 0) + pl.program_id(0) * rows
    angles = position.astype(F32) * freqs
    cosine, sine = jnp.cos(angles), jnp.sin(angles)
    cos_ref[...] = cosine
    sin_a_ref[...] = jnp.where(lane < half, -sine, 0.0)
    sin_b_ref[...] = jnp.where((lane >= half) & (lane < ROT), sine, 0.0)


def rotary_tables(seq_len, head_dim):
    width = 128
    block = pl.BlockSpec((128, width), lambda i: (i, 0))
    return pl.pallas_call(
        partial(tables_kernel, head_dim),
        grid=(seq_len // 128,),
        out_specs=[block] * 3,
        out_shape=[jax.ShapeDtypeStruct((seq_len, width), F32)] * 3,
        cost_estimate=cost(100 * seq_len * width, 12 * seq_len * width),
        name="rotary_tables",
    )()


def per_device(
    inputs,
    span_table,
    ln_gain,
    ln_bias,
    qkv_weight,
    qkv_bias,
    out_weight,
    out_bias,
    fc1_weight,
    fc1_bias,
    fc2_weight,
    fc2_bias,
    cotangent,
):
    rows, width = inputs.shape
    head_dim = width // HEADS
    n_q, n_z = lax.axis_size("q"), lax.axis_size("ctx")
    n_t = 2 * n_z
    n_all = n_q * n_t
    q, core, z = lax.axis_index("q"), lax.axis_index("core"), lax.axis_index("ctx")
    t = core * n_z + z
    at = jnp.stack([core, z, q]).astype(jnp.int32)
    span = rows // 2
    seq_len = rows * n_z
    heads = HEADS // n_t
    own_width = heads * head_dim
    split = 3 * own_width
    units = fc2_weight.shape[0]
    own_units = units * n_q
    d_rows = qkv_weight.shape[0]
    every = ("q", "core", "ctx")
    z_order = list(range(n_z))
    q_order = [0, 1, 3, 2] if n_q == 4 else list(range(n_q))
    turns, order = find_places(at, span_table, n_q, n_z, q_order)
    whole_heads = out_weight.shape[0] == head_dim

    tables = rotary_tables(seq_len, head_dim)

    owned = [ln_gain, ln_bias, out_bias, fc2_bias, qkv_bias, fc1_bias]
    small = lax.all_gather(pack_small(owned), every, axis=0, tiled=True)

    came = scattered(to_blocks(at, qkv_weight, fc1_weight, n_q, n_t, heads, head_dim, units), "ctx")
    w2_block = jnp.concatenate([fc2_weight, out_weight], 0) if whole_heads else fc2_weight
    w2_arrays, w2_halves = ring_halves(w2_block, "q", q_order)
    w2_halves = lax.optimization_barrier(w2_halves)
    w2_arrays = w2_arrays + [
        lax.ppermute(half, "q", ring_pairs(q_order, step)) for half, step in zip(w2_halves, (1, -1))
    ]
    plan = []
    for slot, pieces in enumerate(slot_plan(n_q, w2_block.shape[0])):
        for which, first, count in pieces:
            if first < units:
                plan.append((which, 0, min(first + count, units) - first, slot, units, first))
            if first + count > units:
                begin = max(first, units)
                plan.append((which, begin - first, first + count - begin, slot, head_dim, own_units + begin - units))
    w2_sent = w2_arrays[1:]
    if not whole_heads:
        w_out = lax.all_gather(out_weight, every, axis=0, tiled=True).reshape(heads, n_t, head_dim, width)
        w2_arrays = w2_arrays + [lax.dynamic_index_in_dim(w_out, t, 1, False).reshape(own_width, width)]
        plan.append((len(w2_arrays) - 1, 0, own_width, 0, 0, own_units))
    w2 = Gathered(w2_arrays, plan, turns)

    got = swap(theirs([after(came[0], *w2_sent[:-2], turns, order)] + came[1:]))
    w1_block = stack_rows(at, came, got)
    w1_arrays = ring_gathered(w1_block, "q", q_order)
    block_rows = n_t * d_rows
    w1_plan = [
        (which, 0, count, slot, block_rows, first)
        for slot, pieces in enumerate(slot_plan(n_q, block_rows))
        for which, first, count in pieces
    ]
    w1 = Gathered(w1_arrays, w1_plan, turns)

    token_plan = slot_plan(n_z, rows) + slot_plan(n_z, rows, n_z + 1)
    x_line = ring_gathered(after(inputs, *w2_halves), "ctx", z_order)
    x_arrays = x_line + [swap(x_line[0])] + [swap(after(p, *w1_arrays[-2:])) for p in x_line[1:]]

    small = after(small, *x_line[-2:])
    small = small.reshape(n_all, 256, 128)[:, :16]
    lists, row = [], 0
    for vector in owned:
        used = -(-vector.shape[0] // 128)
        lists.append(small[:, row : row + used].reshape(n_all, used * 128)[:, : vector.shape[0]].astype(F32))
        row += used
    gain, shift, b_out, b_down = (v.reshape(1, width) for v in lists[:4])
    b_qkv = lax.dynamic_index_in_dim(lists[4].reshape(3, heads, n_t, head_dim), t, 2, False).reshape(1, split)
    b_up = lax.dynamic_index_in_dim(lists[5].reshape(n_q, n_t, units), t, 1, False).reshape(1, own_units)
    b_project = jnp.concatenate([b_qkv, b_up], 1)

    x_all, hidden, qkv, act, slope = project(x_arrays, token_plan, gain, shift, w1, b_project, split)
    att_other, kept_other = attend(order, qkv, tables, heads, head_dim, span, 1)
    out_other = combine(act, att_other, w2, 1, rows)
    g_line = ring_gathered(after(cotangent, *x_line[-2:]), "ctx", z_order, out_other)
    att_own, kept_own = attend(order, after(qkv, *out_other, *g_line[1:-2]), tables, heads, head_dim, span, 0)
    out_own = combine(act, att_own, w2, 0, rows, [swap(p) for p in out_other])
    g_arrays = g_line + [swap(p) for p in g_line[:-2]] + [swap(after(p, *out_own)) for p in g_line[-2:]]

    g_all, pre_grad, att_grad, g_sums = combine_back(g_arrays, token_plan, w2, after(slope, *out_own))
    up_own, up_sums = weight_grad(turns, hidden, pre_grad)
    out_parts, out_sent = ring_sum(out_own, "ctx", z_order, up_own)
    att_grad = after(att_grad, *up_own, *out_sent).reshape(2, seq_len, own_width)
    qkv_grad = attend_back(order, (kept_own, kept_other), att_grad, tables, heads, head_dim, span).reshape(2 * seq_len, split)
    up_parts, up_sent = ring_sum(up_own, "q", q_order, [qkv_grad])
    normed_other, sums_other = project_back(after(qkv_grad, *up_sent), pre_grad, w1, x_all, 1, rows)
    down, out_apart = down_grad(turns, after(act, *normed_other, *out_parts[1:]), (att_own, att_other), g_all, head_dim if whole_heads else 0)
    up_rows = last_sum(at, [after(up_parts[0], *down)] + up_parts[1:], n_t)
    up_came = scattered(up_rows, "ctx")
    normed_own, sums_own = project_back(
        after(qkv_grad, *down), pre_grad, w1, x_all, 0, rows, [swap(p) for p in normed_other]
    )
    down_parts, down_sent = ring_sum(down, "q", q_order, normed_own)
    vectors = pack_vectors(
        at, sums_own, sums_other, g_sums, up_sums, (n_q, n_t, heads, head_dim, units), (d_rows, qkv_bias.shape[0]), split
    )
    qkv_own, _ = weight_grad(turns, after(hidden, *normed_own, *down_sent), qkv_grad, vectors)
    qkv_first = ring_first(qkv_own, "q", q_order)
    normed_own = [after(p, *up_came[1:]) for p in normed_own]
    normed_first = ring_first(normed_own, "ctx", z_order)
    normed_parts, normed_sent = ring_rest(normed_own, normed_first, "ctx", z_order, qkv_own)
    qkv_parts, qkv_sent = ring_rest(qkv_own, qkv_first, "q", q_order, normed_sent, 2 * n_t)
    output = output_sum(inputs, b_out + b_down, [after(out_parts[0], *normed_sent)] + out_parts[1:])

    qkv_came = scattered(last_sum(at, qkv_parts, n_t, 2 * n_t), "ctx")
    if whole_heads:
        fc2_weight_grad, out_weight_grad = split_sum(down_parts, [units, head_dim])
    else:
        (fc2_weight_grad,) = split_sum(down_parts, [units])
        spread = jnp.zeros((heads, n_t, head_dim, width), F32)
        spread = lax.dynamic_update_slice(spread, out_apart.reshape(heads, 1, head_dim, width), (0, t, 0, 0))
        out_weight_grad = lax.psum_scatter(spread.reshape(width, width), every, scatter_dimension=0, tiled=True)
    input_grad = finish(normed_parts, inputs, cotangent, gain)
    up_got = swap(theirs([after(up_came[0], *normed_parts[1:], output)] + up_came[1:]))
    (fc1_weight_grad,) = from_blocks(at, up_came, up_got, n_q, units)
    qkv_got = swap(theirs([after(qkv_came[0], up_got, fc1_weight_grad, input_grad, fc2_weight_grad)] + qkv_came[1:]))
    qkv_weight_grad, total = from_blocks(at, qkv_came, qkv_got, 3 * heads, head_dim, 16)
    total = total[0]

    cuts = [ln_gain.shape[0], ln_bias.shape[0], out_bias.shape[0], qkv_bias.shape[0], fc1_bias.shape[0]]
    starts = [sum(cuts[:i]) for i in range(len(cuts))]
    gain_grad, shift_grad, bias_grad, qkv_bias_grad, fc1_bias_grad = (total[s : s + c] for s, c in zip(starts, cuts))
    return (
        output,
        input_grad,
        gain_grad,
        shift_grad,
        qkv_weight_grad,
        qkv_bias_grad,
        out_weight_grad,
        bias_grad,
        fc1_weight_grad,
        fc1_bias_grad,
        fc2_weight_grad,
        bias_grad,
    )


def solution(mesh):
    n_dp, n_ctx = mesh.devices.shape
    inner = Mesh(mesh.devices.reshape(n_dp // 2, 2, n_ctx), ("q", "core", "ctx"))
    every = ("q", "core", "ctx")
    matrix, vector = P(every, None), P(every)
    return jax.shard_map(
        per_device,
        mesh=inner,
        in_specs=(
            matrix,
            P(),
            vector,
            vector,
            matrix,
            vector,
            matrix,
            vector,
            matrix,
            vector,
            matrix,
            vector,
            matrix,
        ),
        out_specs=(matrix, matrix, vector, vector, matrix, vector, matrix, vector, matrix, vector, matrix, vector),
        check_vma=False,
    )
```

```python
from functools import partial
import math

import jax
import jax.numpy as jnp
from jax import lax
from jax.experimental import pallas as pl
from jax.experimental.pallas import tpu as pltpu
from jax.sharding import Mesh, PartitionSpec as P

HEADS = 32
ROT = 32
EPS = 1e-05
NEG = -1e30
BLOCK_Q = 256

BF = jnp.bfloat16
F32 = jnp.float32


def dot(a, b):
    return jnp.dot(a, b, preferred_element_type=F32)


def dot_t(a, b):
    return lax.dot_general(a, b, (((1,), (1,)), ((), ())), preferred_element_type=F32)


def t_dot(a, b):
    return lax.dot_general(a, b, (((0,), (0,)), ((), ())), preferred_element_type=F32)


def cost(flops, nbytes):
    return pl.CostEstimate(flops=flops // 1000, bytes_accessed=nbytes // 1000, transcendentals=0)


def across(value, axis, e):
    n = math.prod(lax.axis_size(a) for a in axis) if isinstance(axis, tuple) else lax.axis_size(axis)
    return lax.ppermute(value, axis, [(i, i ^ e) for i in range(n)])


def scattered(parts, axis):
    return [parts[0]] + [across(part, axis, e) for e, part in enumerate(parts) if e]


def ring_pairs(order, step):
    n = len(order)
    return [(order[i], order[(i + step) % n]) for i in range(n)]


def ring_offsets(n):
    return [0] + [o for s in range(1, n // 2) for o in (-s, s)] + [n // 2]


def half_of(rows):
    return rows // 32 * 16


def slot_plan(n, rows, first=0):
    plan = [((first + k, 0, rows),) for k in range(n - 1)]
    return plan + [((first + n - 1, 0, half_of(rows)), (first + n, half_of(rows), rows - half_of(rows)))]


def ring_halves(own, axis, order):
    n = len(order)
    up_pairs, down_pairs = ring_pairs(order, 1), ring_pairs(order, -1)
    out = [own]
    up = down = own
    half = half_of(own.shape[0])
    for _ in range(1, n // 2):
        up, down = lax.ppermute(up, axis, up_pairs), lax.ppermute(down, axis, down_pairs)
        out += [up, down]
    return out, (up[:half], down[half:])


def ring_gathered(own, axis, order, hold=()):
    out, (up, down) = ring_halves(own, axis, order)
    up, down = after(up, *hold), after(down, *hold)
    return out + [lax.ppermute(up, axis, ring_pairs(order, 1)), lax.ppermute(down, axis, ring_pairs(order, -1))]


def ring_first(parts, axis, order):
    n = len(order)
    return [
        lax.ppermute(parts[n - 1], axis, ring_pairs(order, -1)),
        lax.ppermute(parts[n], axis, ring_pairs(order, 1)),
    ]


def ring_rest(parts, arrived, axis, order, hold=(), tail=0):
    n = len(order)
    low, high = arrived
    sent = ()
    for step in range(n // 2 - 1, 0, -1):
        sent = pass_on(parts[2 * step - 1], parts[2 * step], after(low, *hold), high, tail)
        low = lax.ppermute(sent[0], axis, ring_pairs(order, -1))
        high = lax.ppermute(sent[1], axis, ring_pairs(order, 1))
    return [parts[0], low, high], sent


def ring_sum(parts, axis, order, hold=()):
    return ring_rest(parts, ring_first(parts, axis, order), axis, order, hold)


def in_two(values):
    first = values.astype(BF)
    return first, (values - first.astype(F32)).astype(BF)


def add_rows(part, arrived, tail):
    total = part.astype(F32) + arrived.astype(F32)
    if not tail:
        return total.astype(BF)
    cut, half = total.shape[0] - tail, tail // 2
    values = total[cut : cut + half, :] + total[cut + half :, :]
    return jnp.concatenate([total[:cut, :].astype(BF), *in_two(values)], 0)


def pass_on_kernel(tail, low_part_ref, high_part_ref, low_ref, high_ref, to_low_ref, to_high_ref):
    rows = low_part_ref.shape[0]
    cut = low_ref.shape[0]
    if cut < rows:
        to_low_ref[0:cut, :] = add_rows(low_part_ref[0:cut, :], low_ref[...], 0)
        to_low_ref[cut:, :] = low_part_ref[cut:, :]
        to_high_ref[0:cut, :] = high_part_ref[0:cut, :]
        to_high_ref[cut:, :] = add_rows(high_part_ref[cut:, :], high_ref[...], tail)
    else:
        to_low_ref[...] = add_rows(low_part_ref[...], low_ref[...], tail)
        to_high_ref[...] = add_rows(high_part_ref[...], high_ref[...], tail)


def pass_on(low_part, high_part, low, high, tail):
    rows, columns = low_part.shape
    wide = math.gcd(columns, 1024)

    def block(array):
        return pl.BlockSpec((array.shape[0], wide), lambda i: (0, i))

    arrays = [low_part, high_part, low, high]
    return pl.pallas_call(
        partial(pass_on_kernel, tail),
        grid=(columns // wide,),
        in_specs=[block(array) for array in arrays],
        out_specs=[block(low_part)] * 2,
        out_shape=[jax.ShapeDtypeStruct((rows, columns), BF)] * 2,
        cost_estimate=cost(2 * rows * columns, 12 * rows * columns),
        name="pass_on",
    )(*arrays)


def swap(value):
    return lax.ppermute(value, "core", [(0, 1), (1, 0)])


def turn(values, cosine, sine_a, sine_b):
    width = values.shape[1]
    cosine, sine_a, sine_b = (jnp.concatenate([v] * (width // 128), 1) for v in (cosine, sine_a, sine_b))
    return (
        values * cosine
        + pltpu.roll(values, width - ROT // 2, 1) * sine_a
        + pltpu.roll(values, ROT // 2, 1) * sine_b
    )


def head_mask(shape, head, head_dim):
    lane = lax.broadcasted_iota(jnp.int32, shape, 1)
    return (lane >= head * head_dim) & (lane < (head + 1) * head_dim)


def attend_kernel(heads, head_dim, span, order_ref, qkv_ref, cos_ref, sin_a_ref, sin_b_ref, att_ref, sorted_ref, out_scr):
    seq_len = qkv_ref.shape[1]
    width = heads * head_dim
    for slot in range(seq_len // span):
        rows = pl.ds(pl.multiple_of(order_ref[slot] * span, span), span)
        here = pl.ds(slot * span, span)
        tables = (cos_ref[here, :], sin_a_ref[here, :], sin_b_ref[here, :])
        query = turn(qkv_ref[0, rows, 0:width], *tables).astype(BF)
        sorted_ref[0, here, 0:width] = (query.astype(F32) * (head_dim**-0.5)).astype(BF)
        sorted_ref[0, here, width : 2 * width] = turn(qkv_ref[0, rows, width : 2 * width], *tables).astype(BF)
        sorted_ref[0, here, 2 * width :] = qkv_ref[0, rows, 2 * width :].astype(BF)
    block = min(BLOCK_Q, seq_len)
    for i in range(seq_len // block):
        extent = (i + 1) * block
        here = pl.ds(i * block, block)
        queries = sorted_ref[0, here, 0:width]
        keys = sorted_ref[0, 0:extent, width : 2 * width]
        values = sorted_ref[0, 0:extent, 2 * width :]
        row = lax.broadcasted_iota(jnp.int32, (block, extent), 0) + i * block
        col = lax.broadcasted_iota(jnp.int32, (block, extent), 1)
        total = jnp.zeros((block, width), F32)
        for head in range(heads):
            mask = head_mask((block, width), head, head_dim)
            scores = dot_t(jnp.where(mask, queries, jnp.zeros_like(queries)), keys)
            scores = jnp.where(col <= row, scores, NEG)
            top = jnp.max(scores, 1, keepdims=True)
            weights = jnp.exp(scores - top)
            norm = 1.0 / jnp.sum(weights, 1, keepdims=True)
            probs = (weights * norm).astype(BF)
            total = jnp.where(mask, dot(probs, values), total)
        out_scr[here, :] = total.astype(BF)
    for slot in range(seq_len // span):
        rows = pl.ds(pl.multiple_of(order_ref[slot] * span, span), span)
        att_ref[0, rows, :] = out_scr[slot * span : (slot + 1) * span, :]


def attend_back_kernel(
    heads, head_dim, span, order_ref, sorted_ref, grad_ref, cos_ref, sin_a_ref, sin_b_ref, out_ref, grad_scr, key_scr, value_scr
):
    seq_len = sorted_ref.shape[1]
    width = heads * head_dim
    for slot in range(seq_len // span):
        rows = pl.ds(pl.multiple_of(order_ref[slot] * span, span), span)
        grad_scr[slot * span : (slot + 1) * span, :] = grad_ref[0, rows, :]
    key_scr[...] = jnp.zeros_like(key_scr)
    value_scr[...] = jnp.zeros_like(value_scr)
    block = min(BLOCK_Q, seq_len)

    def put(slot, first, values):
        rows = pl.ds(pl.multiple_of(order_ref[slot] * span, span), span)
        out_ref[0, rows, first : first + width] = values.astype(BF)

    def tables(here):
        return (cos_ref[here, :], -sin_a_ref[here, :], -sin_b_ref[here, :])

    for i in range(seq_len // block):
        extent = (i + 1) * block
        here = pl.ds(i * block, block)
        queries = sorted_ref[0, here, 0:width]
        grads = grad_scr[here, :]
        keys = sorted_ref[0, 0:extent, width : 2 * width]
        values = sorted_ref[0, 0:extent, 2 * width :]
        key = lax.broadcasted_iota(jnp.int32, (extent, block), 0)
        query = lax.broadcasted_iota(jnp.int32, (extent, block), 1) + i * block
        query_grad = jnp.zeros((block, width), F32)
        for head in range(heads):
            mask = head_mask((block, width), head, head_dim)
            own_queries = jnp.where(mask, queries, jnp.zeros_like(queries))
            own_grads = jnp.where(mask, grads, jnp.zeros_like(grads))
            scores = jnp.where(key <= query, dot_t(keys, own_queries), NEG)
            weights = jnp.exp(scores - jnp.max(scores, 0, keepdims=True))
            probs = weights * (1.0 / jnp.sum(weights, 0, keepdims=True))
            probs_grad = dot_t(values, own_grads)
            delta = jnp.sum(probs * probs_grad, 0, keepdims=True)
            score_grad = (probs * (probs_grad - delta)).astype(BF)
            value_scr[0:extent, :] += dot(probs.astype(BF), own_grads)
            key_scr[0:extent, :] += dot(score_grad, own_queries)
            query_grad = jnp.where(mask, t_dot(score_grad, keys), query_grad)
        query_grad = turn(query_grad * (head_dim**-0.5), *tables(here))
        for j in range(block // span):
            put(i * (block // span) + j, 0, query_grad[j * span : (j + 1) * span])
    for slot in range(seq_len // span):
        here = pl.ds(slot * span, span)
        put(slot, width, turn(key_scr[here, :], *tables(here)))
        put(slot, 2 * width, value_scr[here, :])


def attend(order, qkv, tables, heads, head_dim, span, part):
    seq_len, wide = qkv.shape[0] // 2, qkv.shape[1]
    width = wide // 3
    whole = pl.BlockSpec((seq_len, 128), lambda s, o: (0, 0))
    return pl.pallas_call(
        partial(attend_kernel, heads, head_dim, span),
        grid_spec=pltpu.PrefetchScalarGridSpec(
            num_scalar_prefetch=1,
            grid=(1,),
            in_specs=[pl.BlockSpec((1, seq_len, wide), lambda s, o: (part, 0, 0)), whole, whole, whole],
            out_specs=[
                pl.BlockSpec((1, seq_len, width), lambda s, o: (0, 0, 0)),
                pl.BlockSpec((1, seq_len, wide), lambda s, o: (0, 0, 0)),
            ],
            scratch_shapes=[pltpu.VMEM((seq_len, width), BF)],
        ),
        out_shape=[
            jax.ShapeDtypeStruct((1, seq_len, width), BF),
            jax.ShapeDtypeStruct((1, seq_len, wide), BF),
        ],
        compiler_params=pltpu.CompilerParams(vmem_limit_bytes=40 * 2**20),
        cost_estimate=cost(8 * heads * seq_len * seq_len * head_dim, 8 * seq_len * wide),
        name="attend",
    )(order, qkv.reshape(2, seq_len, wide), *tables)


def attend_back(order, kept, grads, tables, heads, head_dim, span, part):
    _, seq_len, wide = kept.shape
    width = wide // 3
    whole = pl.BlockSpec((seq_len, 128), lambda s, o: (0, 0))
    one = pl.BlockSpec((1, seq_len, wide), lambda s, o: (0, 0, 0))
    return pl.pallas_call(
        partial(attend_back_kernel, heads, head_dim, span),
        grid_spec=pltpu.PrefetchScalarGridSpec(
            num_scalar_prefetch=1,
            grid=(1,),
            in_specs=[one, pl.BlockSpec((1, seq_len, width), lambda s, o: (part, 0, 0)), whole, whole, whole],
            out_specs=one,
            scratch_shapes=[
                pltpu.VMEM((seq_len, width), BF),
                pltpu.VMEM((seq_len, width), F32),
                pltpu.VMEM((seq_len, width), F32),
            ],
        ),
        out_shape=jax.ShapeDtypeStruct((1, seq_len, wide), BF),
        compiler_params=params(40),
        cost_estimate=cost(20 * heads * seq_len * seq_len * head_dim, 6 * seq_len * wide),
        name="attend_back",
    )(order, kept, grads, *tables).reshape(seq_len, wide)


def after(value, *others):
    return lax.optimization_barrier((value,) + others)[0]


def whole_block(shape):
    return pl.BlockSpec(shape, lambda *_: (0,) * len(shape))


def params(limit):
    return pltpu.CompilerParams(vmem_limit_bytes=limit * 2**20)


ANYWHERE = pl.BlockSpec(memory_space=pl.ANY)
SCALARS = pl.BlockSpec(memory_space=pltpu.SMEM)
VMEM = pl.BlockSpec(memory_space=pltpu.VMEM)
ROWS = 256


def to_blocks_kernel(n_q, n_t, heads, head_dim, units, at_ref, qkv_ref, up_ref, *out_refs):
    n_z = n_t // 2
    width = heads * head_dim
    core, z = at_ref[0], at_ref[1]
    rows = qkv_ref.shape[0]
    low = lax.broadcasted_iota(jnp.int32, (rows, 128), 1) < head_dim
    per = 128 // head_dim
    for c in range(2):
        for s in range(n_z):
            out_ref = out_refs[s].at[pl.ds(c * rows, rows)]
            t = lax.rem(core + c, 2) * n_z + (z ^ s)
            odd = lax.rem(t, per)
            for which in range(3):
                for j in range(0, heads, per):
                    tiles = []
                    for i in range(per):
                        first = (which * heads + j + i) * n_t * head_dim + (t // per) * 128
                        tile = qkv_ref[:, pl.ds(pl.multiple_of(first, 128), 128)].astype(F32)
                        tiles.append(tile)
                    even = jnp.where(low, tiles[0], pltpu.roll(tiles[1], head_dim, 1))
                    uneven = jnp.where(low, pltpu.roll(tiles[0], head_dim, 1), tiles[1])
                    at = which * width + j * head_dim
                    out_ref[:, at : at + 128] = jnp.where(odd == 0, even, uneven).astype(BF)
            for q in range(n_q):
                at = 3 * width + q * units
                if units % 128 == 0:
                    first = pl.multiple_of((q * n_t + t) * units, 128)
                    out_ref[:, at : at + units] = up_ref[:, pl.ds(first, units)]
                else:
                    for k in range(n_t):

                        @pl.when(t == k)
                        def _(at=at, q=q, k=k):
                            first = (q * n_t + k) * units
                            out_ref[:, at : at + units] = up_ref[:, first : first + units]


def to_blocks(at, qkv, up, n_q, n_t, heads, head_dim, units):
    rows = qkv.shape[0]
    wide = 3 * heads * head_dim + n_q * units
    return pl.pallas_call(
        partial(to_blocks_kernel, n_q, n_t, heads, head_dim, units),
        in_specs=[SCALARS, VMEM, VMEM],
        out_specs=[VMEM] * (n_t // 2),
        out_shape=[jax.ShapeDtypeStruct((2 * rows, wide), BF)] * (n_t // 2),
        compiler_params=params(16),
        cost_estimate=cost(0, 4 * rows * wide * n_t),
        name="to_blocks",
    )(at, qkv, up)


def theirs_kernel(*refs):
    pieces, out_ref = refs[:-1], refs[-1]
    rows = pieces[0].shape[0] // 2
    for s, piece in enumerate(pieces):
        out_ref[s * rows : (s + 1) * rows, :] = piece[rows:, :]


def theirs(pieces):
    rows, columns = pieces[0].shape
    return pl.pallas_call(
        theirs_kernel,
        in_specs=[VMEM] * len(pieces),
        out_specs=VMEM,
        out_shape=jax.ShapeDtypeStruct((len(pieces) * rows // 2, columns), BF),
        compiler_params=params(16),
        cost_estimate=cost(0, 2 * len(pieces) * rows * columns),
        name="theirs",
    )(*pieces)


def piece_rows(came_refs, got_ref, at_ref):
    n_z = len(came_refs)
    rows = came_refs[0].shape[0] // 2
    core, z = at_ref[0], at_ref[1]
    for s in range(n_z):
        yield core * n_z + (z ^ s), came_refs[s][0:rows, :]
        yield (1 - core) * n_z + (z ^ s), got_ref[s * rows : (s + 1) * rows, :]


def stack_rows_kernel(at_ref, *refs):
    out_ref = refs[-1]
    for block, values in piece_rows(refs[:-2], refs[-2], at_ref):
        rows = values.shape[0]
        out_ref[pl.ds(pl.multiple_of(block * rows, 16), rows), :] = values


def stack_rows(at, came, got):
    rows, columns = came[0].shape
    return pl.pallas_call(
        stack_rows_kernel,
        in_specs=[SCALARS] + [VMEM] * (len(came) + 1),
        out_specs=VMEM,
        out_shape=jax.ShapeDtypeStruct((len(came) * rows, columns), BF),
        compiler_params=params(16),
        cost_estimate=cost(0, 4 * len(came) * rows * columns),
        name="stack_rows",
    )(at, *came, got)


def last_sum_kernel(n_z, n_parts, tail, at_ref, *refs):
    part_refs, out_refs = refs[:n_parts], refs[n_parts:]
    n_t = 2 * n_z
    below = 16 if tail else 0
    count = part_refs[0].shape[0] - tail
    rows = count // n_t
    core, z = at_ref[0], at_ref[1]
    if tail:
        total = part_refs[0][count:, :].astype(F32)
        for part_ref in part_refs[1:]:
            total = total + part_ref[count:, :].astype(F32)
        values = total[: tail // 2, :] + total[tail // 2 :, :]
        index = lax.broadcasted_iota(jnp.int32, values.shape, 0)
    for c in range(2):
        for s in range(n_z):
            block = lax.rem(core + c, 2) * n_z + (z ^ s)
            here = pl.ds(pl.multiple_of(block * rows, 16), rows)
            total = part_refs[0][here, :].astype(F32)
            for part_ref in part_refs[1:]:
                total = total + part_ref[here, :].astype(F32)
            first = c * (rows + below)
            out_refs[s][first : first + rows, :] = total.astype(BF)
            if tail:
                own = jnp.sum(jnp.where(index == block, values, 0.0), 0, keepdims=True)
                high, low = in_two(own)
                row = lax.broadcasted_iota(jnp.int32, (below, own.shape[1]), 0)
                both = jnp.where(row == 0, high.astype(F32), jnp.where(row == 1, low.astype(F32), 0.0))
                out_refs[s][first + rows : first + rows + below, :] = both.astype(BF)


def last_sum(at, parts, n_t, tail=0):
    columns = parts[0].shape[1]
    rows = 2 * ((parts[0].shape[0] - tail) // n_t + (16 if tail else 0))
    return pl.pallas_call(
        partial(last_sum_kernel, n_t // 2, len(parts), tail),
        in_specs=[SCALARS] + [VMEM] * len(parts),
        out_specs=[VMEM] * (n_t // 2),
        out_shape=[jax.ShapeDtypeStruct((rows, columns), BF)] * (n_t // 2),
        compiler_params=params(24),
        cost_estimate=cost(0, 8 * rows * n_t * columns),
        name="last_sum",
    )(at, *parts)


def from_blocks_kernel(groups, piece, below, at_ref, *refs):
    came_refs, got_ref, refs = refs[: -3 - (below > 0)], refs[-3 - (below > 0)], refs[-2 - (below > 0) :]
    out_ref, held_ref = refs[0], refs[-1]
    n_t = held_ref.shape[0]
    rows = out_ref.shape[0]
    total = 0.0
    for block, values in piece_rows(came_refs, got_ref, at_ref):
        held_ref[block] = values[0:rows, :]
        if below:
            under = values[rows:, :].astype(F32)
            total = total + under[0:1, :] + under[1:2, :]
    for t in range(n_t):
        for j in range(groups):
            first = (j * n_t + t) * piece
            out_ref[:, first : first + piece] = held_ref[t, :, j * piece : (j + 1) * piece].astype(F32)
    if below:
        refs[1][...] = jnp.broadcast_to(total, refs[1].shape)


def from_blocks(at, came, got, groups, piece, below=0):
    n_t = 2 * len(came)
    rows = came[0].shape[0] // 2 - below
    columns = groups * piece
    return pl.pallas_call(
        partial(from_blocks_kernel, groups, piece, below),
        in_specs=[SCALARS] + [VMEM] * (len(came) + 1),
        out_specs=[VMEM] * (1 + (below > 0)),
        out_shape=[jax.ShapeDtypeStruct((rows, columns * n_t), F32)]
        + [jax.ShapeDtypeStruct((8, columns), F32)] * (below > 0),
        scratch_shapes=[pltpu.VMEM((n_t, rows, columns), BF)],
        compiler_params=params(16),
        cost_estimate=cost(0, 8 * rows * columns * n_t),
        name="from_blocks",
    )(at, *came, got)


def places_kernel(n_q, n_z, q_order, at_ref, table_ref, turns_ref, order_ref):
    q, z = at_ref[2], at_ref[1]
    place = 0
    for i, index in enumerate(q_order):
        place = place + jnp.where(q == index, i, 0)
    for k, offset in enumerate(ring_offsets(n_q)):
        at = lax.rem(place + offset + n_q, n_q)
        turn_of = 0
        for i, index in enumerate(q_order):
            turn_of = turn_of + jnp.where(at == i, index, 0)
        turns_ref[k] = turn_of
    for k, offset in enumerate(ring_offsets(n_z)):
        row = lax.rem(z + offset + n_z, n_z)
        for j in range(2):
            order_ref[table_ref[row, j]] = 2 * k + j


def find_places(at, span_table, n_q, n_z, q_order):
    return pl.pallas_call(
        partial(places_kernel, n_q, n_z, q_order),
        in_specs=[SCALARS, SCALARS],
        out_specs=[SCALARS, SCALARS],
        out_shape=[jax.ShapeDtypeStruct((n_q,), jnp.int32), jax.ShapeDtypeStruct((2 * n_z,), jnp.int32)],
        cost_estimate=cost(0, 1000),
        name="places",
    )(at, span_table)


def pack_small_kernel(*refs):
    out_ref = refs[-1]
    row = 0
    for ref in refs[:-1]:
        size = ref.shape[1]
        for first in range(0, size, 128):
            count = min(128, size - first)
            out_ref[row : row + 1, 0:count] = ref[:, first : first + count].astype(F32).astype(BF)
            row += 1


def pack_small(vectors):
    return pl.pallas_call(
        pack_small_kernel,
        in_specs=[VMEM] * len(vectors),
        out_specs=VMEM,
        out_shape=jax.ShapeDtypeStruct((256, 128), BF),
        cost_estimate=cost(0, 65536),
        name="pack_small",
    )(*[v.reshape(1, -1) for v in vectors])


def pack_vectors_kernel(shape, widths, at_ref, norm_a_ref, norm_b_ref, g_ref, up_ref, out_ref):
    n_q, n_t, heads, head_dim, units = shape
    part, biases = widths
    t_here = at_ref[0] * (n_t // 2) + at_ref[1]
    gain = norm_a_ref[0:1, :] + norm_b_ref[0:1, :]
    shift = norm_a_ref[1:2, :] + norm_b_ref[1:2, :]
    qkv = norm_a_ref[2:3, :] + norm_b_ref[2:3, :]
    g = g_ref[0:1, :]
    up = up_ref[0:1, :]
    columns = out_ref.shape[2]
    for q in range(n_q):
        lines = []
        for t in range(n_t):
            owner = q * n_t + t
            here = slice(owner * part, (owner + 1) * part)
            cells = [gain[:, here], shift[:, here], g[:, here]]
            first, end = owner * biases, (owner + 1) * biases
            while first < end:
                which, head = first // (HEADS * head_dim), first // head_dim % HEADS
                stop = min(end, (first // head_dim + 1) * head_dim)
                source = (which * heads + head // n_t) * head_dim + first % head_dim
                cells.append(jnp.where(t_here == head % n_t, qkv[:, source : source + stop - first], 0.0))
                first = stop
            cells.append(jnp.where(t_here == t, up[:, q * units : (q + 1) * units], 0.0))
            used = 3 * part + biases + units
            cells.append(jnp.zeros((1, columns - used), F32))
            lines.append(jnp.concatenate(cells, 1))
        high, low = in_two(jnp.concatenate(lines, 0))
        out_ref[q, 0:n_t, :] = high
        out_ref[q, n_t:, :] = low


def pack_vectors(at, norm_a, norm_b, g, up, shape, widths, columns):
    n_q, n_t = shape[:2]
    return pl.pallas_call(
        partial(pack_vectors_kernel, shape, widths),
        in_specs=[SCALARS] + [VMEM] * 4,
        out_specs=VMEM,
        out_shape=jax.ShapeDtypeStruct((n_q, 2 * n_t, columns), BF),
        cost_estimate=cost(0, 4 * n_q * n_t * columns),
        name="pack_vectors",
    )(at, norm_a, norm_b, g, up)


def load_pieces(plan, turns_ref, piece_refs, target, sem):
    copies = []
    for i, (piece, first, rows, slot, scale, base) in enumerate(plan):
        start = pl.multiple_of(turns_ref[slot] * scale + base, 16)
        copies.append(pltpu.make_async_copy(piece_refs[piece].at[pl.ds(first, rows)], target.at[pl.ds(start, rows)], sem.at[i]))
    return copies


def fetch_slots(plan, slot_refs, buffers, sems):
    i = pl.program_id(0)

    def copies(k):
        return [
            pltpu.make_async_copy(slot_refs[which], buffers.at[k % 2, pl.ds(first, rows)], sems.at[k % 2, part])
            for part, (which, first, rows) in enumerate(plan[k])
        ]

    for k in range(len(plan)):

        @pl.when(i == k)
        def _(k=k):
            for copy in (copies(0) if k == 0 else []) + (copies(k + 1) if k + 1 < len(plan) else []):
                copy.start()
            for copy in copies(k):
                copy.wait()


class Gathered:
    def __init__(self, arrays, plan, turns):
        self.arrays = arrays
        self.plan = tuple(plan)
        self.starts = turns
        self.rows = sum(piece[2] for piece in plan)
        self.columns = arrays[0].shape[1]

    def scratch(self):
        return [pltpu.VMEM((self.rows, self.columns), BF), pltpu.SemaphoreType.DMA((len(self.plan),))]

    def specs(self):
        return [ANYWHERE] * len(self.arrays)


def put_block(plan, block, held_ref, out_refs, sem):
    i = pl.program_id(0)
    held_ref[i] = block

    def copies(k):
        return [
            pltpu.make_async_copy(held_ref.at[k, pl.ds(first, rows)], out_refs[which], sem.at[which])
            for which, first, rows in plan[k]
        ]

    for k in range(len(plan)):

        @pl.when(i == k)
        def _(k=k):
            for copy in copies(k):
                copy.start()

    @pl.when(i == len(plan) - 1)
    def _():
        for k in range(len(plan)):
            for copy in copies(k):
                copy.wait()


def normed(rows):
    mean = jnp.mean(rows, -1, keepdims=True)
    centred = rows - mean
    scale = lax.rsqrt(jnp.mean(centred * centred, -1, keepdims=True) + EPS)
    return centred * scale, scale


def project_kernel(split, x_plan, n_x, w_plan, n_w, starts_ref, *refs):
    x_refs, refs = refs[:n_x], refs[n_x:]
    w_refs, refs = refs[:n_w], refs[n_w:]
    gain_ref, shift_ref, b_ref, x_out_ref, hidden_ref, qkv_ref, act_ref, slope_ref, w_ref, w_sem, x_buf, x_sem = refs

    @pl.when(pl.program_id(0) == 0)
    def _():
        for copy in load_pieces(w_plan, starts_ref, w_refs, w_ref, w_sem):
            copy.start()

    fetch_slots(x_plan, x_refs, x_buf, x_sem)
    x = x_buf[lax.rem(pl.program_id(0), 2)]
    x_out_ref[...] = x
    xhat, _ = normed(x.astype(F32))
    hidden = (xhat * gain_ref[...] + shift_ref[...]).astype(BF)
    hidden_ref[...] = hidden

    @pl.when(pl.program_id(0) == 0)
    def _():
        for copy in load_pieces(w_plan, starts_ref, w_refs, w_ref, w_sem):
            copy.wait()

    pre = dot(hidden, w_ref[:, split:]) + b_ref[:, split:]
    root = math.sqrt(2.0 / math.pi)
    square = pre * pre
    turned = jnp.tanh(root * pre * (1.0 + 0.044715 * square))
    act_ref[...] = (0.5 * pre * (1.0 + turned)).astype(BF)
    slope = 0.5 * (1.0 + turned) + 0.5 * pre * (1.0 - turned * turned) * (root * (1.0 + 3 * 0.044715 * square))
    slope_ref[...] = slope.astype(BF)
    qkv_ref[...] = dot(hidden, w_ref[:, :split]) + b_ref[:, :split]


def project(x_arrays, x_plan, gain, shift, w, b, split):
    rows, width = x_arrays[0].shape
    count = rows * len(x_plan)
    wide = w.columns

    def block(columns):
        return pl.BlockSpec((rows, columns), lambda i, s: (i, 0))

    return pl.pallas_call(
        partial(project_kernel, split, x_plan, len(x_arrays), w.plan, len(w.arrays)),
        grid_spec=pltpu.PrefetchScalarGridSpec(
            num_scalar_prefetch=1,
            grid=(len(x_plan),),
            in_specs=[ANYWHERE] * len(x_arrays) + w.specs() + [whole_block((1, width))] * 2 + [whole_block(b.shape)],
            out_specs=[block(width), block(width), block(split), block(wide - split), block(wide - split)],
            scratch_shapes=w.scratch() + [pltpu.VMEM((2, rows, width), BF), pltpu.SemaphoreType.DMA((2, 2))],
        ),
        out_shape=[
            jax.ShapeDtypeStruct((count, width), BF),
            jax.ShapeDtypeStruct((count, width), BF),
            jax.ShapeDtypeStruct((count, split), F32),
            jax.ShapeDtypeStruct((count, wide - split), BF),
            jax.ShapeDtypeStruct((count, wide - split), BF),
        ],
        compiler_params=params(58),
        cost_estimate=cost(2 * count * width * wide, 8 * count * width + 2 * width * wide),
        name="project",
    )(w.starts, *x_arrays, *w.arrays, gain, shift, b)


def combine_kernel(split, w_plan, n_w, plan, n_arrived, starts_ref, act_ref, att_ref, *refs):
    w_refs, refs = refs[:n_w], refs[n_w:]
    arrived_refs, refs = refs[:n_arrived], refs[n_arrived:]
    out_refs, (w_ref, w_sem, held, held_sem, buf, buf_sem) = refs[:-6], refs[-6:]

    @pl.when(pl.program_id(0) == 0)
    def _():
        copies = load_pieces(w_plan, starts_ref, w_refs, w_ref, w_sem)
        for copy in copies:
            copy.start()
        for copy in copies:
            copy.wait()

    total = dot(act_ref[...], w_ref[:split, :]) + dot(att_ref[...], w_ref[split:, :])
    if n_arrived:
        fetch_slots([((k, 0, total.shape[0]),) for k in range(n_arrived)], arrived_refs, buf, buf_sem)
        total = total + buf[lax.rem(pl.program_id(0), 2)].astype(F32)
    put_block(plan, total.astype(BF), held, out_refs, held_sem)


def held_blocks(steps, rows, width):
    return [pltpu.VMEM((steps, rows, width), BF), pltpu.SemaphoreType.DMA((steps + 1,))]


def combine(act, att, w, part, rows, arrived=()):
    count, split = act.shape[0] // 2, act.shape[1]
    own_width = att.shape[-1]
    att = att.reshape(count, own_width)
    width = w.columns
    steps = count // rows
    base = part * steps
    plan = slot_plan(steps, rows) if arrived else [((k, 0, rows),) for k in range(steps)]
    shapes = [jax.ShapeDtypeStruct((r, width), BF) for slot in plan for _, _, r in slot]
    return pl.pallas_call(
        partial(combine_kernel, split, w.plan, len(w.arrays), plan, len(arrived)),
        grid_spec=pltpu.PrefetchScalarGridSpec(
            num_scalar_prefetch=1,
            grid=(steps,),
            in_specs=[
                pl.BlockSpec((rows, split), lambda i, s: (i + base, 0)),
                pl.BlockSpec((rows, own_width), lambda i, s: (i, 0)),
            ]
            + w.specs()
            + [ANYWHERE] * len(arrived),
            out_specs=[ANYWHERE] * len(shapes),
            scratch_shapes=w.scratch()
            + held_blocks(steps, rows, width)
            + [pltpu.VMEM((2, rows, width), BF), pltpu.SemaphoreType.DMA((2, 2))],
        ),
        out_shape=shapes,
        compiler_params=params(32),
        cost_estimate=cost(2 * count * width * w.rows, 4 * count * width + 2 * width * w.rows),
        name="combine",
    )(w.starts, act, att, *w.arrays, *arrived)


def combine_back_kernel(split, g_plan, n_g, w_plan, n_w, starts_ref, *refs):
    g_refs, refs = refs[:n_g], refs[n_g:]
    w_refs, refs = refs[:n_w], refs[n_w:]
    slope_ref, g_out_ref, pre_grad_ref, att_grad_ref, sums_ref, w_ref, w_sem, g_buf, g_sem = refs

    @pl.when(pl.program_id(0) == 0)
    def _():
        for copy in load_pieces(w_plan, starts_ref, w_refs, w_ref, w_sem):
            copy.start()

    fetch_slots(g_plan, g_refs, g_buf, g_sem)

    @pl.when(pl.program_id(0) == 0)
    def _():
        for copy in load_pieces(w_plan, starts_ref, w_refs, w_ref, w_sem):
            copy.wait()

    grad = g_buf[lax.rem(pl.program_id(0), 2)]
    g_out_ref[...] = grad

    @pl.when(pl.program_id(0) == 0)
    def _():
        sums_ref[...] = jnp.zeros_like(sums_ref)
        sums_ref[0:1, :] = jnp.sum(grad.astype(F32), 0, keepdims=True)

    pre_grad_ref[...] = (dot_t(grad, w_ref[:split, :]) * slope_ref[...].astype(F32)).astype(BF)
    att_grad_ref[...] = dot_t(grad, w_ref[split:, :]).astype(BF)


def combine_back(g_arrays, g_plan, w, slope):
    rows, width = g_arrays[0].shape
    count = rows * len(g_plan)
    split = slope.shape[1]
    rest = w.rows - split

    def block(columns):
        return pl.BlockSpec((rows, columns), lambda i, s: (i, 0))

    return pl.pallas_call(
        partial(combine_back_kernel, split, g_plan, len(g_arrays), w.plan, len(w.arrays)),
        grid_spec=pltpu.PrefetchScalarGridSpec(
            num_scalar_prefetch=1,
            grid=(len(g_plan),),
            in_specs=[ANYWHERE] * len(g_arrays) + w.specs() + [block(split)],
            out_specs=[block(width), block(split), block(rest), whole_block((8, width))],
            scratch_shapes=w.scratch() + [pltpu.VMEM((2, rows, width), BF), pltpu.SemaphoreType.DMA((2, 2))],
        ),
        out_shape=[
            jax.ShapeDtypeStruct((count, width), BF),
            jax.ShapeDtypeStruct((count, split), BF),
            jax.ShapeDtypeStruct((count, rest), BF),
            jax.ShapeDtypeStruct((8, width), F32),
        ],
        compiler_params=params(58),
        cost_estimate=cost(2 * count * width * w.rows, 6 * count * width + 2 * width * w.rows),
        name="combine_back",
    )(w.starts, *g_arrays, *w.arrays, slope)


def project_back_kernel(split, w_plan, n_w, plan, n_arrived, starts_ref, qkv_grad_ref, pre_grad_ref, x_ref, *refs):
    w_refs, refs = refs[:n_w], refs[n_w:]
    arrived_refs, refs = refs[:n_arrived], refs[n_arrived:]
    out_refs, (sums_ref, w_ref, w_sem, held, held_sem, buf, buf_sem) = refs[:-7], refs[-7:]

    @pl.when(pl.program_id(0) == 0)
    def _():
        copies = load_pieces(w_plan, starts_ref, w_refs, w_ref, w_sem)
        for copy in copies:
            copy.start()
        sums_ref[...] = jnp.zeros_like(sums_ref)
        for copy in copies:
            copy.wait()

    grad = dot_t(qkv_grad_ref[...], w_ref[:, :split]) + dot_t(pre_grad_ref[...], w_ref[:, split:])
    xhat, _ = normed(x_ref[...].astype(F32))
    sums_ref[0:1, :] += jnp.sum(grad * xhat, 0, keepdims=True)
    sums_ref[1:2, :] += jnp.sum(grad, 0, keepdims=True)
    sums_ref[2:3, 0:split] += jnp.sum(qkv_grad_ref[...].astype(F32), 0, keepdims=True)
    if n_arrived:
        fetch_slots([((k, 0, grad.shape[0]),) for k in range(n_arrived)], arrived_refs, buf, buf_sem)
        grad = grad + buf[lax.rem(pl.program_id(0), 2)].astype(F32)
    put_block(plan, grad.astype(BF), held, out_refs, held_sem)


def project_back(qkv_grad, pre_grad, w, x, part, rows, arrived=()):
    count, split = qkv_grad.shape
    width = x.shape[1]
    steps = count // rows
    base = part * steps
    plan = slot_plan(steps, rows) if arrived else [((k, 0, rows),) for k in range(steps)]
    shapes = [jax.ShapeDtypeStruct((r, width), BF) for slot in plan for _, _, r in slot]

    def block(columns):
        return pl.BlockSpec((rows, columns), lambda i, s: (i + base, 0))

    *out, sums = pl.pallas_call(
        partial(project_back_kernel, split, w.plan, len(w.arrays), plan, len(arrived)),
        grid_spec=pltpu.PrefetchScalarGridSpec(
            num_scalar_prefetch=1,
            grid=(steps,),
            in_specs=[pl.BlockSpec((rows, split), lambda i, s: (i, 0)), block(pre_grad.shape[1]), block(width)] + w.specs() + [ANYWHERE] * len(arrived),
            out_specs=[ANYWHERE] * len(shapes) + [whole_block((8, width))],
            scratch_shapes=w.scratch()
            + held_blocks(steps, rows, width)
            + [pltpu.VMEM((2, rows, width), BF), pltpu.SemaphoreType.DMA((2, 2))],
        ),
        out_shape=shapes + [jax.ShapeDtypeStruct((8, width), F32)],
        compiler_params=params(58),
        cost_estimate=cost(2 * count * width * w.columns, 6 * count * width + 2 * width * w.columns),
        name="project_back",
    )(w.starts, qkv_grad, pre_grad, x, *w.arrays, *arrived)
    return out, sums


def weight_grad_kernel(n_right, with_tail, turns_ref, left_ref, *refs):
    right_refs, refs = refs[:n_right], refs[n_right:]
    tail_refs, refs = refs[:with_tail], refs[with_tail:]
    out_refs, (sums_ref, held, sem) = refs[:-3], refs[-3:]

    @pl.when(pl.program_id(0) == 0)
    def _():
        sums_ref[...] = jnp.zeros_like(sums_ref)
        sums_ref[0:1, :] = sum(jnp.sum(right_ref[...].astype(F32), 0, keepdims=True) for right_ref in right_refs)

    count = right_refs[0].shape[0]
    total = t_dot(left_ref[0:count, :], right_refs[0][...])
    for k in range(1, n_right):
        total = total + t_dot(left_ref[k * count : (k + 1) * count, :], right_refs[k][...])
    block = total.astype(BF)
    if with_tail:
        block = jnp.concatenate([block, tail_refs[0][0]], 0)
    put_block(slot_plan(held.shape[0], held.shape[1]), block, held, out_refs, sem)


def slot_shapes(n, rows, columns):
    return [jax.ShapeDtypeStruct((r, columns), BF) for slot in slot_plan(n, rows) for _, _, r in slot]


def weight_grad(turns, left, rights, tail=None):
    n_q = turns.shape[0]
    count, wide = left.shape
    columns = rights[0].shape[1]
    part = wide // n_q
    rows = part + (0 if tail is None else tail.shape[1])
    extra = [] if tail is None else [tail]
    shapes = slot_shapes(n_q, rows, columns)
    *out, sums = pl.pallas_call(
        partial(weight_grad_kernel, len(rights), len(extra)),
        grid_spec=pltpu.PrefetchScalarGridSpec(
            num_scalar_prefetch=1,
            grid=(n_q,),
            in_specs=[pl.BlockSpec((count, part), lambda k, s: (0, s[k]))]
            + [whole_block(right.shape) for right in rights]
            + [pl.BlockSpec((1,) + v.shape[1:], lambda k, s: (s[k], 0, 0)) for v in extra],
            out_specs=[ANYWHERE] * len(shapes) + [whole_block((8, columns))],
            scratch_shapes=held_blocks(n_q, rows, columns),
        ),
        out_shape=shapes + [jax.ShapeDtypeStruct((8, columns), F32)],
        compiler_params=params(58),
        cost_estimate=cost(2 * count * wide * columns, 2 * count * (wide + columns) + 2 * wide * columns),
        name="weight_grad",
    )(turns, left, *rights, *extra)
    return out, sums


def down_grad_kernel(head_rows, turns_ref, act_ref, att_a_ref, att_b_ref, g_ref, *refs):
    out_refs, (heads_ref, held, sem) = refs[:-3], refs[-3:]
    units = act_ref.shape[1]
    k = pl.program_id(0)

    @pl.when(k == 0)
    def _():
        half = att_a_ref.shape[0]
        heads_ref[...] = (t_dot(att_a_ref[...], g_ref[0:half, :]) + t_dot(att_b_ref[...], g_ref[half:, :])).astype(BF)

    rows = pl.ds(pl.multiple_of(turns_ref[k] * head_rows, head_rows), head_rows)
    block = jnp.concatenate([t_dot(act_ref[...], g_ref[...]).astype(BF), heads_ref[rows, :]], 0)
    put_block(slot_plan(held.shape[0], held.shape[1]), block, held, out_refs, sem)


def down_grad(turns, act, att, g, head_rows):
    n_q = turns.shape[0]
    count, wide = act.shape
    own_width = att[0].shape[-1]
    att = [a.reshape(count // 2, own_width) for a in att]
    width = g.shape[1]
    units = wide // n_q
    if not head_rows:
        whole = t_dot(act, g).astype(BF).reshape(n_q, units, width)[turns]
        blocks = [whole[k][first : first + r] for k, slot in enumerate(slot_plan(n_q, units)) for _, first, r in slot]
        return blocks, t_dot(jnp.concatenate(att, 0), g)
    out = pl.pallas_call(
        partial(down_grad_kernel, head_rows),
        grid_spec=pltpu.PrefetchScalarGridSpec(
            num_scalar_prefetch=1,
            grid=(n_q,),
            in_specs=[pl.BlockSpec((count, units), lambda k, s: (0, s[k]))] + [whole_block(v.shape) for v in (*att, g)],
            out_specs=[ANYWHERE] * (n_q + 1),
            scratch_shapes=[pltpu.VMEM((own_width, width), BF)] + held_blocks(n_q, units + head_rows, width),
        ),
        out_shape=slot_shapes(n_q, units + head_rows, width),
        compiler_params=params(58),
        cost_estimate=cost(2 * count * (wide + own_width) * width, 2 * count * (wide + width) + 2 * wide * width),
        name="down_grad",
    )(turns, act, *att, g)
    return list(out), None


def finish_kernel(x_ref, g_ref, gain_ref, *refs):
    part_refs, out_ref = refs[:-1], refs[-1]
    grad = part_refs[0][...].astype(F32)
    for part_ref in part_refs[1:]:
        grad = grad + part_ref[...].astype(F32)
    xhat, scale = normed(x_ref[...].astype(F32))
    m = grad * gain_ref[...]
    x_grad = (m - jnp.mean(m, -1, keepdims=True) - xhat * jnp.mean(m * xhat, -1, keepdims=True)) * scale
    out_ref[...] = (g_ref[...].astype(F32) + x_grad).astype(BF)


def finish(parts, x, g, gain):
    count, width = x.shape
    rows = math.gcd(count, 128)
    block = pl.BlockSpec((rows, width), lambda i: (i, 0))
    return pl.pallas_call(
        finish_kernel,
        grid=(count // rows,),
        in_specs=[block] * 2 + [whole_block((1, width))] + [block] * len(parts),
        out_specs=block,
        out_shape=jax.ShapeDtypeStruct((count, width), BF),
        cost_estimate=cost(20 * count * width, 12 * count * width),
        name="finish",
    )(x, g, gain, *parts)


def output_kernel(x_ref, bias_ref, *refs):
    part_refs, out_ref = refs[:-1], refs[-1]
    total = x_ref[...].astype(F32) + bias_ref[...]
    for part_ref in part_refs:
        total = total + part_ref[...].astype(F32)
    out_ref[...] = total.astype(BF)


def output_sum(x, bias, parts):
    count, width = x.shape
    rows = math.gcd(count, 128)
    block = pl.BlockSpec((rows, width), lambda i: (i, 0))
    return pl.pallas_call(
        output_kernel,
        grid=(count // rows,),
        in_specs=[block, whole_block((1, width))] + [block] * len(parts),
        out_specs=block,
        out_shape=jax.ShapeDtypeStruct((count, width), BF),
        cost_estimate=cost(4 * count * width, 10 * count * width),
        name="output_sum",
    )(x, bias, *parts)


def split_sum(parts, cuts):
    count, width = parts[0].shape
    wide = math.gcd(width, 1024)
    ends = [sum(cuts[: i + 1]) for i in range(len(cuts))]

    def kernel(*refs):
        part_refs, out_refs = refs[: len(parts)], refs[len(parts) :]
        total = part_refs[0][...].astype(F32)
        for part_ref in part_refs[1:]:
            total = total + part_ref[...].astype(F32)
        for end, rows, out_ref in zip(ends, cuts, out_refs):
            out_ref[...] = total[end - rows : end, :]

    return pl.pallas_call(
        kernel,
        grid=(width // wide,),
        in_specs=[pl.BlockSpec((count, wide), lambda i: (0, i))] * len(parts),
        out_specs=[pl.BlockSpec((rows, wide), lambda i: (0, i)) for rows in cuts],
        out_shape=[jax.ShapeDtypeStruct((rows, width), F32) for rows in cuts],
        cost_estimate=cost(4 * count * width, 12 * count * width),
        name="split_sum",
    )(*parts)


def tables_kernel(head_dim, cos_ref, sin_a_ref, sin_b_ref):
    rows = cos_ref.shape[0]
    half = ROT // 2
    lane = lax.broadcasted_iota(jnp.int32, (1, 128), 1) % head_dim
    step = (lane % half).astype(F32) * (-2.0 * math.log(10000.0) / ROT)
    freqs = jnp.where(lane < ROT, jnp.exp(step), 0.0)
    position = lax.broadcasted_iota(jnp.int32, (rows, 128), 0) + pl.program_id(0) * rows
    angles = position.astype(F32) * freqs
    cosine, sine = jnp.cos(angles), jnp.sin(angles)
    cos_ref[...] = cosine
    sin_a_ref[...] = jnp.where(lane < half, -sine, 0.0)
    sin_b_ref[...] = jnp.where((lane >= half) & (lane < ROT), sine, 0.0)


def rotary_tables(seq_len, head_dim):
    width = 128
    block = pl.BlockSpec((128, width), lambda i: (i, 0))
    return pl.pallas_call(
        partial(tables_kernel, head_dim),
        grid=(seq_len // 128,),
        out_specs=[block] * 3,
        out_shape=[jax.ShapeDtypeStruct((seq_len, width), F32)] * 3,
        cost_estimate=cost(100 * seq_len * width, 12 * seq_len * width),
        name="rotary_tables",
    )()


def per_device(
    inputs,
    span_table,
    ln_gain,
    ln_bias,
    qkv_weight,
    qkv_bias,
    out_weight,
    out_bias,
    fc1_weight,
    fc1_bias,
    fc2_weight,
    fc2_bias,
    cotangent,
):
    rows, width = inputs.shape
    head_dim = width // HEADS
    n_q, n_z = lax.axis_size("q"), lax.axis_size("ctx")
    n_t = 2 * n_z
    n_all = n_q * n_t
    q, core, z = lax.axis_index("q"), lax.axis_index("core"), lax.axis_index("ctx")
    t = core * n_z + z
    at = jnp.stack([core, z, q]).astype(jnp.int32)
    span = rows // 2
    seq_len = rows * n_z
    heads = HEADS // n_t
    own_width = heads * head_dim
    split = 3 * own_width
    units = fc2_weight.shape[0]
    own_units = units * n_q
    d_rows = qkv_weight.shape[0]
    every = ("q", "core", "ctx")
    z_order = list(range(n_z))
    q_order = [0, 1, 3, 2] if n_q == 4 else list(range(n_q))
    turns, order = find_places(at, span_table, n_q, n_z, q_order)
    whole_heads = out_weight.shape[0] == head_dim

    tables = rotary_tables(seq_len, head_dim)

    owned = [ln_gain, ln_bias, out_bias, fc2_bias, qkv_bias, fc1_bias]
    small = lax.all_gather(pack_small(owned), every, axis=0, tiled=True)

    came = scattered(to_blocks(at, qkv_weight, fc1_weight, n_q, n_t, heads, head_dim, units), "ctx")
    w2_block = jnp.concatenate([fc2_weight, out_weight], 0) if whole_heads else fc2_weight
    w2_arrays, w2_halves = ring_halves(w2_block, "q", q_order)
    w2_halves = lax.optimization_barrier(w2_halves)
    w2_arrays = w2_arrays + [
        lax.ppermute(half, "q", ring_pairs(q_order, step)) for half, step in zip(w2_halves, (1, -1))
    ]
    plan = []
    for slot, pieces in enumerate(slot_plan(n_q, w2_block.shape[0])):
        for which, first, count in pieces:
            if first < units:
                plan.append((which, 0, min(first + count, units) - first, slot, units, first))
            if first + count > units:
                begin = max(first, units)
                plan.append((which, begin - first, first + count - begin, slot, head_dim, own_units + begin - units))
    w2_sent = w2_arrays[1:]
    if not whole_heads:
        w_out = lax.all_gather(out_weight, every, axis=0, tiled=True).reshape(heads, n_t, head_dim, width)
        w2_arrays = w2_arrays + [lax.dynamic_index_in_dim(w_out, t, 1, False).reshape(own_width, width)]
        plan.append((len(w2_arrays) - 1, 0, own_width, 0, 0, own_units))
    w2 = Gathered(w2_arrays, plan, turns)

    got = swap(theirs([after(came[0], *w2_sent[:-2], turns, order)] + came[1:]))
    w1_block = stack_rows(at, came, got)
    w1_arrays = ring_gathered(w1_block, "q", q_order)
    block_rows = n_t * d_rows
    w1_plan = [
        (which, 0, count, slot, block_rows, first)
        for slot, pieces in enumerate(slot_plan(n_q, block_rows))
        for which, first, count in pieces
    ]
    w1 = Gathered(w1_arrays, w1_plan, turns)

    token_plan = slot_plan(n_z, rows) + slot_plan(n_z, rows, n_z + 1)
    x_line = ring_gathered(after(inputs, *w2_halves), "ctx", z_order)
    x_arrays = x_line + [swap(x_line[0])] + [swap(after(p, *w1_arrays[-2:])) for p in x_line[1:]]

    small = after(small, *x_line[-2:])
    small = small.reshape(n_all, 256, 128)[:, :16]
    lists, row = [], 0
    for vector in owned:
        used = -(-vector.shape[0] // 128)
        lists.append(small[:, row : row + used].reshape(n_all, used * 128)[:, : vector.shape[0]].astype(F32))
        row += used
    gain, shift, b_out, b_down = (v.reshape(1, width) for v in lists[:4])
    b_qkv = lax.dynamic_index_in_dim(lists[4].reshape(3, heads, n_t, head_dim), t, 2, False).reshape(1, split)
    b_up = lax.dynamic_index_in_dim(lists[5].reshape(n_q, n_t, units), t, 1, False).reshape(1, own_units)
    b_project = jnp.concatenate([b_qkv, b_up], 1)

    x_all, hidden, qkv, act, slope = project(x_arrays, token_plan, gain, shift, w1, b_project, split)
    att_other, kept_other = attend(order, qkv, tables, heads, head_dim, span, 1)
    out_other = combine(act, att_other, w2, 1, rows)
    g_line = ring_gathered(after(cotangent, *x_line[-2:]), "ctx", z_order, out_other)
    att_own, kept_own = attend(order, after(qkv, *out_other, *g_line[1:-2]), tables, heads, head_dim, span, 0)
    out_own = combine(act, att_own, w2, 0, rows, [swap(p) for p in out_other])
    g_arrays = g_line + [swap(p) for p in g_line[:-2]] + [swap(after(p, *out_own)) for p in g_line[-2:]]

    g_all, pre_grad, att_grad, g_sums = combine_back(g_arrays, token_plan, w2, after(slope, *out_own))
    up_own, up_sums = weight_grad(turns, hidden, [pre_grad])
    out_parts, out_sent = ring_sum(out_own, "ctx", z_order, up_own)
    up_first = ring_first(up_own, "q", q_order)
    att_grad = after(att_grad, *up_own, *out_sent).reshape(2, seq_len, own_width)
    grad_other = attend_back(order, kept_other, att_grad, tables, heads, head_dim, span, 1)
    up_parts, up_sent = ring_rest(up_own, up_first, "q", q_order, [grad_other])
    normed_other, sums_other = project_back(after(grad_other, *up_sent), pre_grad, w1, x_all, 1, rows)
    att_grad = after(att_grad, *normed_other)
    grad_own = attend_back(order, kept_own, att_grad, tables, heads, head_dim, span, 0)
    up_rows = last_sum(at, [after(up_parts[0], grad_own)] + up_parts[1:], n_t)
    up_came = scattered(up_rows, "ctx")
    normed_own, sums_own = project_back(
        after(grad_own, *out_parts[1:], *up_rows), pre_grad, w1, x_all, 0, rows, [swap(p) for p in normed_other]
    )
    vectors = pack_vectors(
        at, sums_own, sums_other, g_sums, up_sums, (n_q, n_t, heads, head_dim, units), (d_rows, qkv_bias.shape[0]), split
    )
    qkv_own, _ = weight_grad(turns, after(hidden, *normed_own), [grad_own, grad_other], vectors)
    qkv_first = ring_first(qkv_own, "q", q_order)
    normed_own = [after(p, *up_came[1:]) for p in normed_own]
    normed_first = ring_first(normed_own, "ctx", z_order)
    normed_parts, normed_sent = ring_rest(normed_own, normed_first, "ctx", z_order, qkv_own)
    qkv_parts, qkv_sent = ring_rest(qkv_own, qkv_first, "q", q_order, normed_sent, 2 * n_t)
    qkv_rows = last_sum(at, qkv_parts, n_t, 2 * n_t)
    down, out_apart = down_grad(turns, after(act, *qkv_sent), (att_own, att_other), g_all, head_dim if whole_heads else 0)
    down_parts, down_sent = ring_sum([after(p, *qkv_parts[1:]) for p in down], "q", q_order, [normed_parts[1], *qkv_rows])
    output = output_sum(inputs, b_out + b_down, [after(out_parts[0], *normed_sent, *down)] + out_parts[1:])

    qkv_came = scattered(qkv_rows, "ctx")
    if whole_heads:
        fc2_weight_grad, out_weight_grad = split_sum(down_parts, [units, head_dim])
    else:
        (fc2_weight_grad,) = split_sum(down_parts, [units])
        spread = jnp.zeros((heads, n_t, head_dim, width), F32)
        spread = lax.dynamic_update_slice(spread, out_apart.reshape(heads, 1, head_dim, width), (0, t, 0, 0))
        out_weight_grad = lax.psum_scatter(spread.reshape(width, width), every, scatter_dimension=0, tiled=True)
    input_grad = finish(normed_parts, inputs, cotangent, gain)
    up_got = swap(theirs([after(up_came[0], *normed_parts[1:], output)] + up_came[1:]))
    (fc1_weight_grad,) = from_blocks(at, up_came, up_got, n_q, units)
    qkv_got = swap(theirs([after(qkv_came[0], up_got, fc1_weight_grad, input_grad, fc2_weight_grad)] + qkv_came[1:]))
    qkv_weight_grad, total = from_blocks(at, qkv_came, qkv_got, 3 * heads, head_dim, 16)
    total = total[0]

    cuts = [ln_gain.shape[0], ln_bias.shape[0], out_bias.shape[0], qkv_bias.shape[0], fc1_bias.shape[0]]
    starts = [sum(cuts[:i]) for i in range(len(cuts))]
    gain_grad, shift_grad, bias_grad, qkv_bias_grad, fc1_bias_grad = (total[s : s + c] for s, c in zip(starts, cuts))
    return (
        output,
        input_grad,
        gain_grad,
        shift_grad,
        qkv_weight_grad,
        qkv_bias_grad,
        out_weight_grad,
        bias_grad,
        fc1_weight_grad,
        fc1_bias_grad,
        fc2_weight_grad,
        bias_grad,
    )


def solution(mesh):
    n_dp, n_ctx = mesh.devices.shape
    inner = Mesh(mesh.devices.reshape(n_dp // 2, 2, n_ctx), ("q", "core", "ctx"))
    every = ("q", "core", "ctx")
    matrix, vector = P(every, None), P(every)
    return jax.shard_map(
        per_device,
        mesh=inner,
        in_specs=(
            matrix,
            P(),
            vector,
            vector,
            matrix,
            vector,
            matrix,
            vector,
            matrix,
            vector,
            matrix,
            vector,
            matrix,
        ),
        out_specs=(matrix, matrix, vector, vector, matrix, vector, matrix, vector, matrix, vector, matrix, vector),
        check_vma=False,
    )
```

```python
from functools import partial
import math

import jax
import jax.numpy as jnp
from jax import lax
from jax.experimental import pallas as pl
from jax.experimental.pallas import tpu as pltpu
from jax.sharding import Mesh, PartitionSpec as P

HEADS = 32
ROT = 32
EPS = 1e-05
NEG = -1e30
BLOCK_Q = 256

BF = jnp.bfloat16
F32 = jnp.float32


def dot(a, b):
    return jnp.dot(a, b, preferred_element_type=F32)


def dot_t(a, b):
    return lax.dot_general(a, b, (((1,), (1,)), ((), ())), preferred_element_type=F32)


def t_dot(a, b):
    return lax.dot_general(a, b, (((0,), (0,)), ((), ())), preferred_element_type=F32)


def cost(flops, nbytes):
    return pl.CostEstimate(flops=flops // 1000, bytes_accessed=nbytes // 1000, transcendentals=0)


def across(value, axis, e):
    n = math.prod(lax.axis_size(a) for a in axis) if isinstance(axis, tuple) else lax.axis_size(axis)
    return lax.ppermute(value, axis, [(i, i ^ e) for i in range(n)])


def scattered(parts, axis):
    return [parts[0]] + [across(part, axis, e) for e, part in enumerate(parts) if e]


def ring_pairs(order, step):
    n = len(order)
    return [(order[i], order[(i + step) % n]) for i in range(n)]


def ring_offsets(n):
    return [0] + [o for s in range(1, n // 2) for o in (-s, s)] + [n // 2]


def half_of(rows):
    return rows // 32 * 16


def slot_plan(n, rows, first=0):
    plan = [((first + k, 0, rows),) for k in range(n - 1)]
    return plan + [((first + n - 1, 0, half_of(rows)), (first + n, half_of(rows), rows - half_of(rows)))]


def direct_scattered(parts, axis, order):
    return [parts[0]] + [
        lax.ppermute(part, axis, ring_pairs(order, o)) for part, o in zip(parts[1:], ring_offsets(len(order))[1:])
    ]


def ring_halves(own, axis, order):
    n = len(order)
    up_pairs, down_pairs = ring_pairs(order, 1), ring_pairs(order, -1)
    out = [own]
    up = down = own
    half = half_of(own.shape[0])
    for _ in range(1, n // 2):
        up, down = lax.ppermute(up, axis, up_pairs), lax.ppermute(down, axis, down_pairs)
        out += [up, down]
    return out, (up[:half], down[half:])


def ring_gathered(own, axis, order, hold=()):
    out, (up, down) = ring_halves(own, axis, order)
    up, down = after(up, *hold), after(down, *hold)
    return out + [lax.ppermute(up, axis, ring_pairs(order, 1)), lax.ppermute(down, axis, ring_pairs(order, -1))]


def ring_first(parts, axis, order):
    n = len(order)
    return [
        lax.ppermute(parts[n - 1], axis, ring_pairs(order, -1)),
        lax.ppermute(parts[n], axis, ring_pairs(order, 1)),
    ]


def ring_rest(parts, arrived, axis, order, hold=(), tail=0):
    n = len(order)
    low, high = arrived
    sent = ()
    for step in range(n // 2 - 1, 0, -1):
        sent = pass_on(parts[2 * step - 1], parts[2 * step], after(low, *hold), high, tail)
        low = lax.ppermute(sent[0], axis, ring_pairs(order, -1))
        high = lax.ppermute(sent[1], axis, ring_pairs(order, 1))
    return [parts[0], low, high], sent


def ring_sum(parts, axis, order, hold=()):
    return ring_rest(parts, ring_first(parts, axis, order), axis, order, hold)


def in_two(values):
    first = values.astype(BF)
    return first, (values - first.astype(F32)).astype(BF)


def add_rows(part, arrived, tail):
    total = part.astype(F32) + arrived.astype(F32)
    if not tail:
        return total.astype(BF)
    cut, half = total.shape[0] - tail, tail // 2
    values = total[cut : cut + half, :] + total[cut + half :, :]
    return jnp.concatenate([total[:cut, :].astype(BF), *in_two(values)], 0)


def pass_on_kernel(tail, low_part_ref, high_part_ref, low_ref, high_ref, to_low_ref, to_high_ref):
    rows = low_part_ref.shape[0]
    cut = low_ref.shape[0]
    if cut < rows:
        to_low_ref[0:cut, :] = add_rows(low_part_ref[0:cut, :], low_ref[...], 0)
        to_low_ref[cut:, :] = low_part_ref[cut:, :]
        to_high_ref[0:cut, :] = high_part_ref[0:cut, :]
        to_high_ref[cut:, :] = add_rows(high_part_ref[cut:, :], high_ref[...], tail)
    else:
        to_low_ref[...] = add_rows(low_part_ref[...], low_ref[...], tail)
        to_high_ref[...] = add_rows(high_part_ref[...], high_ref[...], tail)


def pass_on(low_part, high_part, low, high, tail):
    rows, columns = low_part.shape
    wide = math.gcd(columns, 1024)

    def block(array):
        return pl.BlockSpec((array.shape[0], wide), lambda i: (0, i))

    arrays = [low_part, high_part, low, high]
    return pl.pallas_call(
        partial(pass_on_kernel, tail),
        grid=(columns // wide,),
        in_specs=[block(array) for array in arrays],
        out_specs=[block(low_part)] * 2,
        out_shape=[jax.ShapeDtypeStruct((rows, columns), BF)] * 2,
        cost_estimate=cost(2 * rows * columns, 12 * rows * columns),
        name="pass_on",
    )(*arrays)


def swap(value):
    return lax.ppermute(value, "core", [(0, 1), (1, 0)])


def turn(values, cosine, sine_a, sine_b):
    width = values.shape[1]
    cosine, sine_a, sine_b = (jnp.concatenate([v] * (width // 128), 1) for v in (cosine, sine_a, sine_b))
    return (
        values * cosine
        + pltpu.roll(values, width - ROT // 2, 1) * sine_a
        + pltpu.roll(values, ROT // 2, 1) * sine_b
    )


def head_mask(shape, head, head_dim):
    lane = lax.broadcasted_iota(jnp.int32, shape, 1)
    return (lane >= head * head_dim) & (lane < (head + 1) * head_dim)


def attend_kernel(heads, head_dim, span, order_ref, qkv_ref, cos_ref, sin_a_ref, sin_b_ref, att_ref, sorted_ref, out_scr):
    seq_len = qkv_ref.shape[1]
    width = heads * head_dim
    for slot in range(seq_len // span):
        rows = pl.ds(pl.multiple_of(order_ref[slot] * span, span), span)
        here = pl.ds(slot * span, span)
        tables = (cos_ref[here, :], sin_a_ref[here, :], sin_b_ref[here, :])
        query = turn(qkv_ref[0, rows, 0:width], *tables).astype(BF)
        sorted_ref[0, here, 0:width] = (query.astype(F32) * (head_dim**-0.5)).astype(BF)
        sorted_ref[0, here, width : 2 * width] = turn(qkv_ref[0, rows, width : 2 * width], *tables).astype(BF)
        sorted_ref[0, here, 2 * width :] = qkv_ref[0, rows, 2 * width :].astype(BF)
    block = min(BLOCK_Q, seq_len)
    for i in range(seq_len // block):
        extent = (i + 1) * block
        here = pl.ds(i * block, block)
        queries = sorted_ref[0, here, 0:width]
        keys = sorted_ref[0, 0:extent, width : 2 * width]
        values = sorted_ref[0, 0:extent, 2 * width :]
        row = lax.broadcasted_iota(jnp.int32, (block, extent), 0) + i * block
        col = lax.broadcasted_iota(jnp.int32, (block, extent), 1)
        total = jnp.zeros((block, width), F32)
        for head in range(heads):
            mask = head_mask((block, width), head, head_dim)
            scores = dot_t(jnp.where(mask, queries, jnp.zeros_like(queries)), keys)
            scores = jnp.where(col <= row, scores, NEG)
            top = jnp.max(scores, 1, keepdims=True)
            weights = jnp.exp(scores - top)
            norm = 1.0 / jnp.sum(weights, 1, keepdims=True)
            probs = (weights * norm).astype(BF)
            total = jnp.where(mask, dot(probs, values), total)
        out_scr[here, :] = total.astype(BF)
    for slot in range(seq_len // span):
        rows = pl.ds(pl.multiple_of(order_ref[slot] * span, span), span)
        att_ref[0, rows, :] = out_scr[slot * span : (slot + 1) * span, :]


def attend_back_kernel(
    heads, head_dim, span, order_ref, sorted_ref, grad_ref, cos_ref, sin_a_ref, sin_b_ref, out_ref, grad_scr, key_scr, value_scr
):
    seq_len = sorted_ref.shape[1]
    width = heads * head_dim
    for slot in range(seq_len // span):
        rows = pl.ds(pl.multiple_of(order_ref[slot] * span, span), span)
        grad_scr[slot * span : (slot + 1) * span, :] = grad_ref[0, rows, :]
    key_scr[...] = jnp.zeros_like(key_scr)
    value_scr[...] = jnp.zeros_like(value_scr)
    block = min(BLOCK_Q, seq_len)

    def put(slot, first, values):
        rows = pl.ds(pl.multiple_of(order_ref[slot] * span, span), span)
        out_ref[0, rows, first : first + width] = values.astype(BF)

    def tables(here):
        return (cos_ref[here, :], -sin_a_ref[here, :], -sin_b_ref[here, :])

    for i in range(seq_len // block):
        extent = (i + 1) * block
        here = pl.ds(i * block, block)
        queries = sorted_ref[0, here, 0:width]
        grads = grad_scr[here, :]
        keys = sorted_ref[0, 0:extent, width : 2 * width]
        values = sorted_ref[0, 0:extent, 2 * width :]
        key = lax.broadcasted_iota(jnp.int32, (extent, block), 0)
        query = lax.broadcasted_iota(jnp.int32, (extent, block), 1) + i * block
        query_grad = jnp.zeros((block, width), F32)
        for head in range(heads):
            mask = head_mask((block, width), head, head_dim)
            own_queries = jnp.where(mask, queries, jnp.zeros_like(queries))
            own_grads = jnp.where(mask, grads, jnp.zeros_like(grads))
            scores = jnp.where(key <= query, dot_t(keys, own_queries), NEG)
            weights = jnp.exp(scores - jnp.max(scores, 0, keepdims=True))
            probs = weights * (1.0 / jnp.sum(weights, 0, keepdims=True))
            probs_grad = dot_t(values, own_grads)
            delta = jnp.sum(probs * probs_grad, 0, keepdims=True)
            score_grad = (probs * (probs_grad - delta)).astype(BF)
            value_scr[0:extent, :] += dot(probs.astype(BF), own_grads)
            key_scr[0:extent, :] += dot(score_grad, own_queries)
            query_grad = jnp.where(mask, t_dot(score_grad, keys), query_grad)
        query_grad = turn(query_grad * (head_dim**-0.5), *tables(here))
        for j in range(block // span):
            put(i * (block // span) + j, 0, query_grad[j * span : (j + 1) * span])
    for slot in range(seq_len // span):
        here = pl.ds(slot * span, span)
        put(slot, width, turn(key_scr[here, :], *tables(here)))
        put(slot, 2 * width, value_scr[here, :])


def attend(order, qkv, tables, heads, head_dim, span, part):
    seq_len, wide = qkv.shape[0] // 2, qkv.shape[1]
    width = wide // 3
    whole = pl.BlockSpec((seq_len, 128), lambda s, o: (0, 0))
    return pl.pallas_call(
        partial(attend_kernel, heads, head_dim, span),
        grid_spec=pltpu.PrefetchScalarGridSpec(
            num_scalar_prefetch=1,
            grid=(1,),
            in_specs=[pl.BlockSpec((1, seq_len, wide), lambda s, o: (part, 0, 0)), whole, whole, whole],
            out_specs=[
                pl.BlockSpec((1, seq_len, width), lambda s, o: (0, 0, 0)),
                pl.BlockSpec((1, seq_len, wide), lambda s, o: (0, 0, 0)),
            ],
            scratch_shapes=[pltpu.VMEM((seq_len, width), BF)],
        ),
        out_shape=[
            jax.ShapeDtypeStruct((1, seq_len, width), BF),
            jax.ShapeDtypeStruct((1, seq_len, wide), BF),
        ],
        compiler_params=pltpu.CompilerParams(vmem_limit_bytes=40 * 2**20),
        cost_estimate=cost(8 * heads * seq_len * seq_len * head_dim, 8 * seq_len * wide),
        name="attend",
    )(order, qkv.reshape(2, seq_len, wide), *tables)


def attend_back(order, kept, grads, tables, heads, head_dim, span, part):
    _, seq_len, wide = kept.shape
    width = wide // 3
    whole = pl.BlockSpec((seq_len, 128), lambda s, o: (0, 0))
    one = pl.BlockSpec((1, seq_len, wide), lambda s, o: (0, 0, 0))
    return pl.pallas_call(
        partial(attend_back_kernel, heads, head_dim, span),
        grid_spec=pltpu.PrefetchScalarGridSpec(
            num_scalar_prefetch=1,
            grid=(1,),
            in_specs=[one, pl.BlockSpec((1, seq_len, width), lambda s, o: (part, 0, 0)), whole, whole, whole],
            out_specs=one,
            scratch_shapes=[
                pltpu.VMEM((seq_len, width), BF),
                pltpu.VMEM((seq_len, width), F32),
                pltpu.VMEM((seq_len, width), F32),
            ],
        ),
        out_shape=jax.ShapeDtypeStruct((1, seq_len, wide), BF),
        compiler_params=params(40),
        cost_estimate=cost(20 * heads * seq_len * seq_len * head_dim, 6 * seq_len * wide),
        name="attend_back",
    )(order, kept, grads, *tables).reshape(seq_len, wide)


def after(value, *others):
    return lax.optimization_barrier((value,) + others)[0]


def whole_block(shape):
    return pl.BlockSpec(shape, lambda *_: (0,) * len(shape))


def params(limit):
    return pltpu.CompilerParams(vmem_limit_bytes=limit * 2**20)


ANYWHERE = pl.BlockSpec(memory_space=pl.ANY)
SCALARS = pl.BlockSpec(memory_space=pltpu.SMEM)
VMEM = pl.BlockSpec(memory_space=pltpu.VMEM)
ROWS = 256


def to_blocks_kernel(n_q, n_t, heads, head_dim, units, at_ref, qkv_ref, up_ref, *out_refs):
    n_z = n_t // 2
    width = heads * head_dim
    core, z = at_ref[0], at_ref[1]
    rows = qkv_ref.shape[0]
    low = lax.broadcasted_iota(jnp.int32, (rows, 128), 1) < head_dim
    per = 128 // head_dim
    for c in range(2):
        for s in range(n_z):
            out_ref = out_refs[s].at[pl.ds(c * rows, rows)]
            t = lax.rem(core + c, 2) * n_z + (z ^ s)
            odd = lax.rem(t, per)
            for which in range(3):
                for j in range(0, heads, per):
                    tiles = []
                    for i in range(per):
                        first = (which * heads + j + i) * n_t * head_dim + (t // per) * 128
                        tile = qkv_ref[:, pl.ds(pl.multiple_of(first, 128), 128)].astype(F32)
                        tiles.append(tile)
                    even = jnp.where(low, tiles[0], pltpu.roll(tiles[1], head_dim, 1))
                    uneven = jnp.where(low, pltpu.roll(tiles[0], head_dim, 1), tiles[1])
                    at = which * width + j * head_dim
                    out_ref[:, at : at + 128] = jnp.where(odd == 0, even, uneven).astype(BF)
            for q in range(n_q):
                at = 3 * width + q * units
                if units % 128 == 0:
                    first = pl.multiple_of((q * n_t + t) * units, 128)
                    out_ref[:, at : at + units] = up_ref[:, pl.ds(first, units)]
                else:
                    for k in range(n_t):

                        @pl.when(t == k)
                        def _(at=at, q=q, k=k):
                            first = (q * n_t + k) * units
                            out_ref[:, at : at + units] = up_ref[:, first : first + units]


def to_blocks(at, qkv, up, n_q, n_t, heads, head_dim, units):
    rows = qkv.shape[0]
    wide = 3 * heads * head_dim + n_q * units
    return pl.pallas_call(
        partial(to_blocks_kernel, n_q, n_t, heads, head_dim, units),
        in_specs=[SCALARS, VMEM, VMEM],
        out_specs=[VMEM] * (n_t // 2),
        out_shape=[jax.ShapeDtypeStruct((2 * rows, wide), BF)] * (n_t // 2),
        compiler_params=params(16),
        cost_estimate=cost(0, 4 * rows * wide * n_t),
        name="to_blocks",
    )(at, qkv, up)


def theirs_kernel(*refs):
    pieces, out_ref = refs[:-1], refs[-1]
    rows = pieces[0].shape[0] // 2
    for s, piece in enumerate(pieces):
        out_ref[s * rows : (s + 1) * rows, :] = piece[rows:, :]


def theirs(pieces):
    rows, columns = pieces[0].shape
    return pl.pallas_call(
        theirs_kernel,
        in_specs=[VMEM] * len(pieces),
        out_specs=VMEM,
        out_shape=jax.ShapeDtypeStruct((len(pieces) * rows // 2, columns), BF),
        compiler_params=params(16),
        cost_estimate=cost(0, 2 * len(pieces) * rows * columns),
        name="theirs",
    )(*pieces)


def piece_rows(came_refs, got_ref, at_ref):
    n_z = len(came_refs)
    rows = came_refs[0].shape[0] // 2
    core, z = at_ref[0], at_ref[1]
    for s in range(n_z):
        yield core * n_z + (z ^ s), came_refs[s][0:rows, :]
        yield (1 - core) * n_z + (z ^ s), got_ref[s * rows : (s + 1) * rows, :]


def stack_rows_kernel(at_ref, *refs):
    out_ref = refs[-1]
    for block, values in piece_rows(refs[:-2], refs[-2], at_ref):
        rows = values.shape[0]
        out_ref[pl.ds(pl.multiple_of(block * rows, 16), rows), :] = values


def stack_rows(at, came, got):
    rows, columns = came[0].shape
    return pl.pallas_call(
        stack_rows_kernel,
        in_specs=[SCALARS] + [VMEM] * (len(came) + 1),
        out_specs=VMEM,
        out_shape=jax.ShapeDtypeStruct((len(came) * rows, columns), BF),
        compiler_params=params(16),
        cost_estimate=cost(0, 4 * len(came) * rows * columns),
        name="stack_rows",
    )(at, *came, got)


def last_sum_kernel(n_z, n_parts, tail, at_ref, *refs):
    part_refs, out_refs = refs[:n_parts], refs[n_parts:]
    n_t = 2 * n_z
    below = 16 if tail else 0
    count = part_refs[0].shape[0] - tail
    rows = count // n_t
    core, z = at_ref[0], at_ref[1]
    if tail:
        total = part_refs[0][count:, :].astype(F32)
        for part_ref in part_refs[1:]:
            total = total + part_ref[count:, :].astype(F32)
        values = total[: tail // 2, :] + total[tail // 2 :, :]
        index = lax.broadcasted_iota(jnp.int32, values.shape, 0)
    for c in range(2):
        for s in range(n_z):
            block = lax.rem(core + c, 2) * n_z + (z ^ s)
            here = pl.ds(pl.multiple_of(block * rows, 16), rows)
            total = part_refs[0][here, :].astype(F32)
            for part_ref in part_refs[1:]:
                total = total + part_ref[here, :].astype(F32)
            first = c * (rows + below)
            out_refs[s][first : first + rows, :] = total.astype(BF)
            if tail:
                own = jnp.sum(jnp.where(index == block, values, 0.0), 0, keepdims=True)
                high, low = in_two(own)
                row = lax.broadcasted_iota(jnp.int32, (below, own.shape[1]), 0)
                both = jnp.where(row == 0, high.astype(F32), jnp.where(row == 1, low.astype(F32), 0.0))
                out_refs[s][first + rows : first + rows + below, :] = both.astype(BF)


def last_sum(at, parts, n_t, tail=0):
    columns = parts[0].shape[1]
    rows = 2 * ((parts[0].shape[0] - tail) // n_t + (16 if tail else 0))
    return pl.pallas_call(
        partial(last_sum_kernel, n_t // 2, len(parts), tail),
        in_specs=[SCALARS] + [VMEM] * len(parts),
        out_specs=[VMEM] * (n_t // 2),
        out_shape=[jax.ShapeDtypeStruct((rows, columns), BF)] * (n_t // 2),
        compiler_params=params(24),
        cost_estimate=cost(0, 8 * rows * n_t * columns),
        name="last_sum",
    )(at, *parts)


def from_blocks_kernel(groups, piece, below, at_ref, *refs):
    came_refs, got_ref, refs = refs[: -3 - (below > 0)], refs[-3 - (below > 0)], refs[-2 - (below > 0) :]
    out_ref, held_ref = refs[0], refs[-1]
    n_t = held_ref.shape[0]
    rows = out_ref.shape[0]
    total = 0.0
    for block, values in piece_rows(came_refs, got_ref, at_ref):
        held_ref[block] = values[0:rows, :]
        if below:
            under = values[rows:, :].astype(F32)
            total = total + under[0:1, :] + under[1:2, :]
    for t in range(n_t):
        for j in range(groups):
            first = (j * n_t + t) * piece
            out_ref[:, first : first + piece] = held_ref[t, :, j * piece : (j + 1) * piece].astype(F32)
    if below:
        refs[1][...] = jnp.broadcast_to(total, refs[1].shape)


def from_blocks(at, came, got, groups, piece, below=0):
    n_t = 2 * len(came)
    rows = came[0].shape[0] // 2 - below
    columns = groups * piece
    return pl.pallas_call(
        partial(from_blocks_kernel, groups, piece, below),
        in_specs=[SCALARS] + [VMEM] * (len(came) + 1),
        out_specs=[VMEM] * (1 + (below > 0)),
        out_shape=[jax.ShapeDtypeStruct((rows, columns * n_t), F32)]
        + [jax.ShapeDtypeStruct((8, columns), F32)] * (below > 0),
        scratch_shapes=[pltpu.VMEM((n_t, rows, columns), BF)],
        compiler_params=params(16),
        cost_estimate=cost(0, 8 * rows * columns * n_t),
        name="from_blocks",
    )(at, *came, got)


def places_kernel(n_q, n_z, q_order, at_ref, table_ref, turns_ref, order_ref):
    q, z = at_ref[2], at_ref[1]
    place = 0
    for i, index in enumerate(q_order):
        place = place + jnp.where(q == index, i, 0)
    for k, offset in enumerate(ring_offsets(n_q)):
        at = lax.rem(place + offset + n_q, n_q)
        turn_of = 0
        for i, index in enumerate(q_order):
            turn_of = turn_of + jnp.where(at == i, index, 0)
        turns_ref[k] = turn_of
    for k, offset in enumerate(ring_offsets(n_z)):
        row = lax.rem(z + offset + n_z, n_z)
        for j in range(2):
            order_ref[table_ref[row, j]] = 2 * k + j


def find_places(at, span_table, n_q, n_z, q_order):
    return pl.pallas_call(
        partial(places_kernel, n_q, n_z, q_order),
        in_specs=[SCALARS, SCALARS],
        out_specs=[SCALARS, SCALARS],
        out_shape=[jax.ShapeDtypeStruct((n_q,), jnp.int32), jax.ShapeDtypeStruct((2 * n_z,), jnp.int32)],
        cost_estimate=cost(0, 1000),
        name="places",
    )(at, span_table)


def pack_small_kernel(*refs):
    out_ref = refs[-1]
    row = 0
    for ref in refs[:-1]:
        size = ref.shape[1]
        for first in range(0, size, 128):
            count = min(128, size - first)
            out_ref[row : row + 1, 0:count] = ref[:, first : first + count].astype(F32).astype(BF)
            row += 1


def pack_small(vectors):
    return pl.pallas_call(
        pack_small_kernel,
        in_specs=[VMEM] * len(vectors),
        out_specs=VMEM,
        out_shape=jax.ShapeDtypeStruct((256, 128), BF),
        cost_estimate=cost(0, 65536),
        name="pack_small",
    )(*[v.reshape(1, -1) for v in vectors])


def pack_vectors_kernel(shape, widths, at_ref, norm_a_ref, norm_b_ref, g_ref, up_ref, out_ref):
    n_q, n_t, heads, head_dim, units = shape
    part, biases = widths
    t_here = at_ref[0] * (n_t // 2) + at_ref[1]
    gain = norm_a_ref[0:1, :] + norm_b_ref[0:1, :]
    shift = norm_a_ref[1:2, :] + norm_b_ref[1:2, :]
    qkv = norm_a_ref[2:3, :] + norm_b_ref[2:3, :]
    g = g_ref[0:1, :]
    up = up_ref[0:1, :]
    columns = out_ref.shape[2]
    for q in range(n_q):
        lines = []
        for t in range(n_t):
            owner = q * n_t + t
            here = slice(owner * part, (owner + 1) * part)
            cells = [gain[:, here], shift[:, here], g[:, here]]
            first, end = owner * biases, (owner + 1) * biases
            while first < end:
                which, head = first // (HEADS * head_dim), first // head_dim % HEADS
                stop = min(end, (first // head_dim + 1) * head_dim)
                source = (which * heads + head // n_t) * head_dim + first % head_dim
                cells.append(jnp.where(t_here == head % n_t, qkv[:, source : source + stop - first], 0.0))
                first = stop
            cells.append(jnp.where(t_here == t, up[:, q * units : (q + 1) * units], 0.0))
            used = 3 * part + biases + units
            cells.append(jnp.zeros((1, columns - used), F32))
            lines.append(jnp.concatenate(cells, 1))
        high, low = in_two(jnp.concatenate(lines, 0))
        out_ref[q, 0:n_t, :] = high
        out_ref[q, n_t:, :] = low


def pack_vectors(at, norm_a, norm_b, g, up, shape, widths, columns):
    n_q, n_t = shape[:2]
    return pl.pallas_call(
        partial(pack_vectors_kernel, shape, widths),
        in_specs=[SCALARS] + [VMEM] * 4,
        out_specs=VMEM,
        out_shape=jax.ShapeDtypeStruct((n_q, 2 * n_t, columns), BF),
        cost_estimate=cost(0, 4 * n_q * n_t * columns),
        name="pack_vectors",
    )(at, norm_a, norm_b, g, up)


def load_pieces(plan, turns_ref, piece_refs, target, sem):
    copies = []
    for i, (piece, first, rows, slot, scale, base) in enumerate(plan):
        start = pl.multiple_of(turns_ref[slot] * scale + base, 16)
        copies.append(pltpu.make_async_copy(piece_refs[piece].at[pl.ds(first, rows)], target.at[pl.ds(start, rows)], sem.at[i]))
    return copies


def fetch_slots(plan, slot_refs, buffers, sems):
    i = pl.program_id(0)

    def copies(k):
        return [
            pltpu.make_async_copy(slot_refs[which], buffers.at[k % 2, pl.ds(first, rows)], sems.at[k % 2, part])
            for part, (which, first, rows) in enumerate(plan[k])
        ]

    for k in range(len(plan)):

        @pl.when(i == k)
        def _(k=k):
            for copy in (copies(0) if k == 0 else []) + (copies(k + 1) if k + 1 < len(plan) else []):
                copy.start()
            for copy in copies(k):
                copy.wait()


class Gathered:
    def __init__(self, arrays, plan, turns):
        self.arrays = arrays
        self.plan = tuple(plan)
        self.starts = turns
        self.rows = sum(piece[2] for piece in plan)
        self.columns = arrays[0].shape[1]

    def scratch(self):
        return [pltpu.VMEM((self.rows, self.columns), BF), pltpu.SemaphoreType.DMA((len(self.plan),))]

    def specs(self):
        return [ANYWHERE] * len(self.arrays)


def put_block(plan, block, held_ref, out_refs, sem):
    i = pl.program_id(0)
    held_ref[i] = block

    def copies(k):
        return [
            pltpu.make_async_copy(held_ref.at[k, pl.ds(first, rows)], out_refs[which], sem.at[which])
            for which, first, rows in plan[k]
        ]

    for k in range(len(plan)):

        @pl.when(i == k)
        def _(k=k):
            for copy in copies(k):
                copy.start()

    @pl.when(i == len(plan) - 1)
    def _():
        for k in range(len(plan)):
            for copy in copies(k):
                copy.wait()


def normed(rows):
    mean = jnp.mean(rows, -1, keepdims=True)
    centred = rows - mean
    scale = lax.rsqrt(jnp.mean(centred * centred, -1, keepdims=True) + EPS)
    return centred * scale, scale


def project_kernel(split, x_plan, n_x, w_plan, n_w, starts_ref, *refs):
    x_refs, refs = refs[:n_x], refs[n_x:]
    w_refs, refs = refs[:n_w], refs[n_w:]
    gain_ref, shift_ref, b_ref, x_out_ref, hidden_ref, qkv_ref, act_ref, slope_ref, w_ref, w_sem, x_buf, x_sem = refs

    @pl.when(pl.program_id(0) == 0)
    def _():
        for copy in load_pieces(w_plan, starts_ref, w_refs, w_ref, w_sem):
            copy.start()

    fetch_slots(x_plan, x_refs, x_buf, x_sem)
    x = x_buf[lax.rem(pl.program_id(0), 2)]
    x_out_ref[...] = x
    xhat, _ = normed(x.astype(F32))
    hidden = (xhat * gain_ref[...] + shift_ref[...]).astype(BF)
    hidden_ref[...] = hidden

    @pl.when(pl.program_id(0) == 0)
    def _():
        for copy in load_pieces(w_plan, starts_ref, w_refs, w_ref, w_sem):
            copy.wait()

    pre = dot(hidden, w_ref[:, split:]) + b_ref[:, split:]
    root = math.sqrt(2.0 / math.pi)
    square = pre * pre
    turned = jnp.tanh(root * pre * (1.0 + 0.044715 * square))
    act_ref[...] = (0.5 * pre * (1.0 + turned)).astype(BF)
    slope = 0.5 * (1.0 + turned) + 0.5 * pre * (1.0 - turned * turned) * (root * (1.0 + 3 * 0.044715 * square))
    slope_ref[...] = slope.astype(BF)
    qkv_ref[...] = dot(hidden, w_ref[:, :split]) + b_ref[:, :split]


def project(x_arrays, x_plan, gain, shift, w, b, split):
    rows, width = x_arrays[0].shape
    count = rows * len(x_plan)
    wide = w.columns

    def block(columns):
        return pl.BlockSpec((rows, columns), lambda i, s: (i, 0))

    return pl.pallas_call(
        partial(project_kernel, split, x_plan, len(x_arrays), w.plan, len(w.arrays)),
        grid_spec=pltpu.PrefetchScalarGridSpec(
            num_scalar_prefetch=1,
            grid=(len(x_plan),),
            in_specs=[ANYWHERE] * len(x_arrays) + w.specs() + [whole_block((1, width))] * 2 + [whole_block(b.shape)],
            out_specs=[block(width), block(width), block(split), block(wide - split), block(wide - split)],
            scratch_shapes=w.scratch() + [pltpu.VMEM((2, rows, width), BF), pltpu.SemaphoreType.DMA((2, 2))],
        ),
        out_shape=[
            jax.ShapeDtypeStruct((count, width), BF),
            jax.ShapeDtypeStruct((count, width), BF),
            jax.ShapeDtypeStruct((count, split), F32),
            jax.ShapeDtypeStruct((count, wide - split), BF),
            jax.ShapeDtypeStruct((count, wide - split), BF),
        ],
        compiler_params=params(58),
        cost_estimate=cost(2 * count * width * wide, 8 * count * width + 2 * width * wide),
        name="project",
    )(w.starts, *x_arrays, *w.arrays, gain, shift, b)


def combine_kernel(split, w_plan, n_w, plan, n_arrived, starts_ref, act_ref, att_ref, *refs):
    w_refs, refs = refs[:n_w], refs[n_w:]
    arrived_refs, refs = refs[:n_arrived], refs[n_arrived:]
    out_refs, (w_ref, w_sem, held, held_sem, buf, buf_sem) = refs[:-6], refs[-6:]

    @pl.when(pl.program_id(0) == 0)
    def _():
        copies = load_pieces(w_plan, starts_ref, w_refs, w_ref, w_sem)
        for copy in copies:
            copy.start()
        for copy in copies:
            copy.wait()

    total = dot(act_ref[...], w_ref[:split, :]) + dot(att_ref[...], w_ref[split:, :])
    if n_arrived:
        fetch_slots([((k, 0, total.shape[0]),) for k in range(n_arrived)], arrived_refs, buf, buf_sem)
        total = total + buf[lax.rem(pl.program_id(0), 2)].astype(F32)
    put_block(plan, total.astype(BF), held, out_refs, held_sem)


def held_blocks(steps, rows, width):
    return [pltpu.VMEM((steps, rows, width), BF), pltpu.SemaphoreType.DMA((steps + 1,))]


def combine(act, att, w, part, rows, arrived=()):
    count, split = act.shape[0] // 2, act.shape[1]
    own_width = att.shape[-1]
    att = att.reshape(count, own_width)
    width = w.columns
    steps = count // rows
    base = part * steps
    plan = slot_plan(steps, rows) if arrived else [((k, 0, rows),) for k in range(steps)]
    shapes = [jax.ShapeDtypeStruct((r, width), BF) for slot in plan for _, _, r in slot]
    return pl.pallas_call(
        partial(combine_kernel, split, w.plan, len(w.arrays), plan, len(arrived)),
        grid_spec=pltpu.PrefetchScalarGridSpec(
            num_scalar_prefetch=1,
            grid=(steps,),
            in_specs=[
                pl.BlockSpec((rows, split), lambda i, s: (i + base, 0)),
                pl.BlockSpec((rows, own_width), lambda i, s: (i, 0)),
            ]
            + w.specs()
            + [ANYWHERE] * len(arrived),
            out_specs=[ANYWHERE] * len(shapes),
            scratch_shapes=w.scratch()
            + held_blocks(steps, rows, width)
            + [pltpu.VMEM((2, rows, width), BF), pltpu.SemaphoreType.DMA((2, 2))],
        ),
        out_shape=shapes,
        compiler_params=params(32),
        cost_estimate=cost(2 * count * width * w.rows, 4 * count * width + 2 * width * w.rows),
        name="combine",
    )(w.starts, act, att, *w.arrays, *arrived)


def combine_back_kernel(split, g_plan, n_g, w_plan, n_w, starts_ref, *refs):
    g_refs, refs = refs[:n_g], refs[n_g:]
    w_refs, refs = refs[:n_w], refs[n_w:]
    slope_ref, g_out_ref, pre_grad_ref, att_grad_ref, sums_ref, w_ref, w_sem, g_buf, g_sem = refs

    @pl.when(pl.program_id(0) == 0)
    def _():
        for copy in load_pieces(w_plan, starts_ref, w_refs, w_ref, w_sem):
            copy.start()

    fetch_slots(g_plan, g_refs, g_buf, g_sem)

    @pl.when(pl.program_id(0) == 0)
    def _():
        for copy in load_pieces(w_plan, starts_ref, w_refs, w_ref, w_sem):
            copy.wait()

    grad = g_buf[lax.rem(pl.program_id(0), 2)]
    g_out_ref[...] = grad

    @pl.when(pl.program_id(0) == 0)
    def _():
        sums_ref[...] = jnp.zeros_like(sums_ref)
        sums_ref[0:1, :] = jnp.sum(grad.astype(F32), 0, keepdims=True)

    pre_grad_ref[...] = (dot_t(grad, w_ref[:split, :]) * slope_ref[...].astype(F32)).astype(BF)
    att_grad_ref[...] = dot_t(grad, w_ref[split:, :]).astype(BF)


def combine_back(g_arrays, g_plan, w, slope):
    rows, width = g_arrays[0].shape
    count = rows * len(g_plan)
    split = slope.shape[1]
    rest = w.rows - split

    def block(columns):
        return pl.BlockSpec((rows, columns), lambda i, s: (i, 0))

    return pl.pallas_call(
        partial(combine_back_kernel, split, g_plan, len(g_arrays), w.plan, len(w.arrays)),
        grid_spec=pltpu.PrefetchScalarGridSpec(
            num_scalar_prefetch=1,
            grid=(len(g_plan),),
            in_specs=[ANYWHERE] * len(g_arrays) + w.specs() + [block(split)],
            out_specs=[block(width), block(split), block(rest), whole_block((8, width))],
            scratch_shapes=w.scratch() + [pltpu.VMEM((2, rows, width), BF), pltpu.SemaphoreType.DMA((2, 2))],
        ),
        out_shape=[
            jax.ShapeDtypeStruct((count, width), BF),
            jax.ShapeDtypeStruct((count, split), BF),
            jax.ShapeDtypeStruct((count, rest), BF),
            jax.ShapeDtypeStruct((8, width), F32),
        ],
        compiler_params=params(58),
        cost_estimate=cost(2 * count * width * w.rows, 6 * count * width + 2 * width * w.rows),
        name="combine_back",
    )(w.starts, *g_arrays, *w.arrays, slope)


def project_back_kernel(split, w_plan, n_w, plan, n_arrived, starts_ref, qkv_grad_ref, pre_grad_ref, x_ref, *refs):
    w_refs, refs = refs[:n_w], refs[n_w:]
    arrived_refs, refs = refs[:n_arrived], refs[n_arrived:]
    out_refs, (sums_ref, w_ref, w_sem, held, held_sem, buf, buf_sem) = refs[:-7], refs[-7:]

    @pl.when(pl.program_id(0) == 0)
    def _():
        copies = load_pieces(w_plan, starts_ref, w_refs, w_ref, w_sem)
        for copy in copies:
            copy.start()
        sums_ref[...] = jnp.zeros_like(sums_ref)
        for copy in copies:
            copy.wait()

    grad = dot_t(qkv_grad_ref[...], w_ref[:, :split]) + dot_t(pre_grad_ref[...], w_ref[:, split:])
    xhat, _ = normed(x_ref[...].astype(F32))
    sums_ref[0:1, :] += jnp.sum(grad * xhat, 0, keepdims=True)
    sums_ref[1:2, :] += jnp.sum(grad, 0, keepdims=True)
    sums_ref[2:3, 0:split] += jnp.sum(qkv_grad_ref[...].astype(F32), 0, keepdims=True)
    if n_arrived:
        fetch_slots([((k, 0, grad.shape[0]),) for k in range(n_arrived)], arrived_refs, buf, buf_sem)
        grad = grad + buf[lax.rem(pl.program_id(0), 2)].astype(F32)
    put_block(plan, grad.astype(BF), held, out_refs, held_sem)


def project_back(qkv_grad, pre_grad, w, x, part, rows, arrived=()):
    count, split = qkv_grad.shape
    width = x.shape[1]
    steps = count // rows
    base = part * steps
    plan = slot_plan(steps, rows) if arrived else [((k, 0, rows),) for k in range(steps)]
    shapes = [jax.ShapeDtypeStruct((r, width), BF) for slot in plan for _, _, r in slot]

    def block(columns):
        return pl.BlockSpec((rows, columns), lambda i, s: (i + base, 0))

    *out, sums = pl.pallas_call(
        partial(project_back_kernel, split, w.plan, len(w.arrays), plan, len(arrived)),
        grid_spec=pltpu.PrefetchScalarGridSpec(
            num_scalar_prefetch=1,
            grid=(steps,),
            in_specs=[pl.BlockSpec((rows, split), lambda i, s: (i, 0)), block(pre_grad.shape[1]), block(width)] + w.specs() + [ANYWHERE] * len(arrived),
            out_specs=[ANYWHERE] * len(shapes) + [whole_block((8, width))],
            scratch_shapes=w.scratch()
            + held_blocks(steps, rows, width)
            + [pltpu.VMEM((2, rows, width), BF), pltpu.SemaphoreType.DMA((2, 2))],
        ),
        out_shape=shapes + [jax.ShapeDtypeStruct((8, width), F32)],
        compiler_params=params(58),
        cost_estimate=cost(2 * count * width * w.columns, 6 * count * width + 2 * width * w.columns),
        name="project_back",
    )(w.starts, qkv_grad, pre_grad, x, *w.arrays, *arrived)
    return out, sums


def weight_grad_kernel(n_right, with_tail, turns_ref, left_ref, *refs):
    right_refs, refs = refs[:n_right], refs[n_right:]
    tail_refs, refs = refs[:with_tail], refs[with_tail:]
    out_refs, (sums_ref, held, sem) = refs[:-3], refs[-3:]

    @pl.when(pl.program_id(0) == 0)
    def _():
        sums_ref[...] = jnp.zeros_like(sums_ref)
        sums_ref[0:1, :] = sum(jnp.sum(right_ref[...].astype(F32), 0, keepdims=True) for right_ref in right_refs)

    count = right_refs[0].shape[0]
    total = t_dot(left_ref[0:count, :], right_refs[0][...])
    for k in range(1, n_right):
        total = total + t_dot(left_ref[k * count : (k + 1) * count, :], right_refs[k][...])
    block = total.astype(BF)
    if with_tail:
        block = jnp.concatenate([block, tail_refs[0][0]], 0)
    if with_tail:
        plan = [((k, 0, held.shape[1]),) for k in range(held.shape[0])]
    else:
        plan = slot_plan(held.shape[0], held.shape[1])
    put_block(plan, block, held, out_refs, sem)


def slot_shapes(n, rows, columns):
    return [jax.ShapeDtypeStruct((r, columns), BF) for slot in slot_plan(n, rows) for _, _, r in slot]


def weight_grad(turns, left, rights, tail=None):
    n_q = turns.shape[0]
    count, wide = left.shape
    columns = rights[0].shape[1]
    part = wide // n_q
    rows = part + (0 if tail is None else tail.shape[1])
    extra = [] if tail is None else [tail]
    shapes = slot_shapes(n_q, rows, columns) if tail is None else [jax.ShapeDtypeStruct((rows, columns), BF)] * n_q
    *out, sums = pl.pallas_call(
        partial(weight_grad_kernel, len(rights), len(extra)),
        grid_spec=pltpu.PrefetchScalarGridSpec(
            num_scalar_prefetch=1,
            grid=(n_q,),
            in_specs=[pl.BlockSpec((count, part), lambda k, s: (0, s[k]))]
            + [whole_block(right.shape) for right in rights]
            + [pl.BlockSpec((1,) + v.shape[1:], lambda k, s: (s[k], 0, 0)) for v in extra],
            out_specs=[ANYWHERE] * len(shapes) + [whole_block((8, columns))],
            scratch_shapes=held_blocks(n_q, rows, columns),
        ),
        out_shape=shapes + [jax.ShapeDtypeStruct((8, columns), F32)],
        compiler_params=params(58),
        cost_estimate=cost(2 * count * wide * columns, 2 * count * (wide + columns) + 2 * wide * columns),
        name="weight_grad",
    )(turns, left, *rights, *extra)
    return out, sums


def down_grad_kernel(head_rows, turns_ref, act_ref, att_a_ref, att_b_ref, g_ref, *refs):
    out_refs, (heads_ref, held, sem) = refs[:-3], refs[-3:]
    units = act_ref.shape[1]
    k = pl.program_id(0)

    @pl.when(k == 0)
    def _():
        half = att_a_ref.shape[0]
        heads_ref[...] = (t_dot(att_a_ref[...], g_ref[0:half, :]) + t_dot(att_b_ref[...], g_ref[half:, :])).astype(BF)

    rows = pl.ds(pl.multiple_of(turns_ref[k] * head_rows, head_rows), head_rows)
    block = jnp.concatenate([t_dot(act_ref[...], g_ref[...]).astype(BF), heads_ref[rows, :]], 0)
    put_block(slot_plan(held.shape[0], held.shape[1]), block, held, out_refs, sem)


def down_grad(turns, act, att, g, head_rows):
    n_q = turns.shape[0]
    count, wide = act.shape
    own_width = att[0].shape[-1]
    att = [a.reshape(count // 2, own_width) for a in att]
    width = g.shape[1]
    units = wide // n_q
    if not head_rows:
        whole = t_dot(act, g).astype(BF).reshape(n_q, units, width)[turns]
        blocks = [whole[k][first : first + r] for k, slot in enumerate(slot_plan(n_q, units)) for _, first, r in slot]
        return blocks, t_dot(jnp.concatenate(att, 0), g)
    out = pl.pallas_call(
        partial(down_grad_kernel, head_rows),
        grid_spec=pltpu.PrefetchScalarGridSpec(
            num_scalar_prefetch=1,
            grid=(n_q,),
            in_specs=[pl.BlockSpec((count, units), lambda k, s: (0, s[k]))] + [whole_block(v.shape) for v in (*att, g)],
            out_specs=[ANYWHERE] * (n_q + 1),
            scratch_shapes=[pltpu.VMEM((own_width, width), BF)] + held_blocks(n_q, units + head_rows, width),
        ),
        out_shape=slot_shapes(n_q, units + head_rows, width),
        compiler_params=params(58),
        cost_estimate=cost(2 * count * (wide + own_width) * width, 2 * count * (wide + width) + 2 * wide * width),
        name="down_grad",
    )(turns, act, *att, g)
    return list(out), None


def finish_kernel(x_ref, g_ref, gain_ref, *refs):
    part_refs, out_ref = refs[:-1], refs[-1]
    grad = part_refs[0][...].astype(F32)
    for part_ref in part_refs[1:]:
        grad = grad + part_ref[...].astype(F32)
    xhat, scale = normed(x_ref[...].astype(F32))
    m = grad * gain_ref[...]
    x_grad = (m - jnp.mean(m, -1, keepdims=True) - xhat * jnp.mean(m * xhat, -1, keepdims=True)) * scale
    out_ref[...] = (g_ref[...].astype(F32) + x_grad).astype(BF)


def finish(parts, x, g, gain):
    count, width = x.shape
    rows = math.gcd(count, 128)
    block = pl.BlockSpec((rows, width), lambda i: (i, 0))
    return pl.pallas_call(
        finish_kernel,
        grid=(count // rows,),
        in_specs=[block] * 2 + [whole_block((1, width))] + [block] * len(parts),
        out_specs=block,
        out_shape=jax.ShapeDtypeStruct((count, width), BF),
        cost_estimate=cost(20 * count * width, 12 * count * width),
        name="finish",
    )(x, g, gain, *parts)


def output_kernel(x_ref, bias_ref, *refs):
    part_refs, out_ref = refs[:-1], refs[-1]
    total = x_ref[...].astype(F32) + bias_ref[...]
    for part_ref in part_refs:
        total = total + part_ref[...].astype(F32)
    out_ref[...] = total.astype(BF)


def output_sum(x, bias, parts):
    count, width = x.shape
    rows = math.gcd(count, 128)
    block = pl.BlockSpec((rows, width), lambda i: (i, 0))
    return pl.pallas_call(
        output_kernel,
        grid=(count // rows,),
        in_specs=[block, whole_block((1, width))] + [block] * len(parts),
        out_specs=block,
        out_shape=jax.ShapeDtypeStruct((count, width), BF),
        cost_estimate=cost(4 * count * width, 10 * count * width),
        name="output_sum",
    )(x, bias, *parts)


def split_sum(parts, cuts):
    count, width = parts[0].shape
    wide = math.gcd(width, 1024)
    ends = [sum(cuts[: i + 1]) for i in range(len(cuts))]

    def kernel(*refs):
        part_refs, out_refs = refs[: len(parts)], refs[len(parts) :]
        total = part_refs[0][...].astype(F32)
        for part_ref in part_refs[1:]:
            total = total + part_ref[...].astype(F32)
        for end, rows, out_ref in zip(ends, cuts, out_refs):
            out_ref[...] = total[end - rows : end, :]

    return pl.pallas_call(
        kernel,
        grid=(width // wide,),
        in_specs=[pl.BlockSpec((count, wide), lambda i: (0, i))] * len(parts),
        out_specs=[pl.BlockSpec((rows, wide), lambda i: (0, i)) for rows in cuts],
        out_shape=[jax.ShapeDtypeStruct((rows, width), F32) for rows in cuts],
        cost_estimate=cost(4 * count * width, 12 * count * width),
        name="split_sum",
    )(*parts)


def tables_kernel(head_dim, cos_ref, sin_a_ref, sin_b_ref):
    rows = cos_ref.shape[0]
    half = ROT // 2
    lane = lax.broadcasted_iota(jnp.int32, (1, 128), 1) % head_dim
    step = (lane % half).astype(F32) * (-2.0 * math.log(10000.0) / ROT)
    freqs = jnp.where(lane < ROT, jnp.exp(step), 0.0)
    position = lax.broadcasted_iota(jnp.int32, (rows, 128), 0) + pl.program_id(0) * rows
    angles = position.astype(F32) * freqs
    cosine, sine = jnp.cos(angles), jnp.sin(angles)
    cos_ref[...] = cosine
    sin_a_ref[...] = jnp.where(lane < half, -sine, 0.0)
    sin_b_ref[...] = jnp.where((lane >= half) & (lane < ROT), sine, 0.0)


def rotary_tables(seq_len, head_dim):
    width = 128
    block = pl.BlockSpec((128, width), lambda i: (i, 0))
    return pl.pallas_call(
        partial(tables_kernel, head_dim),
        grid=(seq_len // 128,),
        out_specs=[block] * 3,
        out_shape=[jax.ShapeDtypeStruct((seq_len, width), F32)] * 3,
        cost_estimate=cost(100 * seq_len * width, 12 * seq_len * width),
        name="rotary_tables",
    )()


def per_device(
    inputs,
    span_table,
    ln_gain,
    ln_bias,
    qkv_weight,
    qkv_bias,
    out_weight,
    out_bias,
    fc1_weight,
    fc1_bias,
    fc2_weight,
    fc2_bias,
    cotangent,
):
    rows, width = inputs.shape
    head_dim = width // HEADS
    n_q, n_z = lax.axis_size("q"), lax.axis_size("ctx")
    n_t = 2 * n_z
    n_all = n_q * n_t
    q, core, z = lax.axis_index("q"), lax.axis_index("core"), lax.axis_index("ctx")
    t = core * n_z + z
    at = jnp.stack([core, z, q]).astype(jnp.int32)
    span = rows // 2
    seq_len = rows * n_z
    heads = HEADS // n_t
    own_width = heads * head_dim
    split = 3 * own_width
    units = fc2_weight.shape[0]
    own_units = units * n_q
    d_rows = qkv_weight.shape[0]
    every = ("q", "core", "ctx")
    z_order = list(range(n_z))
    q_order = [0, 1, 3, 2] if n_q == 4 else list(range(n_q))
    turns, order = find_places(at, span_table, n_q, n_z, q_order)
    whole_heads = out_weight.shape[0] == head_dim

    tables = rotary_tables(seq_len, head_dim)

    owned = [ln_gain, ln_bias, out_bias, fc2_bias, qkv_bias, fc1_bias]
    small = lax.all_gather(pack_small(owned), every, axis=0, tiled=True)

    came = scattered(to_blocks(at, qkv_weight, fc1_weight, n_q, n_t, heads, head_dim, units), "ctx")
    w2_block = jnp.concatenate([fc2_weight, out_weight], 0) if whole_heads else fc2_weight
    w2_arrays, w2_halves = ring_halves(w2_block, "q", q_order)
    w2_halves = lax.optimization_barrier(w2_halves)
    w2_arrays = w2_arrays + [
        lax.ppermute(half, "q", ring_pairs(q_order, step)) for half, step in zip(w2_halves, (1, -1))
    ]
    plan = []
    for slot, pieces in enumerate(slot_plan(n_q, w2_block.shape[0])):
        for which, first, count in pieces:
            if first < units:
                plan.append((which, 0, min(first + count, units) - first, slot, units, first))
            if first + count > units:
                begin = max(first, units)
                plan.append((which, begin - first, first + count - begin, slot, head_dim, own_units + begin - units))
    w2_sent = w2_arrays[1:]
    if not whole_heads:
        w_out = lax.all_gather(out_weight, every, axis=0, tiled=True).reshape(heads, n_t, head_dim, width)
        w2_arrays = w2_arrays + [lax.dynamic_index_in_dim(w_out, t, 1, False).reshape(own_width, width)]
        plan.append((len(w2_arrays) - 1, 0, own_width, 0, 0, own_units))
    w2 = Gathered(w2_arrays, plan, turns)

    got = swap(theirs([after(came[0], *w2_sent[:-2], turns, order)] + came[1:]))
    w1_block = stack_rows(at, came, got)
    w1_arrays = ring_gathered(w1_block, "q", q_order)
    block_rows = n_t * d_rows
    w1_plan = [
        (which, 0, count, slot, block_rows, first)
        for slot, pieces in enumerate(slot_plan(n_q, block_rows))
        for which, first, count in pieces
    ]
    w1 = Gathered(w1_arrays, w1_plan, turns)

    token_plan = slot_plan(n_z, rows) + slot_plan(n_z, rows, n_z + 1)
    x_line = ring_gathered(after(inputs, *w2_halves), "ctx", z_order)
    x_arrays = x_line + [swap(x_line[0])] + [swap(after(p, *w1_arrays[-2:])) for p in x_line[1:]]

    small = after(small, *x_line[-2:])
    small = small.reshape(n_all, 256, 128)[:, :16]
    lists, row = [], 0
    for vector in owned:
        used = -(-vector.shape[0] // 128)
        lists.append(small[:, row : row + used].reshape(n_all, used * 128)[:, : vector.shape[0]].astype(F32))
        row += used
    gain, shift, b_out, b_down = (v.reshape(1, width) for v in lists[:4])
    b_qkv = lax.dynamic_index_in_dim(lists[4].reshape(3, heads, n_t, head_dim), t, 2, False).reshape(1, split)
    b_up = lax.dynamic_index_in_dim(lists[5].reshape(n_q, n_t, units), t, 1, False).reshape(1, own_units)
    b_project = jnp.concatenate([b_qkv, b_up], 1)

    x_all, hidden, qkv, act, slope = project(x_arrays, token_plan, gain, shift, w1, b_project, split)
    att_other, kept_other = attend(order, qkv, tables, heads, head_dim, span, 1)
    out_other = combine(act, att_other, w2, 1, rows)
    g_line = ring_gathered(after(cotangent, *x_line[-2:]), "ctx", z_order, out_other)
    att_own, kept_own = attend(order, after(qkv, *out_other, *g_line[1:-2]), tables, heads, head_dim, span, 0)
    out_own = combine(act, att_own, w2, 0, rows, [swap(p) for p in out_other])
    g_arrays = g_line + [swap(p) for p in g_line[:-2]] + [swap(after(p, *out_own)) for p in g_line[-2:]]

    g_all, pre_grad, att_grad, g_sums = combine_back(g_arrays, token_plan, w2, after(slope, *out_own))
    up_own, up_sums = weight_grad(turns, hidden, [pre_grad])
    out_parts, out_sent = ring_sum(out_own, "ctx", z_order, up_own)
    up_first = ring_first(up_own, "q", q_order)
    att_grad = after(att_grad, *up_own, *out_sent).reshape(2, seq_len, own_width)
    grad_other = attend_back(order, kept_other, att_grad, tables, heads, head_dim, span, 1)
    up_parts, up_sent = ring_rest(up_own, up_first, "q", q_order, [grad_other])
    normed_other, sums_other = project_back(after(grad_other, *up_sent), pre_grad, w1, x_all, 1, rows)
    att_grad = after(att_grad, *normed_other)
    grad_own = attend_back(order, kept_own, att_grad, tables, heads, head_dim, span, 0)
    up_rows = last_sum(at, [after(up_parts[0], grad_own)] + up_parts[1:], n_t)
    up_came = scattered(up_rows, "ctx")
    normed_own, sums_own = project_back(
        after(grad_own, *out_parts[1:], *up_rows), pre_grad, w1, x_all, 0, rows, [swap(p) for p in normed_other]
    )
    vectors = pack_vectors(
        at, sums_own, sums_other, g_sums, up_sums, (n_q, n_t, heads, head_dim, units), (d_rows, qkv_bias.shape[0]), split
    )
    qkv_own, _ = weight_grad(turns, after(hidden, *normed_own), [grad_own, grad_other], vectors)
    qkv_parts = direct_scattered(qkv_own, "q", q_order)
    normed_own = [after(p, *up_came[1:]) for p in normed_own]
    normed_first = ring_first(normed_own, "ctx", z_order)
    normed_parts, normed_sent = ring_rest(normed_own, normed_first, "ctx", z_order, qkv_own)
    qkv_rows = last_sum(at, qkv_parts, n_t, 2 * n_t)
    down, out_apart = down_grad(turns, after(act, *normed_sent), (att_own, att_other), g_all, head_dim if whole_heads else 0)
    down_parts, down_sent = ring_sum([after(p, *qkv_parts[1:-1]) for p in down], "q", q_order, [normed_parts[1], *qkv_rows])
    output = output_sum(inputs, b_out + b_down, [after(out_parts[0], *normed_sent, *down)] + out_parts[1:])

    qkv_came = scattered(qkv_rows, "ctx")
    if whole_heads:
        fc2_weight_grad, out_weight_grad = split_sum(down_parts, [units, head_dim])
    else:
        (fc2_weight_grad,) = split_sum(down_parts, [units])
        spread = jnp.zeros((heads, n_t, head_dim, width), F32)
        spread = lax.dynamic_update_slice(spread, out_apart.reshape(heads, 1, head_dim, width), (0, t, 0, 0))
        out_weight_grad = lax.psum_scatter(spread.reshape(width, width), every, scatter_dimension=0, tiled=True)
    input_grad = finish(normed_parts, inputs, cotangent, gain)
    up_got = swap(theirs([after(up_came[0], *normed_parts[1:], output)] + up_came[1:]))
    (fc1_weight_grad,) = from_blocks(at, up_came, up_got, n_q, units)
    qkv_got = swap(theirs([after(qkv_came[0], up_got, fc1_weight_grad, input_grad, fc2_weight_grad)] + qkv_came[1:]))
    qkv_weight_grad, total = from_blocks(at, qkv_came, qkv_got, 3 * heads, head_dim, 16)
    total = total[0]

    cuts = [ln_gain.shape[0], ln_bias.shape[0], out_bias.shape[0], qkv_bias.shape[0], fc1_bias.shape[0]]
    starts = [sum(cuts[:i]) for i in range(len(cuts))]
    gain_grad, shift_grad, bias_grad, qkv_bias_grad, fc1_bias_grad = (total[s : s + c] for s, c in zip(starts, cuts))
    return (
        output,
        input_grad,
        gain_grad,
        shift_grad,
        qkv_weight_grad,
        qkv_bias_grad,
        out_weight_grad,
        bias_grad,
        fc1_weight_grad,
        fc1_bias_grad,
        fc2_weight_grad,
        bias_grad,
    )


def solution(mesh):
    n_dp, n_ctx = mesh.devices.shape
    inner = Mesh(mesh.devices.reshape(n_dp // 2, 2, n_ctx), ("q", "core", "ctx"))
    every = ("q", "core", "ctx")
    matrix, vector = P(every, None), P(every)
    return jax.shard_map(
        per_device,
        mesh=inner,
        in_specs=(
            matrix,
            P(),
            vector,
            vector,
            matrix,
            vector,
            matrix,
            vector,
            matrix,
            vector,
            matrix,
            vector,
            matrix,
        ),
        out_specs=(matrix, matrix, vector, vector, matrix, vector, matrix, vector, matrix, vector, matrix, vector),
        check_vma=False,
    )
```
